256 devices in a mesh: gx: 32 (over x, z), gy: 8 (over y, core).
Axes of the slice: x: 4, y: 4, z: 8, core: 2. Of those that a mesh axis runs over, the one named last changes fastest.
Arguments:
- right_sides: float32 [16, 32, 128, 1024], P(None, None, 'gx', 'gy'), may hold values from -2000 to 2000
- region_labels: int32 [32, 128, 1024], P(None, 'gx', 'gy'), may hold values from 0 to 7
- face_flags: int32 [2, 128, 1024], P(None, 'gx', 'gy'), may hold values 0 or 1
- region_perm: float32 [8], replicated, may hold values from 0.1 to 10
Outputs:
- orthonormal: float32 [80, 32, 128, 1024], P(None, None, 'gx', 'gy')
- triangular_factor: float32 [80, 80], replicated
The draws below stay inside these ranges and needn't reach their ends.
All inputs are finite; a program needn't handle non-finite values. No bound on the sum of `face_flags` on one device may be relied on, other than what follows from the above.
Results may differ from the reference program's by a relative error of at most 0.0003.
Values sent between devices are 32-bit elements; how exact they have to be, the bound alone decides.
A program may use at most 128 MiB of HBM per device.

```python
import math
import jax
import jax.numpy as jnp
from jax import lax

RHS = 16
S = 4
REGIONS = 8
NZ = 32
BASIS = 80
NX = 128
NY = 1024
CELLS = 4194304


def draw_right_sides(key, part):
    key = jax.random.fold_in(key, 17)
    fluct_key, scale_key = jax.random.split(key)
    across_x = jnp.arange(NX, dtype=jnp.float32) / max(NX - 1, 1)
    along_y = jnp.arange(NY, dtype=jnp.float32) / max(NY - 1, 1)
    column_scale = jnp.exp(jax.random.uniform(scale_key, (RHS, 1, 1, 1), jnp.float32, 0.0, math.log(10.0)))
    growth = math.log(3.0)
    fluctuation = jnp.clip(jax.random.normal(fluct_key, (RHS, NZ, NX, NY), jnp.float32), -4.0, 4.0)
    amplitude = jnp.exp(growth * (across_x[:, None] + along_y[None, :]))
    return (fluctuation * amplitude * column_scale).astype(jnp.float32)


def plant(result, own_key, smallest, high):
    longest = result.shape.index(max(result.shape))
    spots = []
    for shift in (0, 1):
        where = [jax.random.randint(jax.random.fold_in(own_key, axis), (), 0, length) for axis, length in enumerate(result.shape)]
        where[longest] = (where[longest] + shift) % result.shape[longest]
        spots.append(tuple(where))
    return result.at[spots[0]].set(smallest).at[spots[1]].set(high)


def setup_inputs(seed: int = 0) -> dict:
    keys = jax.random.split(jax.random.key(seed), 5)
    right_sides = draw_right_sides(jax.random.fold_in(keys[4], 71), 0)
    region_labels = plant(jax.random.randint(keys[1], (NZ, NX, NY), 0, REGIONS), jax.random.fold_in(keys[1], 1), 0, REGIONS - 1).astype(jnp.int32)
    face_flags = plant((jax.random.randint(keys[2], (2, NX, NY), 0, 2) < 1).astype(jnp.int32), jax.random.fold_in(keys[2], 1), 0, 1)
    region_perm = jnp.clip(jnp.exp(jax.random.uniform(keys[3], (REGIONS,), jnp.float32, math.log(0.1), math.log(10.0))), 0.1, 10.0)
    return {"right_sides": right_sides, "region_labels": region_labels, "face_flags": face_flags, "region_perm": region_perm}


def harmonic(centre, neighbour):
    summed = centre + neighbour
    return 2.0 * centre * neighbour / jnp.where(summed > 0, summed, 1.0)

def weights(extended, layers):
    permeability = extended[:layers]
    centre = permeability[:, 1:-1, 1:-1]
    blank_plane = jnp.zeros_like(centre[:1])
    beneath = jnp.concatenate([blank_plane, centre[:-1]], 0)
    overhead = jnp.concatenate([centre[1:], blank_plane], 0)
    couplings = [harmonic(centre, permeability[:, :-2, 1:-1]), harmonic(centre, permeability[:, 2:, 1:-1]), harmonic(centre, permeability[:, 1:-1, :-2]), harmonic(centre, permeability[:, 1:-1, 2:]), harmonic(centre, beneath), harmonic(centre, overhead)]
    bottom_face = 2.0 * centre[:1] * extended[layers:layers + 1, 1:-1, 1:-1]
    top_face = 2.0 * centre[-1:] * extended[layers + 1:layers + 2, 1:-1, 1:-1]
    boundary = jnp.concatenate([bottom_face, jnp.zeros_like(centre[1:-1]), top_face], 0)
    diagonal = couplings[0] + couplings[1] + couplings[2] + couplings[3] + couplings[4] + couplings[5] + boundary
    divisor = jnp.where(diagonal > 0, diagonal, 1.0)
    return jnp.stack([single / divisor for single in couplings])

def jacobi(coupling, extended):
    centre = extended[:, :, 1:-1, 1:-1]
    blank_plane = jnp.zeros_like(centre[:, :1])
    beneath = jnp.concatenate([blank_plane, centre[:, :-1]], 1)
    overhead = jnp.concatenate([centre[:, 1:], blank_plane], 1)
    summed = coupling[0] * extended[:, :, :-2, 1:-1] + coupling[1] * extended[:, :, 2:, 1:-1] + coupling[2] * extended[:, :, 1:-1, :-2] + coupling[3] * extended[:, :, 1:-1, 2:] + coupling[4] * beneath + coupling[5] * overhead
    return -summed

def padded(field):
    return jnp.pad(field, ((0, 0), (0, 0), (1, 1), (1, 1)))

def reference(right_sides, region_labels, face_flags, region_perm):
    permeability = region_perm[region_labels]
    stacked_coeff = jnp.concatenate([permeability, face_flags.astype(jnp.float32)], 0)
    extended = jnp.pad(stacked_coeff, ((0, 0), (1, 1), (1, 1)))
    coupling = weights(extended, NZ)
    previous = right_sides
    current = jacobi(coupling, padded(right_sides))
    columns = [right_sides, current]
    for power_index in range(1, S):
        following = 2.0 * jacobi(coupling, padded(current)) - previous
        previous, current = (current, following)
        columns.append(following)
    stacked = jnp.stack(columns).reshape(BASIS, NZ * NX * NY)
    gram_matrix = jnp.dot(stacked.astype(jnp.float32), stacked.T.astype(jnp.float32), preferred_element_type=jnp.float32, precision=lax.Precision.HIGHEST) / CELLS
    lower_factor = jnp.linalg.cholesky(gram_matrix)
    orthonormal = jax.scipy.linalg.solve_triangular(lower_factor, stacked, lower=True)
    return (orthonormal.reshape(BASIS, NZ, NX, NY), lower_factor.T)
```

```python
import functools
import jax
import jax.numpy as jnp
from jax import lax
from jax.experimental import pallas as pl
from jax.experimental.pallas import tpu as pltpu
from jax.sharding import PartitionSpec as P

RHS = 16
S = 4
VECS = S + 1
COLS = RHS * VECS
NZ = 32
BX = 4
BY = 128
HALF = 8
MESH = pl.DeviceIdType.MESH
f32 = jnp.float32
bf16 = jnp.bfloat16


def split(value):
    high = value.astype(bf16)
    low = (value - high.astype(f32)).astype(bf16)
    return high, low


def harmonic(centre, neighbour):
    summed = centre + neighbour
    return 2.0 * centre * neighbour / jnp.where(summed > 0, summed, 1.0)


def basis_kernel(
    sizes,
    rs, labels, flags, perm,
    v, gram,
    stage, xl, xr, yl, yr, el, eh, kown, kxl, kxr, kyl, kyr, ct, cb, ar_y, ar_z, ar_x,
    load_sem, ksend, krecv, xsend, xrecv, ysend, yrecv, asend, arecv,
):
    gx_n, gy_n, zg, xg = sizes
    gx = lax.axis_index("gx")
    gy = lax.axis_index("gy")
    right = lax.rem(gx + 1, gx_n)
    left = lax.rem(gx + gx_n - 1, gx_n)
    above = lax.rem(gy + 1, gy_n)
    below = lax.rem(gy + gy_n - 1, gy_n)
    zi = lax.rem(gx, zg)
    xi = lax.div(gx, zg)

    def z_peer(k):
        return (xi * zg + lax.rem(zi + k, zg), gy)

    def x_peer(k):
        return (lax.rem(xi + k, xg) * zg + zi, gy)

    def y_peer(k):
        return (gx, lax.rem(gy + k, gy_n))

    peers = [(right, gy), (left, gy)]
    peers += [y_peer(k) for k in range(1, gy_n)]
    peers += [z_peer(k) for k in range(1, zg)]
    peers += [x_peer(k) for k in range(1, xg)]
    barrier = pltpu.get_barrier_semaphore()
    for peer in peers:
        pl.semaphore_signal(barrier, inc=1, device_id=peer, device_id_type=MESH)

    loads = [
        pltpu.make_async_copy(rs.at[pl.ds(c * HALF * NZ * BX, HALF * NZ * BX), :],
                              stage.at[pl.ds(c * HALF * NZ * BX, HALF * NZ * BX), :], load_sem.at[c])
        for c in range(2)
    ]
    for load in loads:
        load.start()

    for x in range(BX):
        label = labels[pl.ds(x, NZ, stride=BX), :]
        value = jnp.zeros((NZ, BY), f32)
        for region in range(perm.shape[0]):
            value = jnp.where(label == region, perm[region], value)
        kown[x] = value

    def remote(src, dst, send, recv, peer):
        return pltpu.make_async_remote_copy(
            src_ref=src, dst_ref=dst, send_sem=send, recv_sem=recv, device_id=peer, device_id_type=MESH
        )

    kcopies = [
        remote(kown.at[BX - 1], kxl, ksend.at[0], krecv.at[0], (right, gy)),
        remote(kown.at[0], kxr, ksend.at[1], krecv.at[1], (left, gy)),
        remote(kown, kyl, ksend.at[2], krecv.at[2], (gx, above)),
        remote(kown, kyr, ksend.at[3], krecv.at[3], (gx, below)),
    ]

    def xcopies(j, c):
        plane = pl.ds(j * RHS + c * HALF, HALF)
        return [
            remote(v.at[:, BX - 1, plane, :], xl.at[j, c], xsend.at[j, c, 0], xrecv.at[j, c, 0], (right, gy)),
            remote(v.at[:, 0, plane, :], xr.at[j, c], xsend.at[j, c, 1], xrecv.at[j, c, 1], (left, gy)),
        ]

    def ycopies(j, c):
        return [
            remote(eh.at[j, c], yl.at[j, c], ysend.at[j, c, 0], yrecv.at[j, c, 0], (gx, above)),
            remote(el.at[j, c], yr.at[j, c], ysend.at[j, c, 1], yrecv.at[j, c, 1], (gx, below)),
        ]

    lane = lax.broadcasted_iota(jnp.int32, (HALF, BY), 1)
    blank = jnp.zeros((HALF, BY), f32)

    def pack(value, r, low, high):
        low = jnp.where(lane == r, pltpu.roll(value, r, 1), low)
        high = jnp.where(lane == r, pltpu.roll(value, lax.rem(r + 1, BY), 1), high)
        return low, high

    pl.semaphore_wait(barrier, len(peers))
    for copy in kcopies:
        copy.start()

    for c in range(2):
        loads[c].wait()

        def relayout(z, carry, c=c):
            low, high = carry
            for x in range(BX):
                r = z * BX + x
                value = stage[pl.ds(c * HALF * NZ * BX + r, HALF, stride=NZ * BX), :]
                v[z, x, pl.ds(c * HALF, HALF), :] = value
                low, high = pack(value, r, low, high)
            return low, high

        low, high = lax.fori_loop(0, NZ, relayout, (blank, blank))
        for copy in xcopies(0, c):
            copy.start()
        el[0, c] = low
        eh[0, c] = high
        for copy in ycopies(0, c):
            copy.start()

    for copy in kcopies:
        copy.wait_recv()
    wide_lane = lax.broadcasted_iota(jnp.int32, (NZ, BY), 1)
    level = lax.broadcasted_iota(jnp.int32, (NZ, BY), 0)
    for x in range(BX):
        centre = kown[x]
        xm = kown[x - 1] if x > 0 else jnp.where(gx == 0, 0.0, kxl[...])
        xp = kown[x + 1] if x < BX - 1 else jnp.where(gx == gx_n - 1, 0.0, kxr[...])
        from_below = jnp.where(gy == 0, 0.0, kyl[x])
        from_above = jnp.where(gy == gy_n - 1, 0.0, kyr[x])
        ym = jnp.where(wide_lane == 0, pltpu.roll(from_below, 1, 1), pltpu.roll(centre, 1, 1))
        yp = jnp.where(wide_lane == BY - 1, pltpu.roll(from_above, BY - 1, 1), pltpu.roll(centre, BY - 1, 1))
        zm = jnp.where(level == 0, 0.0, pltpu.roll(centre, 1, 0))
        zp = jnp.where(level == NZ - 1, 0.0, pltpu.roll(centre, NZ - 1, 0))
        t = [harmonic(centre, other) for other in (xm, xp, ym, yp, zm, zp)]
        bottom = flags[pl.ds(x, 1), :].astype(f32)
        top = flags[pl.ds(BX + x, 1), :].astype(f32)
        boundary = jnp.where(level == 0, 2.0 * centre * bottom, 0.0)
        boundary = boundary + jnp.where(level == NZ - 1, 2.0 * centre * top, 0.0)
        diagonal = t[0] + t[1] + t[2] + t[3] + t[4] + t[5] + boundary
        divisor = jnp.where(diagonal > 0, diagonal, 1.0)
        for n in range(6):
            ct[n, x] = -(t[n] / divisor)

    def spread(block, carry):
        for n in range(6):
            for x in range(BX):
                rows = ct[n, x, pl.ds(pl.multiple_of(block * 8, 8), 8), :]
                for s in range(8):
                    cb[block * 8 + s, x, n] = jnp.broadcast_to(rows[s : s + 1, :], (HALF, BY))
        return carry

    lax.fori_loop(0, NZ // 8, spread, 0)

    for j in range(S):
        for c in range(2):
            for copy in xcopies(j, c) + ycopies(j, c):
                copy.wait_recv()
            ylow = yl[j, c]
            yhigh = yr[j, c]
            here = pl.ds(j * RHS + c * HALF, HALF)
            before = pl.ds((j - 1) * RHS + c * HALF, HALF)
            after = pl.ds((j + 1) * RHS + c * HALF, HALF)

            def advance(z, carry, j=j, c=c, ylow=ylow, yhigh=yhigh, here=here, before=before, after=after):
                low, high = carry
                zm = lax.rem(z + NZ - 1, NZ)
                zp = lax.rem(z + 1, NZ)
                row = [xl[j, c, z]] + [v[z, x, here, :] for x in range(BX)] + [xr[j, c, z]]
                for x in range(BX):
                    r = z * BX + x
                    centre = row[x + 1]
                    ym = jnp.where(lane == 0, pltpu.roll(ylow, lax.rem(BY - r, BY), 1), pltpu.roll(centre, 1, 1))
                    yp = jnp.where(lane == BY - 1, pltpu.roll(yhigh, BY - 1 - r, 1), pltpu.roll(centre, BY - 1, 1))
                    summed = (
                        cb[z, x, 0] * row[x]
                        + cb[z, x, 1] * row[x + 2]
                        + cb[z, x, 2] * ym
                        + cb[z, x, 3] * yp
                        + cb[z, x, 4] * v[zm, x, here, :]
                        + cb[z, x, 5] * v[zp, x, here, :]
                    )
                    value = summed if j == 0 else 2.0 * summed - v[z, x, before, :]
                    v[z, x, after, :] = value
                    if j < S - 1:
                        low, high = pack(value, r, low, high)
                return low, high

            low, high = lax.fori_loop(0, NZ, advance, (blank, blank))
            if j < S - 1:
                for copy in xcopies(j + 1, c):
                    copy.start()
                el[j + 1, c] = low
                eh[j + 1, c] = high
                for copy in ycopies(j + 1, c):
                    copy.start()

    def products(z, acc):
        for h in range(2):
            both = jnp.concatenate([v[z, 2 * h], v[z, 2 * h + 1]], axis=1)
            high, low = split(both)
            acc = acc + lax.dot_general(
                high, jnp.concatenate([high, low], axis=0), (((1,), (1,)), ((), ())), preferred_element_type=f32
            )
        return acc

    acc = lax.fori_loop(0, NZ, products, jnp.zeros((COLS, 2 * COLS), f32))
    cross = jnp.concatenate([acc[:, COLS:], jnp.zeros((COLS, 128 - COLS), f32)], axis=1)
    cross = jnp.concatenate([cross, jnp.zeros((128 - COLS, 128), f32)], axis=0)
    main = jnp.concatenate([acc[:, :COLS], jnp.zeros((COLS, 128 - COLS), f32)], axis=1)
    total = main + cross[:COLS] + cross.T[:COLS]

    waits = []
    for phase, (buffer, index, count, peer_of) in enumerate(
        [(ar_y, gy, gy_n, y_peer), (ar_z, zi, zg, z_peer), (ar_x, xi, xg, x_peer)]
    ):
        buffer[index] = total
        copies = [
            remote(buffer.at[index], buffer.at[index], asend.at[phase, k - 1], arecv.at[phase, k - 1], peer_of(k))
            for k in range(1, count)
        ]
        for copy in copies:
            copy.start()
        for copy in copies:
            copy.wait_recv()
        waits += copies
        total = buffer[0]
        for k in range(1, count):
            total = total + buffer[k]
    gram[...] = total

    for copy in kcopies + waits:
        copy.wait_send()
    for j in range(S):
        for c in range(2):
            for copy in xcopies(j, c) + ycopies(j, c):
                copy.wait_send()


def factor(gram):
    count = COLS // 8
    lane = lax.broadcasted_iota(jnp.int32, (8, 128), 1)
    row = lax.broadcasted_iota(jnp.int32, (8, 128), 0)
    left = [gram[8 * b : 8 * b + 8, :] for b in range(count)]
    right = [jnp.where(lane == row + 8 * b, 1.0, 0.0).astype(f32) for b in range(count)]
    for k in range(COLS):
        b, s = divmod(k, 8)
        pivot_left = left[b][s : s + 1, :]
        pivot_right = right[b][s : s + 1, :]
        inverse = 1.0 / pivot_left[:, k : k + 1]
        scaled_left = pivot_left * inverse
        scaled_right = pivot_right * inverse
        for i in range(b, count):
            column = left[i][:, k : k + 1]
            if i == b:
                column = jnp.where(row[:, :1] > s, column, 0.0)
            left[i] = left[i] - column * scaled_left
            right[i] = right[i] - column * scaled_right
    for b in range(count):
        diagonal = jnp.sum(jnp.where(lane == row + 8 * b, left[b], 0.0), axis=1, keepdims=True)
        scale = 1.0 / jnp.sqrt(diagonal)
        left[b] = jnp.where(lane >= row + 8 * b, left[b], 0.0) * scale
        right[b] = right[b] * scale
    return jnp.concatenate(left, axis=0), jnp.concatenate(right, axis=0)


def finish_kernel(cells, v, gram, out, r_out, stage, sems):
    upper, inverse = factor(gram[...] / cells)
    r_out[...] = upper[:, :COLS]
    high = inverse.astype(bf16).astype(f32)
    low = inverse - high
    wide_high = jnp.concatenate([high, jnp.zeros((COLS, 128), f32)], axis=1)
    wide_low = jnp.concatenate([low, jnp.zeros((COLS, 128), f32)], axis=1)
    weights = wide_high + pltpu.roll(wide_high, COLS, 1) + pltpu.roll(wide_low, 2 * COLS, 1)
    weights = weights[:, : 3 * COLS].astype(bf16)
    groups = 4
    per = NZ // groups
    copies = []
    for group in range(groups):
        def block(z, carry):
            for h in range(2):
                both = jnp.concatenate([v[z, 2 * h], v[z, 2 * h + 1]], axis=1)
                vh, vl = split(both)
                q = jnp.dot(weights, jnp.concatenate([vh, vl, vh], axis=0), preferred_element_type=f32)
                r = z * BX + 2 * h
                stage[pl.ds(r, COLS, stride=NZ * BX), :] = q[:, :BY]
                stage[pl.ds(r + 1, COLS, stride=NZ * BX), :] = q[:, BY:]
            return carry

        lax.fori_loop(group * per, (group + 1) * per, block, 0)
        rows = pl.ds(group * per * BX, per * BX)
        copy = pltpu.make_async_copy(
            stage.reshape(COLS, NZ * BX, BY).at[:, rows, :], out.at[:, rows, :], sems.at[group]
        )
        copy.start()
        copies.append(copy)
    for copy in copies:
        copy.wait()


def per_device(sizes, cells, right_sides, region_labels, face_flags, region_perm):
    gx_n, gy_n, zg, xg = sizes
    vmem = pl.BlockSpec(memory_space=pltpu.VMEM)
    hbm = pl.BlockSpec(memory_space=pl.ANY)
    v, gram = pl.pallas_call(
        functools.partial(basis_kernel, sizes),
        out_shape=(pltpu.VMEM((NZ, BX, COLS, BY), f32), pltpu.VMEM((COLS, 128), f32)),
        in_specs=[hbm, vmem, vmem, pl.BlockSpec(memory_space=pltpu.SMEM)],
        out_specs=(vmem, vmem),
        scratch_shapes=[
            pltpu.VMEM((RHS * NZ * BX, BY), f32),
            pltpu.VMEM((S, 2, NZ, HALF, BY), f32),
            pltpu.VMEM((S, 2, NZ, HALF, BY), f32),
            pltpu.VMEM((S, 2, HALF, BY), f32),
            pltpu.VMEM((S, 2, HALF, BY), f32),
            pltpu.VMEM((S, 2, HALF, BY), f32),
            pltpu.VMEM((S, 2, HALF, BY), f32),
            pltpu.VMEM((BX, NZ, BY), f32),
            pltpu.VMEM((NZ, BY), f32),
            pltpu.VMEM((NZ, BY), f32),
            pltpu.VMEM((BX, NZ, BY), f32),
            pltpu.VMEM((BX, NZ, BY), f32),
            pltpu.VMEM((6, BX, NZ, BY), f32),
            pltpu.VMEM((NZ, BX, 6, HALF, BY), f32),
            pltpu.VMEM((gy_n, COLS, 128), f32),
            pltpu.VMEM((zg, COLS, 128), f32),
            pltpu.VMEM((xg, COLS, 128), f32),
            pltpu.SemaphoreType.DMA((2,)),
            pltpu.SemaphoreType.DMA((4,)),
            pltpu.SemaphoreType.DMA((4,)),
            pltpu.SemaphoreType.DMA((S, 2, 2)),
            pltpu.SemaphoreType.DMA((S, 2, 2)),
            pltpu.SemaphoreType.DMA((S, 2, 2)),
            pltpu.SemaphoreType.DMA((S, 2, 2)),
            pltpu.SemaphoreType.DMA((3, 8)),
            pltpu.SemaphoreType.DMA((3, 8)),
        ],
        compiler_params=pltpu.CompilerParams(
            collective_id=0, has_side_effects=True, vmem_limit_bytes=40 * 1024 * 1024
        ),
        name="basis",
    )(
        right_sides.reshape(RHS * NZ * BX, BY),
        region_labels.reshape(NZ * BX, BY),
        face_flags.reshape(2 * BX, BY),
        region_perm,
    )
    out, upper = pl.pallas_call(
        functools.partial(finish_kernel, cells),
        out_shape=(
            jax.ShapeDtypeStruct((COLS, NZ * BX, BY), f32),
            jax.ShapeDtypeStruct((COLS, COLS), f32),
        ),
        in_specs=[vmem, vmem],
        out_specs=(hbm, vmem),
        scratch_shapes=[pltpu.VMEM((COLS * NZ * BX, BY), f32), pltpu.SemaphoreType.DMA((4,))],
        compiler_params=pltpu.CompilerParams(vmem_limit_bytes=40 * 1024 * 1024),
        name="finish",
    )(v, gram)
    return out.reshape(COLS, NZ, BX, BY), upper


def solution(mesh):
    gx_n, gy_n = mesh.shape["gx"], mesh.shape["gy"]
    zg = 8 if gx_n % 8 == 0 else 2
    sizes = (gx_n, gy_n, zg, gx_n // zg)
    cells = NZ * BX * BY * gx_n * gy_n
    placed = (P(None, None, "gx", "gy"), P(None, "gx", "gy"), P(None, "gx", "gy"), P())
    return jax.shard_map(
        functools.partial(per_device, sizes, cells),
        mesh=mesh,
        in_specs=placed,
        out_specs=(P(None, None, "gx", "gy"), P()),
        check_vma=False,
    )
```

```python
import functools
import jax
import jax.numpy as jnp
from jax import lax
from jax.experimental import pallas as pl
from jax.experimental.pallas import tpu as pltpu
from jax.sharding import PartitionSpec as P

RHS = 16
S = 4
VECS = S + 1
COLS = RHS * VECS
NZ = 32
BX = 4
BY = 128
HALF = 8
LEAD = RHS * S
LEVELS = 8
CHUNKS = NZ // LEVELS
ROWS = LEVELS * BX
NT = (((1,), (1,)), ((), ()))
NN = (((1,), (0,)), ((), ()))
MESH = pl.DeviceIdType.MESH
f32 = jnp.float32
bf16 = jnp.bfloat16


def split(value):
    high = value.astype(bf16)
    low = (value - high.astype(f32)).astype(bf16)
    return high, low


def harmonic(centre, neighbour):
    summed = centre + neighbour
    return 2.0 * centre * neighbour / jnp.where(summed > 0, summed, 1.0)


def basis_kernel(
    sizes, cells,
    rs, labels_hbm, flags_hbm, perm,
    v, last_gram, lead,
    stage, labels, flags, xl, xr, edge, yl, yr, kown, kxl, kxr, kyl, kyr, ct, cb,
    acc_lead, acc_last, lead_own, lead_y, lead_z, lead_x, lead_all, last_y, last_z, last_x,
    load_sem, ksend, krecv, xsend, xrecv, ysend, yrecv, asend, arecv,
):
    gx_n, gy_n, zg, xg = sizes
    gx = lax.axis_index("gx")
    gy = lax.axis_index("gy")
    right = lax.rem(gx + 1, gx_n)
    left = lax.rem(gx + gx_n - 1, gx_n)
    above = lax.rem(gy + 1, gy_n)
    below = lax.rem(gy + gy_n - 1, gy_n)
    zi = lax.rem(gx, zg)
    xi = lax.div(gx, zg)

    def z_peer(k):
        return (xi * zg + lax.rem(zi + k, zg), gy)

    def x_peer(k):
        return (lax.rem(xi + k, xg) * zg + zi, gy)

    def y_peer(k):
        return (gx, lax.rem(gy + k, gy_n))

    loads = [
        pltpu.make_async_copy(labels_hbm, labels, load_sem.at[CHUNKS]),
        pltpu.make_async_copy(flags_hbm, flags, load_sem.at[CHUNKS + 1]),
    ] + [
        pltpu.make_async_copy(
            rs.at[:, pl.ds(q * ROWS, ROWS), :], stage.reshape(CHUNKS, RHS, ROWS, BY).at[q], load_sem.at[q]
        )
        for q in range(CHUNKS)
    ]
    for load in loads:
        load.start()
    peers = [(right, gy), (left, gy)]
    peers += [y_peer(k) for k in range(1, gy_n)]
    peers += [z_peer(k) for k in range(1, zg)]
    peers += [x_peer(k) for k in range(1, xg)]
    barrier = pltpu.get_barrier_semaphore()
    for peer in peers:
        pl.semaphore_signal(barrier, inc=1, device_id=peer, device_id_type=MESH)

    loads[0].wait()
    loads[1].wait()
    for x in range(BX):
        label = labels[pl.ds(x, NZ, stride=BX), :]
        value = jnp.zeros((NZ, BY), f32)
        for region in range(perm.shape[0]):
            value = jnp.where(label == region, perm[region], value)
        kown[x] = value

    def remote(src, dst, send, recv, peer):
        return pltpu.make_async_remote_copy(
            src_ref=src, dst_ref=dst, send_sem=send, recv_sem=recv, device_id=peer, device_id_type=MESH
        )

    kcopies = [
        remote(kown.at[BX - 1], kxl, ksend.at[0], krecv.at[0], (right, gy)),
        remote(kown.at[0], kxr, ksend.at[1], krecv.at[1], (left, gy)),
        remote(kown, kyl, ksend.at[2], krecv.at[2], (gx, above)),
        remote(kown, kyr, ksend.at[3], krecv.at[3], (gx, below)),
    ]

    def copies_of(j, q):
        levels = pl.ds(q * LEVELS, LEVELS)
        plane = pl.ds(j * RHS, RHS)
        return [
            remote(v.at[levels, BX - 1, plane, :], xl.at[j, q], xsend.at[j, q, 0], xrecv.at[j, q, 0], (right, gy)),
            remote(v.at[levels, 0, plane, :], xr.at[j, q], xsend.at[j, q, 1], xrecv.at[j, q, 1], (left, gy)),
            remote(edge.at[j, q], yl.at[j, q], ysend.at[j, q, 0], yrecv.at[j, q, 0], (gx, above)),
            remote(edge.at[j, q], yr.at[j, q], ysend.at[j, q, 1], yrecv.at[j, q, 1], (gx, below)),
        ]

    lane = lax.broadcasted_iota(jnp.int32, (HALF, BY), 1)
    pair = lax.div(lane, 2)
    odd = lax.rem(lane, 2) == 1

    def pack(value, rr, packed):
        return jnp.where(pair == rr, pltpu.roll(value, 2 * rr + 1, 1), packed)

    pl.semaphore_wait(barrier, len(peers))
    for copy in kcopies:
        copy.start()
    for q in range(CHUNKS):
        loads[2 + q].wait()

    def relayout(q, carry):
        packed = [jnp.zeros((HALF, BY), f32) for _ in range(2)]
        for s in range(LEVELS):
            for x in range(BX):
                rr = s * BX + x
                value = stage[pl.ds(q * RHS * ROWS + rr, RHS, stride=ROWS), :]
                v[q * LEVELS + s, x, :RHS, :] = value
                for h in range(2):
                    packed[h] = pack(value[h * HALF : (h + 1) * HALF], rr, packed[h])
        for h in range(2):
            edge[0, q, h] = packed[h]
        for copy in copies_of(0, q):
            copy.start()
        return carry

    lax.fori_loop(0, CHUNKS, relayout, 0)

    for copy in kcopies:
        copy.wait_recv()
    wide_lane = lax.broadcasted_iota(jnp.int32, (NZ, BY), 1)
    level = lax.broadcasted_iota(jnp.int32, (NZ, BY), 0)
    for x in range(BX):
        centre = kown[x]
        xm = kown[x - 1] if x > 0 else jnp.where(gx == 0, 0.0, kxl[...])
        xp = kown[x + 1] if x < BX - 1 else jnp.where(gx == gx_n - 1, 0.0, kxr[...])
        from_below = jnp.where(gy == 0, 0.0, kyl[x])
        from_above = jnp.where(gy == gy_n - 1, 0.0, kyr[x])
        ym = jnp.where(wide_lane == 0, pltpu.roll(from_below, 1, 1), pltpu.roll(centre, 1, 1))
        yp = jnp.where(wide_lane == BY - 1, pltpu.roll(from_above, BY - 1, 1), pltpu.roll(centre, BY - 1, 1))
        zm = jnp.where(level == 0, 0.0, pltpu.roll(centre, 1, 0))
        zp = jnp.where(level == NZ - 1, 0.0, pltpu.roll(centre, NZ - 1, 0))
        t = [harmonic(centre, other) for other in (xm, xp, ym, yp, zm, zp)]
        bottom = flags[pl.ds(x, 1), :].astype(f32)
        top = flags[pl.ds(BX + x, 1), :].astype(f32)
        boundary = jnp.where(level == 0, 2.0 * centre * bottom, 0.0)
        boundary = boundary + jnp.where(level == NZ - 1, 2.0 * centre * top, 0.0)
        diagonal = t[0] + t[1] + t[2] + t[3] + t[4] + t[5] + boundary
        divisor = jnp.where(diagonal > 0, diagonal, 1.0)
        for n in range(6):
            ct[n, x] = -(t[n] / divisor)

    def spread(block, carry):
        for n in range(6):
            for x in range(BX):
                rows = ct[n, x, pl.ds(pl.multiple_of(block * 8, 8), 8), :]
                for s in range(8):
                    cb[block * 8 + s, x, n] = jnp.broadcast_to(rows[s : s + 1, :], (HALF, BY))
        return carry

    lax.fori_loop(0, NZ // 8, spread, 0)

    def advance(j, q):
        for copy in copies_of(j, q):
            copy.wait_recv()
        base = q * LEVELS
        merged = [
            jnp.where(odd, pltpu.roll(yl[j, q, h], 1, 1), pltpu.roll(yr[j, q, h], BY - 1, 1)) for h in range(2)
        ]
        packed = [jnp.zeros((HALF, BY), f32) for _ in range(2)]
        for s in range(LEVELS):
            z = base + s
            zm = lax.rem(z + NZ - 1, NZ) if s == 0 else z - 1
            zp = lax.rem(z + 1, NZ) if s == LEVELS - 1 else z + 1
            for x in range(BX):
                rr = s * BX + x
                coupling = [cb[z, x, n] for n in range(6)]
                for h in range(2):
                    here = pl.ds(j * RHS + h * HALF, HALF)
                    rows = pl.ds(h * HALF, HALF)
                    centre = v[z, x, here, :]
                    xm = v[z, x - 1, here, :] if x > 0 else xl[j, q, s, rows, :]
                    xp = v[z, x + 1, here, :] if x < BX - 1 else xr[j, q, s, rows, :]
                    ends = pltpu.roll(merged[h], BY - 1 - 2 * rr, 1)
                    ym = jnp.where(lane == 0, ends, pltpu.roll(centre, 1, 1))
                    yp = jnp.where(lane == BY - 1, ends, pltpu.roll(centre, BY - 1, 1))
                    summed = (
                        coupling[0] * xm
                        + coupling[1] * xp
                        + coupling[2] * ym
                        + coupling[3] * yp
                        + coupling[4] * v[zm, x, here, :]
                        + coupling[5] * v[zp, x, here, :]
                    )
                    value = summed if j == 0 else 2.0 * summed - v[z, x, pl.ds((j - 1) * RHS + h * HALF, HALF), :]
                    v[z, x, pl.ds((j + 1) * RHS + h * HALF, HALF), :] = value
                    if j < S - 1:
                        packed[h] = pack(value, rr, packed[h])
        if j < S - 1:
            for h in range(2):
                edge[j + 1, q, h] = packed[h]
            for copy in copies_of(j + 1, q):
                copy.start()

    def lead_products(q):
        total = jnp.zeros((LEAD, 2 * LEAD), f32)
        for s in range(LEVELS):
            wide = jnp.concatenate([v[q * LEVELS + s, x, :LEAD, :] for x in range(BX)], axis=1)
            high, low = split(wide)
            total = total + lax.dot_general(high, jnp.concatenate([high, low], axis=0), NT, preferred_element_type=f32)
        acc_lead[...] += total

    def last_products(q):
        total = jnp.zeros((2 * RHS, 2 * COLS), f32)
        for s in range(LEVELS):
            wide = jnp.concatenate([v[q * LEVELS + s, x] for x in range(BX)], axis=1)
            high, low = split(wide)
            total = total + lax.dot_general(
                jnp.concatenate([high[LEAD:], low[LEAD:]], axis=0),
                jnp.concatenate([high, low], axis=0),
                NT,
                preferred_element_type=f32,
            )
        acc_last[...] += total

    def exchange(phase, buffer, index, count, peer_of, source=None):
        def of(k):
            src = buffer.at[index] if source is None else source.at[lax.rem(index + k, count)]
            return remote(src, buffer.at[index], asend.at[phase, k - 1], arecv.at[phase, k - 1], peer_of(k))

        return [of(k) for k in range(1, count)]

    steps_lead = [
        exchange(0, lead_y, gy, gy_n, y_peer, lead_own),
        exchange(1, lead_z, zi, zg, z_peer),
        exchange(2, lead_x, xi, xg, x_peer),
        exchange(3, lead_all, gy, gy_n, y_peer),
    ]
    steps_last = [
        exchange(4, last_y, gy, gy_n, y_peer),
        exchange(5, last_z, zi, zg, z_peer),
        exchange(6, last_x, xi, xg, x_peer),
    ]

    def send(step):
        for copy in step:
            copy.start()

    def collect(step, buffer):
        for copy in step:
            copy.wait_recv()
        total = buffer[0]
        for k in range(1, len(step) + 1):
            total = total + buffer[k]
        return total

    acc_lead[...] = jnp.zeros_like(acc_lead)
    acc_last[...] = jnp.zeros_like(acc_last)

    def loop(j, more=None):
        def body(q, carry):
            advance(j, q)
            if more is not None:
                more(q)
            return carry

        lax.fori_loop(0, CHUNKS, body, 0)

    loop(0)
    loop(1)
    loop(2, lead_products)

    partial = acc_lead[...]
    mirrored = jnp.concatenate([partial, jnp.zeros((128 - LEAD, 128), f32)], axis=0).T[LEAD : 2 * LEAD]
    lead_lane = lax.broadcasted_iota(jnp.int32, (LEAD, 128), 1)
    partial = jnp.where(lead_lane < LEAD, partial + pltpu.roll(partial, LEAD, 1), 0.0) + mirrored
    for b in range(LEAD // 8):
        lead_own[b] = partial[8 * b : 8 * b + 8]
    lead_y[gy] = lead_own[gy]
    send(steps_lead[0])

    def beside(q):
        last_products(q)

        @pl.when(q == 0)
        def _():
            lead_z[zi] = collect(steps_lead[0], lead_y)
            send(steps_lead[1])

        @pl.when(q == 1)
        def _():
            lead_x[xi] = collect(steps_lead[1], lead_z)
            send(steps_lead[2])

        @pl.when(q == 2)
        def _():
            lead_all[gy] = collect(steps_lead[2], lead_x)
            send(steps_lead[3])

    loop(3, beside)

    partial = acc_last[...]
    last_y[gy] = jnp.concatenate(
        [partial[:RHS, :COLS] + partial[:RHS, COLS:] + partial[RHS:, :COLS], jnp.zeros((RHS, 128 - COLS), f32)], axis=1
    )
    send(steps_last[0])
    for copy in steps_lead[3]:
        copy.wait_recv()
    rows = eliminate_start([lead_all[b] * (1.0 / cells) for b in range(LEAD // 8)], LEAD)
    rows = eliminate(rows, 0, 24)
    last_z[zi] = collect(steps_last[0], last_y)
    send(steps_last[1])
    rows = eliminate(rows, 24, 48)
    last_x[xi] = collect(steps_last[1], last_z)
    send(steps_last[2])
    rows = eliminate(rows, 48, LEAD)
    lead[...] = jnp.concatenate(eliminate_end(rows, LEAD), axis=0)
    last_gram[...] = collect(steps_last[2], last_x) * (1.0 / cells)

    for copy in kcopies:
        copy.wait_send()

    def drain(q, carry):
        for j in range(S):
            for copy in copies_of(j, q):
                copy.wait_send()
        return carry

    lax.fori_loop(0, CHUNKS, drain, 0)
    for step in steps_lead + steps_last:
        for copy in step:
            copy.wait_send()


def eliminate_start(blocks, size):
    lane = lax.broadcasted_iota(jnp.int32, (8, 128), 1)
    row = lax.broadcasted_iota(jnp.int32, (8, 128), 0)
    return [
        jnp.where(lane < size, block, jnp.where(lane - size == row + 8 * b, 1.0, 0.0).astype(f32))
        for b, block in enumerate(blocks)
    ]


def eliminate(rows, begin, end):
    rows = list(rows)
    sub = lax.broadcasted_iota(jnp.int32, (8, 1), 0)
    for k in range(begin, end):
        b, s = divmod(k, 8)
        pivot = rows[b][s : s + 1, :]
        scaled = pivot * (1.0 / pivot[:, k : k + 1])
        for i in range(b, len(rows)):
            column = rows[i][:, k : k + 1]
            if i == b:
                column = jnp.where(sub > s, column, 0.0)
            rows[i] = rows[i] - column * scaled
    return rows


def eliminate_end(rows, size):
    lane = lax.broadcasted_iota(jnp.int32, (8, 128), 1)
    row = lax.broadcasted_iota(jnp.int32, (8, 128), 0)
    done = []
    for b, block in enumerate(rows):
        diagonal = jnp.sum(jnp.where(lane == row + 8 * b, block, 0.0), axis=1, keepdims=True)
        block = jnp.where((lane >= row + 8 * b) & (lane - size <= row + 8 * b), block, 0.0)
        done.append(block / jnp.sqrt(diagonal))
    return done


def exact(a, b, dims):
    return lax.dot_general(a, b, dims, precision=lax.Precision.HIGHEST, preferred_element_type=f32)


def finish_kernel(v, last_gram, lead, out, r_out, stage, sems):
    upper = lead[:, :LEAD]
    inverse = lead[:, LEAD:]
    against = last_gram[:, :LEAD]
    cross = exact(against, inverse, NT)
    schur = last_gram[:, LEAD:COLS] - exact(cross, cross, NT)
    back = exact(cross, inverse, NN)
    padded = jnp.concatenate([schur, jnp.zeros((RHS, 128 - RHS), f32)], axis=1)
    rows = eliminate_start([padded[:8], padded[8:]], RHS)
    rows = eliminate_end(eliminate(rows, 0, RHS), RHS)
    corner = jnp.concatenate(rows, axis=0)
    corner_upper = corner[:, :RHS]
    corner_inverse = corner[:, RHS : 2 * RHS]
    back = -exact(corner_inverse, back, NN)

    tall = jnp.concatenate([cross, jnp.zeros((RHS, 128 - LEAD), f32)], axis=1)
    tall = jnp.concatenate([tall, jnp.zeros((128 - RHS, 128), f32)], axis=0).T[:LEAD, :RHS]
    r_out[...] = jnp.concatenate(
        [
            jnp.concatenate([upper, tall], axis=1),
            jnp.concatenate([jnp.zeros((RHS, LEAD), f32), corner_upper], axis=1),
        ],
        axis=0,
    )
    whole = jnp.concatenate(
        [
            jnp.concatenate([inverse, jnp.zeros((LEAD, 256 - LEAD), f32)], axis=1),
            jnp.concatenate([back, corner_inverse, jnp.zeros((RHS, 256 - COLS), f32)], axis=1),
        ],
        axis=0,
    )
    high = whole.astype(bf16).astype(f32)
    low = whole - high
    weights = high + pltpu.roll(high, COLS, 1) + pltpu.roll(low, 2 * COLS, 1)
    weights = weights[:, : 3 * COLS].astype(bf16)
    groups = 4
    per = NZ // groups
    copies = []
    for group in range(groups):
        def block(step, carry):
            for s in range(4):
                z = step * 4 + s
                for h in range(2):
                    both = jnp.concatenate([v[z, 2 * h], v[z, 2 * h + 1]], axis=1)
                    vh, vl = split(both)
                    q = jnp.dot(weights, jnp.concatenate([vh, vl, vh], axis=0), preferred_element_type=f32)
                    r = z * BX + 2 * h
                    stage[pl.ds(r, COLS, stride=NZ * BX), :] = q[:, :BY]
                    stage[pl.ds(r + 1, COLS, stride=NZ * BX), :] = q[:, BY:]
            return carry

        lax.fori_loop(group * per // 4, (group + 1) * per // 4, block, 0)
        rows = pl.ds(group * per * BX, per * BX)
        copy = pltpu.make_async_copy(
            stage.reshape(COLS, NZ * BX, BY).at[:, rows, :], out.at[:, rows, :], sems.at[group]
        )
        copy.start()
        copies.append(copy)
    for copy in copies:
        copy.wait()


def per_device(sizes, cells, right_sides, region_labels, face_flags, region_perm):
    gx_n, gy_n, zg, xg = sizes
    vmem = pl.BlockSpec(memory_space=pltpu.VMEM)
    hbm = pl.BlockSpec(memory_space=pltpu.HBM)
    scratch = [
        (CHUNKS * RHS * ROWS, BY),
        (NZ * BX, BY, jnp.int32),
        (2 * BX, BY, jnp.int32),
        (S, CHUNKS, LEVELS, RHS, BY),
        (S, CHUNKS, LEVELS, RHS, BY),
        (S, CHUNKS, 2, HALF, BY),
        (S, CHUNKS, 2, HALF, BY),
        (S, CHUNKS, 2, HALF, BY),
        (BX, NZ, BY),
        (NZ, BY),
        (NZ, BY),
        (BX, NZ, BY),
        (BX, NZ, BY),
        (6, BX, NZ, BY),
        (NZ, BX, 6, HALF, BY),
        (LEAD, 2 * LEAD),
        (2 * RHS, 2 * COLS),
        (LEAD // 8, 8, 128),
        (gy_n, 8, 128),
        (zg, 8, 128),
        (xg, 8, 128),
        (LEAD // 8, 8, 128),
        (gy_n, RHS, 128),
        (zg, RHS, 128),
        (xg, RHS, 128),
    ]
    scratch = [
        pltpu.VMEM(shape[:-1], shape[-1]) if shape[-1] is jnp.int32 else pltpu.VMEM(shape, f32) for shape in scratch
    ]
    dma = pltpu.SemaphoreType.DMA
    scratch += [dma((CHUNKS + 2,)), dma((4,)), dma((4,))]
    scratch += [dma((S, CHUNKS, 2)) for _ in range(4)] + [dma((7, 8)), dma((7, 8))]
    v, last_gram, lead = pl.pallas_call(
        functools.partial(basis_kernel, sizes, cells),
        out_shape=(
            pltpu.VMEM((NZ, BX, COLS, BY), f32),
            pltpu.VMEM((RHS, 128), f32),
            pltpu.VMEM((LEAD, 2 * LEAD), f32),
        ),
        in_specs=[hbm, hbm, hbm, pl.BlockSpec(memory_space=pltpu.SMEM)],
        out_specs=(vmem, vmem, vmem),
        scratch_shapes=scratch,
        compiler_params=pltpu.CompilerParams(
            collective_id=0, has_side_effects=True, vmem_limit_bytes=40 * 1024 * 1024
        ),
        name="basis",
    )(
        *(pltpu.with_memory_space_constraint(a, pltpu.HBM) for a in (
            right_sides.reshape(RHS, NZ * BX, BY),
            region_labels.reshape(NZ * BX, BY),
            face_flags.reshape(2 * BX, BY),
            region_perm,
        )),
    )
    out, upper = pl.pallas_call(
        finish_kernel,
        out_shape=(
            jax.ShapeDtypeStruct((COLS, NZ * BX, BY), f32),
            jax.ShapeDtypeStruct((COLS, COLS), f32),
        ),
        in_specs=[vmem, vmem, vmem],
        out_specs=(hbm, vmem),
        scratch_shapes=[pltpu.VMEM((COLS * NZ * BX, BY), f32), dma((4,))],
        compiler_params=pltpu.CompilerParams(vmem_limit_bytes=40 * 1024 * 1024),
        name="finish",
    )(v, last_gram, lead)
    return out.reshape(COLS, NZ, BX, BY), upper


def solution(mesh):
    gx_n, gy_n = mesh.shape["gx"], mesh.shape["gy"]
    zg = 8 if gx_n % 8 == 0 else 2
    sizes = (gx_n, gy_n, zg, gx_n // zg)
    cells = NZ * BX * BY * gx_n * gy_n
    placed = (P(None, None, "gx", "gy"), P(None, "gx", "gy"), P(None, "gx", "gy"), P())
    return jax.shard_map(
        functools.partial(per_device, sizes, cells),
        mesh=mesh,
        in_specs=placed,
        out_specs=(P(None, None, "gx", "gy"), P()),
        check_vma=False,
    )
```

```python
import functools
import jax
import jax.numpy as jnp
from jax import lax
from jax.experimental import pallas as pl
from jax.experimental.pallas import tpu as pltpu
from jax.sharding import PartitionSpec as P

RHS = 16
S = 4
VECS = S + 1
COLS = RHS * VECS
NZ = 32
BX = 4
BY = 128
HALF = 8
LEAD = RHS * S
LEVELS = 8
CHUNKS = NZ // LEVELS
ROWS = LEVELS * BX
PITCH = NZ * BX + 8
NT = (((1,), (1,)), ((), ()))
NN = (((1,), (0,)), ((), ()))
MESH = pl.DeviceIdType.MESH
f32 = jnp.float32
bf16 = jnp.bfloat16


def split(value):
    high = value.astype(bf16)
    low = (value - high.astype(f32)).astype(bf16)
    return high, low


def harmonic(centre, neighbour):
    summed = centre + neighbour
    return 2.0 * centre * neighbour / jnp.where(summed > 0, summed, 1.0)


def basis_kernel(
    sizes, cells,
    rs, labels_hbm, flags_hbm, perm,
    v, last_gram, lead,
    stage, labels, flags, xl, xr, edge, yl, yr, kown, kxl, kxr, kyl, kyr, ct, cb,
    acc_lead, acc_last, lead_y, lead_z, lead_x, last_y, last_z, last_x,
    load_sem, ksend, krecv, xsend, xrecv, ysend, yrecv, asend, arecv,
):
    gx_n, gy_n, zg, xg = sizes
    gx = lax.axis_index("gx")
    gy = lax.axis_index("gy")
    right = lax.rem(gx + 1, gx_n)
    left = lax.rem(gx + gx_n - 1, gx_n)
    above = lax.rem(gy + 1, gy_n)
    below = lax.rem(gy + gy_n - 1, gy_n)
    zi = lax.rem(gx, zg)
    xi = lax.div(gx, zg)

    def z_peer(k):
        return (xi * zg + lax.rem(zi + k, zg), gy)

    def x_peer(k):
        return (lax.rem(xi + k, xg) * zg + zi, gy)

    def y_peer(k):
        return (gx, lax.rem(gy + k, gy_n))

    loads = [
        pltpu.make_async_copy(labels_hbm, labels, load_sem.at[CHUNKS]),
        pltpu.make_async_copy(flags_hbm, flags, load_sem.at[CHUNKS + 1]),
    ] + [
        pltpu.make_async_copy(
            rs.at[:, pl.ds(q * ROWS, ROWS), :], stage.reshape(CHUNKS, RHS, ROWS, BY).at[q], load_sem.at[q]
        )
        for q in range(CHUNKS)
    ]
    for load in loads:
        load.start()
    peers = [(right, gy), (left, gy)]
    peers += [y_peer(k) for k in range(1, gy_n)]
    peers += [z_peer(k) for k in range(1, zg)]
    peers += [x_peer(k) for k in range(1, xg)]
    barrier = pltpu.get_barrier_semaphore()
    for peer in peers:
        pl.semaphore_signal(barrier, inc=1, device_id=peer, device_id_type=MESH)

    loads[0].wait()
    loads[1].wait()
    for x in range(BX):
        label = labels[pl.ds(x, NZ, stride=BX), :]
        value = jnp.zeros((NZ, BY), f32)
        for region in range(perm.shape[0]):
            value = jnp.where(label == region, perm[region], value)
        kown[x] = value

    def remote(src, dst, send, recv, peer):
        return pltpu.make_async_remote_copy(
            src_ref=src, dst_ref=dst, send_sem=send, recv_sem=recv, device_id=peer, device_id_type=MESH
        )

    kcopies = [
        remote(kown.at[BX - 1], kxl, ksend.at[0], krecv.at[0], (right, gy)),
        remote(kown.at[0], kxr, ksend.at[1], krecv.at[1], (left, gy)),
        remote(kown, kyl, ksend.at[2], krecv.at[2], (gx, above)),
        remote(kown, kyr, ksend.at[3], krecv.at[3], (gx, below)),
    ]

    def copies_of(j, q):
        levels = pl.ds(q * LEVELS, LEVELS)
        plane = pl.ds(j * RHS, RHS)
        return [
            remote(v.at[levels, BX - 1, plane, :], xl.at[j, q], xsend.at[j, q, 0], xrecv.at[j, q, 0], (right, gy)),
            remote(v.at[levels, 0, plane, :], xr.at[j, q], xsend.at[j, q, 1], xrecv.at[j, q, 1], (left, gy)),
            remote(edge.at[j, q], yl.at[j, q], ysend.at[j, q, 0], yrecv.at[j, q, 0], (gx, above)),
            remote(edge.at[j, q], yr.at[j, q], ysend.at[j, q, 1], yrecv.at[j, q, 1], (gx, below)),
        ]

    lane = lax.broadcasted_iota(jnp.int32, (HALF, BY), 1)
    pair = lax.div(lane, 2)
    odd = lax.rem(lane, 2) == 1

    def pack(value, rr, packed):
        return jnp.where(pair == rr, pltpu.roll(value, 2 * rr + 1, 1), packed)

    for q in range(CHUNKS):
        loads[2 + q].wait()

    def relayout(q, carry):
        packed = [jnp.zeros((HALF, BY), f32) for _ in range(2)]
        for s in range(LEVELS):
            for x in range(BX):
                rr = s * BX + x
                value = stage[pl.ds(q * RHS * ROWS + rr, RHS, stride=ROWS), :]
                v[q * LEVELS + s, x, :RHS, :] = value
                for h in range(2):
                    packed[h] = pack(value[h * HALF : (h + 1) * HALF], rr, packed[h])
        for h in range(2):
            edge[0, q, h] = packed[h]
        return carry

    def first(q, carry):
        for copy in copies_of(0, q):
            copy.start()
        return carry

    lax.fori_loop(0, CHUNKS, relayout, 0)
    pl.semaphore_wait(barrier, len(peers))
    for copy in kcopies:
        copy.start()
    lax.fori_loop(0, CHUNKS, first, 0)

    for copy in kcopies:
        copy.wait_recv()
    wide_lane = lax.broadcasted_iota(jnp.int32, (NZ, BY), 1)
    level = lax.broadcasted_iota(jnp.int32, (NZ, BY), 0)
    for x in range(BX):
        centre = kown[x]
        xm = kown[x - 1] if x > 0 else jnp.where(gx == 0, 0.0, kxl[...])
        xp = kown[x + 1] if x < BX - 1 else jnp.where(gx == gx_n - 1, 0.0, kxr[...])
        from_below = jnp.where(gy == 0, 0.0, kyl[x])
        from_above = jnp.where(gy == gy_n - 1, 0.0, kyr[x])
        ym = jnp.where(wide_lane == 0, pltpu.roll(from_below, 1, 1), pltpu.roll(centre, 1, 1))
        yp = jnp.where(wide_lane == BY - 1, pltpu.roll(from_above, BY - 1, 1), pltpu.roll(centre, BY - 1, 1))
        zm = jnp.where(level == 0, 0.0, pltpu.roll(centre, 1, 0))
        zp = jnp.where(level == NZ - 1, 0.0, pltpu.roll(centre, NZ - 1, 0))
        t = [harmonic(centre, other) for other in (xm, xp, ym, yp, zm, zp)]
        bottom = flags[pl.ds(x, 1), :].astype(f32)
        top = flags[pl.ds(BX + x, 1), :].astype(f32)
        boundary = jnp.where(level == 0, 2.0 * centre * bottom, 0.0)
        boundary = boundary + jnp.where(level == NZ - 1, 2.0 * centre * top, 0.0)
        diagonal = t[0] + t[1] + t[2] + t[3] + t[4] + t[5] + boundary
        divisor = jnp.where(diagonal > 0, diagonal, 1.0)
        for n in range(6):
            ct[n, x] = -(t[n] / divisor)

    def spread(block, carry):
        for n in range(6):
            for x in range(BX):
                rows = ct[n, x, pl.ds(pl.multiple_of(block * 8, 8), 8), :]
                for s in range(8):
                    cb[block * 8 + s, x, n] = jnp.broadcast_to(rows[s : s + 1, :], (HALF, BY))
        return carry

    lax.fori_loop(0, NZ // 8, spread, 0)

    def advance(j, q):
        for copy in copies_of(j, q):
            copy.wait_recv()
        base = q * LEVELS
        merged = [
            jnp.where(odd, pltpu.roll(yl[j, q, h], 1, 1), pltpu.roll(yr[j, q, h], BY - 1, 1)) for h in range(2)
        ]
        packed = [jnp.zeros((HALF, BY), f32) for _ in range(2)]
        for s in range(LEVELS):
            z = base + s
            zm = lax.rem(z + NZ - 1, NZ) if s == 0 else z - 1
            zp = lax.rem(z + 1, NZ) if s == LEVELS - 1 else z + 1
            for x in range(BX):
                rr = s * BX + x
                coupling = [cb[z, x, n] for n in range(6)]
                for h in range(2):
                    here = pl.ds(j * RHS + h * HALF, HALF)
                    rows = pl.ds(h * HALF, HALF)
                    centre = v[z, x, here, :]
                    xm = v[z, x - 1, here, :] if x > 0 else xl[j, q, s, rows, :]
                    xp = v[z, x + 1, here, :] if x < BX - 1 else xr[j, q, s, rows, :]
                    ends = pltpu.roll(merged[h], BY - 1 - 2 * rr, 1)
                    ym = jnp.where(lane == 0, ends, pltpu.roll(centre, 1, 1))
                    yp = jnp.where(lane == BY - 1, ends, pltpu.roll(centre, BY - 1, 1))
                    summed = (
                        coupling[0] * xm
                        + coupling[1] * xp
                        + coupling[2] * ym
                        + coupling[3] * yp
                        + coupling[4] * v[zm, x, here, :]
                        + coupling[5] * v[zp, x, here, :]
                    )
                    value = summed if j == 0 else 2.0 * summed - v[z, x, pl.ds((j - 1) * RHS + h * HALF, HALF), :]
                    v[z, x, pl.ds((j + 1) * RHS + h * HALF, HALF), :] = value
                    if j < S - 1:
                        packed[h] = pack(value, rr, packed[h])
        if j < S - 1:
            for h in range(2):
                edge[j + 1, q, h] = packed[h]
            for copy in copies_of(j + 1, q):
                copy.start()

    def lead_products(q):
        total = jnp.zeros((LEAD, 2 * LEAD), f32)
        for s in range(LEVELS):
            wide = jnp.concatenate([v[q * LEVELS + s, x, :LEAD, :] for x in range(BX)], axis=1)
            high, low = split(wide)
            total = total + lax.dot_general(high, jnp.concatenate([high, low], axis=0), NT, preferred_element_type=f32)
        acc_lead[...] += total

    def last_products(q):
        total = jnp.zeros((2 * RHS, 2 * COLS), f32)
        for s in range(LEVELS):
            wide = jnp.concatenate([v[q * LEVELS + s, x] for x in range(BX)], axis=1)
            high, low = split(wide)
            total = total + lax.dot_general(
                jnp.concatenate([high[LEAD:], low[LEAD:]], axis=0),
                jnp.concatenate([high, low], axis=0),
                NT,
                preferred_element_type=f32,
            )
        acc_last[...] += total

    def exchange(phase, buffer, index, count, peer_of):
        return [
            remote(buffer.at[index], buffer.at[index], asend.at[phase, k - 1], arecv.at[phase, k - 1], peer_of(k))
            for k in range(1, count)
        ]

    steps_lead = [
        exchange(0, lead_y, gy, gy_n, y_peer),
        exchange(1, lead_z, zi, zg, z_peer),
        exchange(2, lead_x, xi, xg, x_peer),
    ]
    steps_last = [
        exchange(3, last_y, gy, gy_n, y_peer),
        exchange(4, last_z, zi, zg, z_peer),
        exchange(5, last_x, xi, xg, x_peer),
    ]

    def send(step):
        for copy in step:
            copy.start()

    def collect(step, buffer):
        for copy in step:
            copy.wait_recv()
        total = buffer[0]
        for k in range(1, len(step) + 1):
            total = total + buffer[k]
        return total

    acc_lead[...] = jnp.zeros_like(acc_lead)
    acc_last[...] = jnp.zeros_like(acc_last)

    def loop(j, more=None):
        def body(q, carry):
            advance(j, q)
            if more is not None:
                more(q)
            return carry

        lax.fori_loop(0, CHUNKS, body, 0)

    loop(0)
    loop(1)
    loop(2, lead_products)

    partial = acc_lead[...]
    mirrored = jnp.concatenate([partial, jnp.zeros((128 - LEAD, 128), f32)], axis=0).T[LEAD : 2 * LEAD]
    lead_lane = lax.broadcasted_iota(jnp.int32, (LEAD, 128), 1)
    partial = jnp.where(lead_lane < LEAD, partial + pltpu.roll(partial, LEAD, 1), 0.0) + mirrored
    lead_y[gy] = partial[: LEAD // 2] + pltpu.roll(partial[LEAD // 2 :], LEAD, 1)
    send(steps_lead[0])

    def beside(q):
        last_products(q)

        @pl.when(q == CHUNKS - 2)
        def _():
            lead_z[zi] = collect(steps_lead[0], lead_y)
            send(steps_lead[1])

    loop(3, beside)

    partial = acc_last[...]
    last_y[gy] = jnp.concatenate(
        [partial[:RHS, :COLS] + partial[:RHS, COLS:] + partial[RHS:, :COLS], jnp.zeros((RHS, 128 - COLS), f32)], axis=1
    )
    send(steps_last[0])
    last_z[zi] = collect(steps_last[0], last_y)
    send(steps_last[1])
    lead_x[xi] = collect(steps_lead[1], lead_z)
    send(steps_lead[2])
    last_x[xi] = collect(steps_last[1], last_z)
    send(steps_last[2])
    summed = collect(steps_lead[2], lead_x) * (1.0 / cells)
    summed = jnp.concatenate([summed, pltpu.roll(summed, LEAD, 1)], axis=0)
    rows, root = scale_start([summed[8 * b : 8 * b + 8] for b in range(LEAD // 8)], LEAD)
    lead[...] = jnp.concatenate(scale_end(eliminate(rows, 0, LEAD), root, LEAD), axis=0)
    last_gram[...] = collect(steps_last[2], last_x) * (1.0 / cells)

    for copy in kcopies:
        copy.wait_send()

    def drain(q, carry):
        for j in range(S):
            for copy in copies_of(j, q):
                copy.wait_send()
        return carry

    lax.fori_loop(0, CHUNKS, drain, 0)
    for step in steps_lead + steps_last:
        for copy in step:
            copy.wait_send()


def scale_start(blocks, size):
    lane = lax.broadcasted_iota(jnp.int32, (8, 128), 1)
    row = lax.broadcasted_iota(jnp.int32, (8, 128), 0)
    scales = []
    across = jnp.zeros((1, 128), f32)
    root = jnp.zeros((1, 128), f32)
    for b, block in enumerate(blocks):
        on = lane == row + 8 * b
        diagonal = jnp.sum(jnp.where(on, block, 0.0), axis=1, keepdims=True)
        rooted = jnp.sqrt(diagonal)
        scale = 1.0 / rooted
        scales.append(scale)
        across = across + jnp.sum(jnp.where(on, scale, 0.0), axis=0, keepdims=True)
        root = root + jnp.sum(jnp.where(on, rooted, 0.0), axis=0, keepdims=True)
    rows = [
        jnp.where(lane < size, block * scale * across, jnp.where(lane - size == row + 8 * b, scale, 0.0))
        for b, (block, scale) in enumerate(zip(blocks, scales))
    ]
    return rows, jnp.where(lane[:1] < size, root, 1.0)


def eliminate(rows, begin, end):
    rows = list(rows)
    sub = lax.broadcasted_iota(jnp.int32, (8, 128), 0)

    def along(block, k):
        return jnp.broadcast_to(block[:, k : k + 1], (8, 128))

    def down(block, k):
        return jnp.broadcast_to(block[k : k + 1, :], (8, 128))

    for k in range(begin, end, 2):
        b, s = divmod(k, 8)
        left = [along(block, k) for block in rows[b:]]
        right = [along(block, k + 1) for block in rows[b:]]
        first, second = down(rows[b], s), down(rows[b], s + 1)
        a, c, d = down(left[0], s), down(right[0], s), down(right[0], s + 1)
        inverse = 1.0 / (a * d - c * c)
        p0 = (d * first - c * second) * inverse
        p1 = (a * second - c * first) * inverse
        inner = (c / a) * first
        for i in range(b, len(rows)):
            change = left[i - b] * p0 + right[i - b] * p1
            if i == b:
                change = jnp.where(sub > s + 1, change, jnp.where(sub == s + 1, inner, 0.0))
            rows[i] = rows[i] - change
    return rows


def scale_end(rows, root, size):
    lane = lax.broadcasted_iota(jnp.int32, (8, 128), 1)
    row = lax.broadcasted_iota(jnp.int32, (8, 128), 0)
    done = []
    for b, block in enumerate(rows):
        diagonal = jnp.sum(jnp.where(lane == row + 8 * b, block, 0.0), axis=1, keepdims=True)
        block = jnp.where((lane >= row + 8 * b) & (lane - size <= row + 8 * b), block, 0.0)
        done.append(block * (1.0 / jnp.sqrt(diagonal)) * root)
    return done


def exact(a, b, dims):
    return lax.dot_general(a, b, dims, precision=lax.Precision.HIGHEST, preferred_element_type=f32)


def finish_kernel(v, last_gram, lead, out, r_out, stage, sems):
    upper = lead[:, :LEAD]
    inverse = lead[:, LEAD:]
    against = last_gram[:, :LEAD]
    cross = exact(against, inverse, NT)
    schur = last_gram[:, LEAD:COLS] - exact(cross, cross, NT)
    back = exact(cross, inverse, NN)
    padded = jnp.concatenate([schur, jnp.zeros((RHS, 128 - RHS), f32)], axis=1)
    rows, root = scale_start([padded[:8], padded[8:]], RHS)
    rows = scale_end(eliminate(rows, 0, RHS), root, RHS)
    corner = jnp.concatenate(rows, axis=0)
    corner_upper = corner[:, :RHS]
    corner_inverse = corner[:, RHS : 2 * RHS]
    back = -exact(corner_inverse, back, NN)

    tall = jnp.concatenate([cross, jnp.zeros((RHS, 128 - LEAD), f32)], axis=1)
    tall = jnp.concatenate([tall, jnp.zeros((128 - RHS, 128), f32)], axis=0).T[:LEAD, :RHS]
    r_out[...] = jnp.concatenate(
        [
            jnp.concatenate([upper, tall], axis=1),
            jnp.concatenate([jnp.zeros((RHS, LEAD), f32), corner_upper], axis=1),
        ],
        axis=0,
    )
    whole = jnp.concatenate(
        [
            jnp.concatenate([inverse, jnp.zeros((LEAD, 256 - LEAD), f32)], axis=1),
            jnp.concatenate([back, corner_inverse, jnp.zeros((RHS, 256 - COLS), f32)], axis=1),
        ],
        axis=0,
    )
    high = whole.astype(bf16).astype(f32)
    low = whole - high
    weights = high + pltpu.roll(high, COLS, 1) + pltpu.roll(low, 2 * COLS, 1)
    weights = weights[:, : 3 * COLS].astype(bf16)
    groups = 8
    per = NZ // groups
    copies = []
    for group in range(groups):
        def block(step, carry):
            for s in range(4):
                z = step * 4 + s
                for h in range(2):
                    both = jnp.concatenate([v[z, 2 * h], v[z, 2 * h + 1]], axis=1)
                    vh, vl = split(both)
                    q = jnp.dot(weights, jnp.concatenate([vh, vl, vh], axis=0), preferred_element_type=f32)
                    r = z * BX + 2 * h
                    stage[pl.ds(r, COLS, stride=PITCH), :] = q[:, :BY]
                    stage[pl.ds(r + 1, COLS, stride=PITCH), :] = q[:, BY:]
            return carry

        lax.fori_loop(group * per // 4, (group + 1) * per // 4, block, 0)
        rows = pl.ds(group * per * BX, per * BX)
        copy = pltpu.make_async_copy(
            stage.reshape(COLS, PITCH, BY).at[:, rows, :], out.at[:, rows, :], sems.at[group]
        )
        copy.start()
        copies.append(copy)
    for copy in copies:
        copy.wait()


def per_device(sizes, cells, right_sides, region_labels, face_flags, region_perm):
    gx_n, gy_n, zg, xg = sizes
    vmem = pl.BlockSpec(memory_space=pltpu.VMEM)
    hbm = pl.BlockSpec(memory_space=pltpu.HBM)
    scratch = [
        (CHUNKS * RHS * ROWS, BY),
        (NZ * BX, BY, jnp.int32),
        (2 * BX, BY, jnp.int32),
        (S, CHUNKS, LEVELS, RHS, BY),
        (S, CHUNKS, LEVELS, RHS, BY),
        (S, CHUNKS, 2, HALF, BY),
        (S, CHUNKS, 2, HALF, BY),
        (S, CHUNKS, 2, HALF, BY),
        (BX, NZ, BY),
        (NZ, BY),
        (NZ, BY),
        (BX, NZ, BY),
        (BX, NZ, BY),
        (6, BX, NZ, BY),
        (NZ, BX, 6, HALF, BY),
        (LEAD, 2 * LEAD),
        (2 * RHS, 2 * COLS),
        (gy_n, LEAD // 2, 128),
        (zg, LEAD // 2, 128),
        (xg, LEAD // 2, 128),
        (gy_n, RHS, 128),
        (zg, RHS, 128),
        (xg, RHS, 128),
    ]
    scratch = [
        pltpu.VMEM(shape[:-1], shape[-1]) if shape[-1] is jnp.int32 else pltpu.VMEM(shape, f32) for shape in scratch
    ]
    dma = pltpu.SemaphoreType.DMA
    scratch += [dma((CHUNKS + 2,)), dma((4,)), dma((4,))]
    scratch += [dma((S, CHUNKS, 2)) for _ in range(4)] + [dma((6, 8)), dma((6, 8))]
    v, last_gram, lead = pl.pallas_call(
        functools.partial(basis_kernel, sizes, cells),
        out_shape=(
            pltpu.VMEM((NZ, BX, COLS, BY), f32),
            pltpu.VMEM((RHS, 128), f32),
            pltpu.VMEM((LEAD, 2 * LEAD), f32),
        ),
        in_specs=[hbm, hbm, hbm, pl.BlockSpec(memory_space=pltpu.SMEM)],
        out_specs=(vmem, vmem, vmem),
        scratch_shapes=scratch,
        compiler_params=pltpu.CompilerParams(
            collective_id=0, has_side_effects=True, vmem_limit_bytes=40 * 1024 * 1024
        ),
        name="basis",
    )(
        *(pltpu.with_memory_space_constraint(a, pltpu.HBM) for a in (
            right_sides.reshape(RHS, NZ * BX, BY),
            region_labels.reshape(NZ * BX, BY),
            face_flags.reshape(2 * BX, BY),
            region_perm,
        )),
    )
    out, upper = pl.pallas_call(
        finish_kernel,
        out_shape=(
            jax.ShapeDtypeStruct((COLS, NZ * BX, BY), f32),
            jax.ShapeDtypeStruct((COLS, COLS), f32),
        ),
        in_specs=[vmem, vmem, vmem],
        out_specs=(hbm, vmem),
        scratch_shapes=[pltpu.VMEM((COLS * PITCH, BY), f32), dma((8,))],
        compiler_params=pltpu.CompilerParams(vmem_limit_bytes=40 * 1024 * 1024),
        name="finish",
    )(v, last_gram, lead)
    return out.reshape(COLS, NZ, BX, BY), upper


def solution(mesh):
    gx_n, gy_n = mesh.shape["gx"], mesh.shape["gy"]
    zg = 8 if gx_n % 8 == 0 else 2
    sizes = (gx_n, gy_n, zg, gx_n // zg)
    cells = NZ * BX * BY * gx_n * gy_n
    placed = (P(None, None, "gx", "gy"), P(None, "gx", "gy"), P(None, "gx", "gy"), P())
    return jax.shard_map(
        functools.partial(per_device, sizes, cells),
        mesh=mesh,
        in_specs=placed,
        out_specs=(P(None, None, "gx", "gy"), P()),
        check_vma=False,
    )
```

```python
import functools
import jax
import jax.numpy as jnp
from jax import lax
from jax.experimental import pallas as pl
from jax.experimental.pallas import tpu as pltpu
from jax.sharding import PartitionSpec as P

RHS = 16
S = 4
VECS = S + 1
COLS = RHS * VECS
NZ = 32
BX = 4
BY = 128
HALF = 8
LEAD = RHS * S
LEVELS = 8
CHUNKS = NZ // LEVELS
ROWS = LEVELS * BX
PITCH = NZ * BX + 8
NT = (((1,), (1,)), ((), ()))
NN = (((1,), (0,)), ((), ()))
MESH = pl.DeviceIdType.MESH
f32 = jnp.float32
bf16 = jnp.bfloat16


def split(value):
    high = value.astype(bf16)
    low = (value - high.astype(f32)).astype(bf16)
    return high, low


def harmonic(centre, neighbour):
    summed = centre + neighbour
    return 2.0 * centre * neighbour / jnp.where(summed > 0, summed, 1.0)


def basis_kernel(
    sizes, cells,
    rs, labels_hbm, flags_hbm, perm,
    v, last_gram, lead,
    stage, labels, flags, xl, xr, edge, yl, yr, kown, kedge, kxl, kxr, kyl, kyr, ct, cb,
    acc_lead, acc_last, lead_y, lead_z, lead_x, last_y, last_z, last_x,
    load_sem, ksend, krecv, xsend, xrecv, ysend, yrecv, asend, arecv,
):
    gx_n, gy_n, zg, xg = sizes
    gx = lax.axis_index("gx")
    gy = lax.axis_index("gy")
    right = lax.rem(gx + 1, gx_n)
    left = lax.rem(gx + gx_n - 1, gx_n)
    above = lax.rem(gy + 1, gy_n)
    below = lax.rem(gy + gy_n - 1, gy_n)
    zi = lax.rem(gx, zg)
    xi = lax.div(gx, zg)

    def z_peer(k):
        return (xi * zg + lax.rem(zi + k, zg), gy)

    def x_peer(k):
        return (lax.rem(xi + k, xg) * zg + zi, gy)

    def y_peer(k):
        return (gx, lax.rem(gy + k, gy_n))

    loads = [
        pltpu.make_async_copy(labels_hbm, labels, load_sem.at[CHUNKS]),
        pltpu.make_async_copy(flags_hbm, flags, load_sem.at[CHUNKS + 1]),
    ]

    def load_of(q):
        return pltpu.make_async_copy(
            rs.at[:, pl.ds(q * ROWS, ROWS), :], stage.reshape(CHUNKS, RHS, ROWS, BY).at[q], load_sem.at[q]
        )

    loads += [load_of(q) for q in range(CHUNKS)]
    for load in loads:
        load.start()
    peers = [z_peer(k) for k in sorted(range(1, zg), key=lambda k: abs(k - zg // 2))]
    peers += [y_peer(k) for k in sorted(range(1, gy_n), key=lambda k: abs(k - gy_n // 2))]
    peers += [x_peer(k) for k in range(1, xg)]
    peers += [(right, gy), (left, gy)]
    barrier = pltpu.get_barrier_semaphore()
    for peer in peers:
        pl.semaphore_signal(barrier, inc=1, device_id=peer, device_id_type=MESH)

    loads[0].wait()
    loads[1].wait()
    for x in range(BX):
        label = labels[pl.ds(x, NZ, stride=BX), :]
        value = jnp.zeros((NZ, BY), f32)
        for region in range(perm.shape[0]):
            value = jnp.where(label == region, perm[region], value)
        kown[x] = value

    def remote(src, dst, send, recv, peer):
        return pltpu.make_async_remote_copy(
            src_ref=src, dst_ref=dst, send_sem=send, recv_sem=recv, device_id=peer, device_id_type=MESH
        )

    wide_lane = lax.broadcasted_iota(jnp.int32, (NZ, BY), 1)
    kends = jnp.zeros((NZ, BY), f32)
    for x in range(BX):
        kends = jnp.where(lax.div(wide_lane, 2) == x, pltpu.roll(kown[x], 2 * x + 1, 1), kends)
    kedge[...] = kends
    kcopies = [
        remote(kedge, kyl, ksend.at[2], krecv.at[2], (gx, above)),
        remote(kedge, kyr, ksend.at[3], krecv.at[3], (gx, below)),
        remote(kown.at[BX - 1], kxl, ksend.at[0], krecv.at[0], (right, gy)),
        remote(kown.at[0], kxr, ksend.at[1], krecv.at[1], (left, gy)),
    ]

    def copies_of(j, q):
        levels = pl.ds(q * LEVELS, LEVELS)
        plane = pl.ds(j * RHS, RHS)
        return [
            remote(v.at[levels, BX - 1, plane, :], xl.at[j, q], xsend.at[j, q, 0], xrecv.at[j, q, 0], (right, gy)),
            remote(v.at[levels, 0, plane, :], xr.at[j, q], xsend.at[j, q, 1], xrecv.at[j, q, 1], (left, gy)),
            remote(edge.at[j, q], yl.at[j, q], ysend.at[j, q, 0], yrecv.at[j, q, 0], (gx, above)),
            remote(edge.at[j, q], yr.at[j, q], ysend.at[j, q, 1], yrecv.at[j, q, 1], (gx, below)),
        ]

    lane = lax.broadcasted_iota(jnp.int32, (HALF, BY), 1)
    pair = lax.div(lane, 2)
    odd = lax.rem(lane, 2) == 1

    def pack(value, rr, packed):
        return jnp.where(pair == rr, pltpu.roll(value, 2 * rr + 1, 1), packed)

    def relayout(q, carry):
        load_of(q).wait()
        packed = [jnp.zeros((HALF, BY), f32) for _ in range(2)]
        for s in range(LEVELS):
            for x in range(BX):
                rr = s * BX + x
                value = stage[pl.ds(q * RHS * ROWS + rr, RHS, stride=ROWS), :]
                v[q * LEVELS + s, x, :RHS, :] = value
                for h in range(2):
                    packed[h] = pack(value[h * HALF : (h + 1) * HALF], rr, packed[h])
        for h in range(2):
            edge[0, q, h] = packed[h]

        @pl.when(q == 0)
        def _():
            pl.semaphore_wait(barrier, len(peers))
            for copy in kcopies:
                copy.start()

        for copy in copies_of(0, q):
            copy.start()
        return carry

    lax.fori_loop(0, CHUNKS, relayout, 0)

    for copy in kcopies:
        copy.wait_recv()
    level = lax.broadcasted_iota(jnp.int32, (NZ, BY), 0)
    merged = jnp.where(lax.rem(wide_lane, 2) == 1, pltpu.roll(kyl[...], 1, 1), pltpu.roll(kyr[...], BY - 1, 1))
    for x in range(BX):
        centre = kown[x]
        xm = kown[x - 1] if x > 0 else jnp.where(gx == 0, 0.0, kxl[...])
        xp = kown[x + 1] if x < BX - 1 else jnp.where(gx == gx_n - 1, 0.0, kxr[...])
        ends = pltpu.roll(merged, BY - 1 - 2 * x, 1)
        from_below = jnp.where(gy == 0, 0.0, ends)
        from_above = jnp.where(gy == gy_n - 1, 0.0, ends)
        ym = jnp.where(wide_lane == 0, from_below, pltpu.roll(centre, 1, 1))
        yp = jnp.where(wide_lane == BY - 1, from_above, pltpu.roll(centre, BY - 1, 1))
        zm = jnp.where(level == 0, 0.0, pltpu.roll(centre, 1, 0))
        zp = jnp.where(level == NZ - 1, 0.0, pltpu.roll(centre, NZ - 1, 0))
        t = [harmonic(centre, other) for other in (xm, xp, ym, yp, zm, zp)]
        bottom = flags[pl.ds(x, 1), :].astype(f32)
        top = flags[pl.ds(BX + x, 1), :].astype(f32)
        boundary = jnp.where(level == 0, 2.0 * centre * bottom, 0.0)
        boundary = boundary + jnp.where(level == NZ - 1, 2.0 * centre * top, 0.0)
        diagonal = t[0] + t[1] + t[2] + t[3] + t[4] + t[5] + boundary
        divisor = jnp.where(diagonal > 0, diagonal, 1.0)
        for n in range(6):
            ct[n, x] = -(t[n] / divisor)

    def spread(block, carry):
        for n in range(6):
            for x in range(BX):
                rows = ct[n, x, pl.ds(pl.multiple_of(block * 8, 8), 8), :]
                for s in range(8):
                    cb[block * 8 + s, x, n] = jnp.broadcast_to(rows[s : s + 1, :], (HALF, BY))
        return carry

    lax.fori_loop(0, NZ // 8, spread, 0)

    def advance(j, q):
        for copy in copies_of(j, q):
            copy.wait_recv()
        base = q * LEVELS
        merged = [
            jnp.where(odd, pltpu.roll(yl[j, q, h], 1, 1), pltpu.roll(yr[j, q, h], BY - 1, 1)) for h in range(2)
        ]
        packed = [jnp.zeros((HALF, BY), f32) for _ in range(2)]
        for s in range(LEVELS):
            z = base + s
            zm = lax.rem(z + NZ - 1, NZ) if s == 0 else z - 1
            zp = lax.rem(z + 1, NZ) if s == LEVELS - 1 else z + 1
            for x in range(BX):
                rr = s * BX + x
                coupling = [cb[z, x, n] for n in range(6)]
                for h in range(2):
                    here = pl.ds(j * RHS + h * HALF, HALF)
                    rows = pl.ds(h * HALF, HALF)
                    centre = v[z, x, here, :]
                    xm = v[z, x - 1, here, :] if x > 0 else xl[j, q, s, rows, :]
                    xp = v[z, x + 1, here, :] if x < BX - 1 else xr[j, q, s, rows, :]
                    ends = pltpu.roll(merged[h], BY - 1 - 2 * rr, 1)
                    ym = jnp.where(lane == 0, ends, pltpu.roll(centre, 1, 1))
                    yp = jnp.where(lane == BY - 1, ends, pltpu.roll(centre, BY - 1, 1))
                    summed = (
                        coupling[0] * xm
                        + coupling[1] * xp
                        + coupling[2] * ym
                        + coupling[3] * yp
                        + coupling[4] * v[zm, x, here, :]
                        + coupling[5] * v[zp, x, here, :]
                    )
                    value = summed if j == 0 else 2.0 * summed - v[z, x, pl.ds((j - 1) * RHS + h * HALF, HALF), :]
                    v[z, x, pl.ds((j + 1) * RHS + h * HALF, HALF), :] = value
                    if j < S - 1:
                        packed[h] = pack(value, rr, packed[h])
        if j < S - 1:
            for h in range(2):
                edge[j + 1, q, h] = packed[h]
            for copy in copies_of(j + 1, q):
                copy.start()

    def lead_products(q):
        total = jnp.zeros((LEAD, 2 * LEAD), f32)
        for s in range(LEVELS):
            wide = jnp.concatenate([v[q * LEVELS + s, x, :LEAD, :] for x in range(BX)], axis=1)
            high, low = split(wide)
            total = total + lax.dot_general(high, jnp.concatenate([high, low], axis=0), NT, preferred_element_type=f32)
        acc_lead[...] += total

    def last_products(q):
        total = jnp.zeros((2 * RHS, 2 * COLS), f32)
        for s in range(LEVELS):
            wide = jnp.concatenate([v[q * LEVELS + s, x] for x in range(BX)], axis=1)
            high, low = split(wide)
            total = total + lax.dot_general(
                jnp.concatenate([high[LEAD:], low[LEAD:]], axis=0),
                jnp.concatenate([high, low], axis=0),
                NT,
                preferred_element_type=f32,
            )
        acc_last[...] += total

    def exchange(phase, buffer, index, count, peer_of):
        return [
            remote(buffer.at[index], buffer.at[index], asend.at[phase, k - 1], arecv.at[phase, k - 1], peer_of(k))
            for k in range(1, count)
        ]

    steps_lead = [
        exchange(0, lead_y, gy, gy_n, y_peer),
        exchange(1, lead_z, zi, zg, z_peer),
        exchange(2, lead_x, xi, xg, x_peer),
    ]
    steps_last = [
        exchange(3, last_y, gy, gy_n, y_peer),
        exchange(4, last_z, zi, zg, z_peer),
        exchange(5, last_x, xi, xg, x_peer),
    ]

    def send(step):
        for copy in step:
            copy.start()

    def collect(step, buffer):
        for copy in step:
            copy.wait_recv()
        total = buffer[0]
        for k in range(1, len(step) + 1):
            total = total + buffer[k]
        return total

    acc_lead[...] = jnp.zeros_like(acc_lead)
    acc_last[...] = jnp.zeros_like(acc_last)

    def loop(j, more=None):
        def body(q, carry):
            advance(j, q)
            if more is not None:
                more(q)
            return carry

        lax.fori_loop(0, CHUNKS, body, 0)

    loop(0)
    loop(1)
    loop(2, lead_products)

    partial = acc_lead[...]
    mirrored = jnp.concatenate([partial, jnp.zeros((128 - LEAD, 128), f32)], axis=0).T[LEAD : 2 * LEAD]
    lead_lane = lax.broadcasted_iota(jnp.int32, (LEAD, 128), 1)
    partial = jnp.where(lead_lane < LEAD, partial + pltpu.roll(partial, LEAD, 1), 0.0) + mirrored
    lead_y[gy] = partial[: LEAD // 2] + pltpu.roll(partial[LEAD // 2 :], LEAD, 1)
    send(steps_lead[0])

    def beside(q):
        last_products(q)

        @pl.when(q == CHUNKS - 2)
        def _():
            lead_z[zi] = collect(steps_lead[0], lead_y)
            send(steps_lead[1])

    loop(3, beside)

    partial = acc_last[...]
    last_y[gy] = jnp.concatenate(
        [partial[:RHS, :COLS] + partial[:RHS, COLS:] + partial[RHS:, :COLS], jnp.zeros((RHS, 128 - COLS), f32)], axis=1
    )
    send(steps_last[0])
    last_z[zi] = collect(steps_last[0], last_y)
    send(steps_last[1])
    lead_x[xi] = collect(steps_lead[1], lead_z)
    send(steps_lead[2])
    last_x[xi] = collect(steps_last[1], last_z)
    send(steps_last[2])
    summed = collect(steps_lead[2], lead_x) * (1.0 / cells)
    summed = jnp.concatenate([summed, pltpu.roll(summed, LEAD, 1)], axis=0)
    rows, root = scale_start([summed[8 * b : 8 * b + 8] for b in range(LEAD // 8)], LEAD)
    lead[...] = jnp.concatenate(scale_end(eliminate(rows, 0, LEAD), root, LEAD), axis=0)
    last_gram[...] = collect(steps_last[2], last_x) * (1.0 / cells)

    for copy in kcopies:
        copy.wait_send()

    def drain(q, carry):
        for j in range(S):
            for copy in copies_of(j, q):
                copy.wait_send()
        return carry

    lax.fori_loop(0, CHUNKS, drain, 0)
    for step in steps_lead + steps_last:
        for copy in step:
            copy.wait_send()


def scale_start(blocks, size):
    lane = lax.broadcasted_iota(jnp.int32, (8, 128), 1)
    row = lax.broadcasted_iota(jnp.int32, (8, 128), 0)
    scales = []
    across = jnp.zeros((1, 128), f32)
    root = jnp.zeros((1, 128), f32)
    for b, block in enumerate(blocks):
        on = lane == row + 8 * b
        diagonal = jnp.sum(jnp.where(on, block, 0.0), axis=1, keepdims=True)
        rooted = jnp.sqrt(diagonal)
        scale = 1.0 / rooted
        scales.append(scale)
        across = across + jnp.sum(jnp.where(on, scale, 0.0), axis=0, keepdims=True)
        root = root + jnp.sum(jnp.where(on, rooted, 0.0), axis=0, keepdims=True)
    rows = [
        jnp.where(lane < size, block * scale * across, jnp.where(lane - size == row + 8 * b, scale, 0.0))
        for b, (block, scale) in enumerate(zip(blocks, scales))
    ]
    return rows, jnp.where(lane[:1] < size, root, 1.0)


def eliminate(rows, begin, end):
    rows = list(rows)
    sub = lax.broadcasted_iota(jnp.int32, (8, 128), 0)

    def along(block, k):
        return jnp.broadcast_to(block[:, k : k + 1], (8, 128))

    def down(block, k):
        return jnp.broadcast_to(block[k : k + 1, :], (8, 128))

    for k in range(begin, end, 2):
        b, s = divmod(k, 8)
        left = [along(block, k) for block in rows[b:]]
        right = [along(block, k + 1) for block in rows[b:]]
        first, second = down(rows[b], s), down(rows[b], s + 1)
        a, c, d = down(left[0], s), down(right[0], s), down(right[0], s + 1)
        inverse = 1.0 / (a * d - c * c)
        p0 = (d * first - c * second) * inverse
        p1 = (a * second - c * first) * inverse
        inner = (c / a) * first
        for i in range(b, len(rows)):
            change = left[i - b] * p0 + right[i - b] * p1
            if i == b:
                change = jnp.where(sub > s + 1, change, jnp.where(sub == s + 1, inner, 0.0))
            rows[i] = rows[i] - change
    return rows


def scale_end(rows, root, size):
    lane = lax.broadcasted_iota(jnp.int32, (8, 128), 1)
    row = lax.broadcasted_iota(jnp.int32, (8, 128), 0)
    done = []
    for b, block in enumerate(rows):
        diagonal = jnp.sum(jnp.where(lane == row + 8 * b, block, 0.0), axis=1, keepdims=True)
        block = jnp.where((lane >= row + 8 * b) & (lane - size <= row + 8 * b), block, 0.0)
        done.append(block * (1.0 / jnp.sqrt(diagonal)) * root)
    return done


def exact(a, b, dims):
    return lax.dot_general(a, b, dims, precision=lax.Precision.HIGHEST, preferred_element_type=f32)


def finish_kernel(v, last_gram, lead, out, r_out, stage, sems):
    upper = lead[:, :LEAD]
    inverse = lead[:, LEAD:]
    against = last_gram[:, :LEAD]
    cross = exact(against, inverse, NT)
    schur = last_gram[:, LEAD:COLS] - exact(cross, cross, NT)
    back = exact(cross, inverse, NN)
    padded = jnp.concatenate([schur, jnp.zeros((RHS, 128 - RHS), f32)], axis=1)
    rows, root = scale_start([padded[:8], padded[8:]], RHS)
    rows = scale_end(eliminate(rows, 0, RHS), root, RHS)
    corner = jnp.concatenate(rows, axis=0)
    corner_upper = corner[:, :RHS]
    corner_inverse = corner[:, RHS : 2 * RHS]
    back = -exact(corner_inverse, back, NN)

    tall = jnp.concatenate([cross, jnp.zeros((RHS, 128 - LEAD), f32)], axis=1)
    tall = jnp.concatenate([tall, jnp.zeros((128 - RHS, 128), f32)], axis=0).T[:LEAD, :RHS]
    r_out[...] = jnp.concatenate(
        [
            jnp.concatenate([upper, tall], axis=1),
            jnp.concatenate([jnp.zeros((RHS, LEAD), f32), corner_upper], axis=1),
        ],
        axis=0,
    )
    whole = jnp.concatenate(
        [
            jnp.concatenate([inverse, jnp.zeros((LEAD, 256 - LEAD), f32)], axis=1),
            jnp.concatenate([back, corner_inverse, jnp.zeros((RHS, 256 - COLS), f32)], axis=1),
        ],
        axis=0,
    )
    high = whole.astype(bf16).astype(f32)
    low = whole - high
    weights = high + pltpu.roll(high, COLS, 1) + pltpu.roll(low, 2 * COLS, 1)
    weights = weights[:, : 3 * COLS].astype(bf16)
    groups = 8
    per = NZ // groups
    copies = []
    for group in range(groups):
        def block(step, carry):
            for s in range(4):
                z = step * 4 + s
                for h in range(2):
                    both = jnp.concatenate([v[z, 2 * h], v[z, 2 * h + 1]], axis=1)
                    vh, vl = split(both)
                    q = jnp.dot(weights, jnp.concatenate([vh, vl, vh], axis=0), preferred_element_type=f32)
                    r = z * BX + 2 * h
                    stage[pl.ds(r, COLS, stride=PITCH), :] = q[:, :BY]
                    stage[pl.ds(r + 1, COLS, stride=PITCH), :] = q[:, BY:]
            return carry

        lax.fori_loop(group * per // 4, (group + 1) * per // 4, block, 0)
        rows = pl.ds(group * per * BX, per * BX)
        copy = pltpu.make_async_copy(
            stage.reshape(COLS, PITCH, BY).at[:, rows, :], out.at[:, rows, :], sems.at[group]
        )
        copy.start()
        copies.append(copy)
    for copy in copies:
        copy.wait()


def per_device(sizes, cells, right_sides, region_labels, face_flags, region_perm):
    gx_n, gy_n, zg, xg = sizes
    vmem = pl.BlockSpec(memory_space=pltpu.VMEM)
    hbm = pl.BlockSpec(memory_space=pltpu.HBM)
    scratch = [
        (CHUNKS * RHS * ROWS, BY),
        (NZ * BX, BY, jnp.int32),
        (2 * BX, BY, jnp.int32),
        (S, CHUNKS, LEVELS, RHS, BY),
        (S, CHUNKS, LEVELS, RHS, BY),
        (S, CHUNKS, 2, HALF, BY),
        (S, CHUNKS, 2, HALF, BY),
        (S, CHUNKS, 2, HALF, BY),
        (BX, NZ, BY),
        (NZ, BY),
        (NZ, BY),
        (NZ, BY),
        (NZ, BY),
        (NZ, BY),
        (6, BX, NZ, BY),
        (NZ, BX, 6, HALF, BY),
        (LEAD, 2 * LEAD),
        (2 * RHS, 2 * COLS),
        (gy_n, LEAD // 2, 128),
        (zg, LEAD // 2, 128),
        (xg, LEAD // 2, 128),
        (gy_n, RHS, 128),
        (zg, RHS, 128),
        (xg, RHS, 128),
    ]
    scratch = [
        pltpu.VMEM(shape[:-1], shape[-1]) if shape[-1] is jnp.int32 else pltpu.VMEM(shape, f32) for shape in scratch
    ]
    dma = pltpu.SemaphoreType.DMA
    scratch += [dma((CHUNKS + 2,)), dma((4,)), dma((4,))]
    scratch += [dma((S, CHUNKS, 2)) for _ in range(4)] + [dma((6, 8)), dma((6, 8))]
    v, last_gram, lead = pl.pallas_call(
        functools.partial(basis_kernel, sizes, cells),
        out_shape=(
            pltpu.VMEM((NZ, BX, COLS, BY), f32),
            pltpu.VMEM((RHS, 128), f32),
            pltpu.VMEM((LEAD, 2 * LEAD), f32),
        ),
        in_specs=[hbm, hbm, hbm, pl.BlockSpec(memory_space=pltpu.SMEM)],
        out_specs=(vmem, vmem, vmem),
        scratch_shapes=scratch,
        compiler_params=pltpu.CompilerParams(
            collective_id=0, has_side_effects=True, vmem_limit_bytes=40 * 1024 * 1024
        ),
        name="basis",
    )(
        *(pltpu.with_memory_space_constraint(a, pltpu.HBM) for a in (
            right_sides.reshape(RHS, NZ * BX, BY),
            region_labels.reshape(NZ * BX, BY),
            face_flags.reshape(2 * BX, BY),
            region_perm,
        )),
    )
    out, upper = pl.pallas_call(
        finish_kernel,
        out_shape=(
            jax.ShapeDtypeStruct((COLS, NZ * BX, BY), f32),
            jax.ShapeDtypeStruct((COLS, COLS), f32),
        ),
        in_specs=[vmem, vmem, vmem],
        out_specs=(hbm, vmem),
        scratch_shapes=[pltpu.VMEM((COLS * PITCH, BY), f32), dma((8,))],
        compiler_params=pltpu.CompilerParams(vmem_limit_bytes=40 * 1024 * 1024),
        name="finish",
    )(v, last_gram, lead)
    return out.reshape(COLS, NZ, BX, BY), upper


def solution(mesh):
    gx_n, gy_n = mesh.shape["gx"], mesh.shape["gy"]
    zg = 8 if gx_n % 8 == 0 else 2
    sizes = (gx_n, gy_n, zg, gx_n // zg)
    cells = NZ * BX * BY * gx_n * gy_n
    placed = (P(None, None, "gx", "gy"), P(None, "gx", "gy"), P(None, "gx", "gy"), P())
    return jax.shard_map(
        functools.partial(per_device, sizes, cells),
        mesh=mesh,
        in_specs=placed,
        out_specs=(P(None, None, "gx", "gy"), P()),
        check_vma=False,
    )
```

```python
import functools
import jax
import jax.numpy as jnp
from jax import lax
from jax.experimental import pallas as pl
from jax.experimental.pallas import tpu as pltpu
from jax.sharding import PartitionSpec as P

RHS = 16
S = 4
VECS = S + 1
COLS = RHS * VECS
NZ = 32
BX = 4
BY = 128
HALF = 8
LEAD = RHS * S
LEVELS = 8
CHUNKS = NZ // LEVELS
ROWS = LEVELS * BX
PITCH = NZ * BX + 8
NT = (((1,), (1,)), ((), ()))
NN = (((1,), (0,)), ((), ()))
MESH = pl.DeviceIdType.MESH
f32 = jnp.float32
bf16 = jnp.bfloat16


def split(value):
    high = value.astype(bf16)
    low = (value - high.astype(f32)).astype(bf16)
    return high, low


def harmonic(centre, neighbour):
    summed = centre + neighbour
    return 2.0 * centre * neighbour / jnp.where(summed > 0, summed, 1.0)


def basis_kernel(
    sizes, cells,
    rs, labels_hbm, flags_hbm, perm,
    v, last_gram, lead,
    stage, labels, flags, xl, xr, edge, yl, yr, kown, kedge, kxl, kxr, kyl, kyr, ct, cb,
    acc_lead, acc_last, lead_own, lead_y, lead_z, lead_x, lead_all, last_y, last_z, last_x,
    load_sem, ksend, krecv, xsend, xrecv, ysend, yrecv, asend, arecv,
):
    gx_n, gy_n, zg, xg = sizes
    gx = lax.axis_index("gx")
    gy = lax.axis_index("gy")
    right = lax.rem(gx + 1, gx_n)
    left = lax.rem(gx + gx_n - 1, gx_n)
    above = lax.rem(gy + 1, gy_n)
    below = lax.rem(gy + gy_n - 1, gy_n)
    zi = lax.rem(gx, zg)
    xi = lax.div(gx, zg)

    def z_peer(k):
        return (xi * zg + lax.rem(zi + k, zg), gy)

    def x_peer(k):
        return (lax.rem(xi + k, xg) * zg + zi, gy)

    def y_peer(k):
        return (gx, lax.rem(gy + k, gy_n))

    loads = [
        pltpu.make_async_copy(labels_hbm, labels, load_sem.at[CHUNKS]),
        pltpu.make_async_copy(flags_hbm, flags, load_sem.at[CHUNKS + 1]),
    ]

    def load_of(q):
        return pltpu.make_async_copy(
            rs.at[:, pl.ds(q * ROWS, ROWS), :], stage.reshape(CHUNKS, RHS, ROWS, BY).at[q], load_sem.at[q]
        )

    loads += [load_of(q) for q in range(CHUNKS)]
    for load in loads:
        load.start()
    peers = [z_peer(k) for k in sorted(range(1, zg), key=lambda k: abs(k - zg // 2))]
    peers += [y_peer(k) for k in sorted(range(1, gy_n), key=lambda k: abs(k - gy_n // 2))]
    peers += [x_peer(k) for k in range(1, xg)]
    peers += [(right, gy), (left, gy)]
    barrier = pltpu.get_barrier_semaphore()
    for peer in peers:
        pl.semaphore_signal(barrier, inc=1, device_id=peer, device_id_type=MESH)

    loads[0].wait()
    loads[1].wait()
    for x in range(BX):
        label = labels[pl.ds(x, NZ, stride=BX), :]
        value = jnp.zeros((NZ, BY), f32)
        for region in range(perm.shape[0]):
            value = jnp.where(label == region, perm[region], value)
        kown[x] = value

    def remote(src, dst, send, recv, peer):
        return pltpu.make_async_remote_copy(
            src_ref=src, dst_ref=dst, send_sem=send, recv_sem=recv, device_id=peer, device_id_type=MESH
        )

    wide_lane = lax.broadcasted_iota(jnp.int32, (NZ, BY), 1)
    kends = jnp.zeros((NZ, BY), f32)
    for x in range(BX):
        kends = jnp.where(lax.div(wide_lane, 2) == x, pltpu.roll(kown[x], 2 * x + 1, 1), kends)
    kedge[...] = kends
    kcopies = [
        remote(kedge, kyl, ksend.at[2], krecv.at[2], (gx, above)),
        remote(kedge, kyr, ksend.at[3], krecv.at[3], (gx, below)),
        remote(kown.at[BX - 1], kxl, ksend.at[0], krecv.at[0], (right, gy)),
        remote(kown.at[0], kxr, ksend.at[1], krecv.at[1], (left, gy)),
    ]

    def copies_of(j, q):
        levels = pl.ds(q * LEVELS, LEVELS)
        plane = pl.ds(j * RHS, RHS)
        return [
            remote(v.at[levels, BX - 1, plane, :], xl.at[j, q], xsend.at[j, q, 0], xrecv.at[j, q, 0], (right, gy)),
            remote(v.at[levels, 0, plane, :], xr.at[j, q], xsend.at[j, q, 1], xrecv.at[j, q, 1], (left, gy)),
            remote(edge.at[j, q], yl.at[j, q], ysend.at[j, q, 0], yrecv.at[j, q, 0], (gx, above)),
            remote(edge.at[j, q], yr.at[j, q], ysend.at[j, q, 1], yrecv.at[j, q, 1], (gx, below)),
        ]

    lane = lax.broadcasted_iota(jnp.int32, (HALF, BY), 1)
    pair = lax.div(lane, 2)
    odd = lax.rem(lane, 2) == 1

    def pack(value, rr, packed):
        return jnp.where(pair == rr, pltpu.roll(value, 2 * rr + 1, 1), packed)

    def relayout(q, carry):
        load_of(q).wait()
        packed = [jnp.zeros((HALF, BY), f32) for _ in range(2)]
        for s in range(LEVELS):
            for x in range(BX):
                rr = s * BX + x
                value = stage[pl.ds(q * RHS * ROWS + rr, RHS, stride=ROWS), :]
                v[q * LEVELS + s, x, :RHS, :] = value
                for h in range(2):
                    packed[h] = pack(value[h * HALF : (h + 1) * HALF], rr, packed[h])
        for h in range(2):
            edge[0, q, h] = packed[h]

        @pl.when(q == 0)
        def _():
            pl.semaphore_wait(barrier, len(peers))
            for copy in kcopies:
                copy.start()

        for copy in copies_of(0, q):
            copy.start()
        return carry

    lax.fori_loop(0, CHUNKS, relayout, 0)

    for copy in kcopies:
        copy.wait_recv()
    level = lax.broadcasted_iota(jnp.int32, (NZ, BY), 0)
    merged = jnp.where(lax.rem(wide_lane, 2) == 1, pltpu.roll(kyl[...], 1, 1), pltpu.roll(kyr[...], BY - 1, 1))
    for x in range(BX):
        centre = kown[x]
        xm = kown[x - 1] if x > 0 else jnp.where(gx == 0, 0.0, kxl[...])
        xp = kown[x + 1] if x < BX - 1 else jnp.where(gx == gx_n - 1, 0.0, kxr[...])
        ends = pltpu.roll(merged, BY - 1 - 2 * x, 1)
        from_below = jnp.where(gy == 0, 0.0, ends)
        from_above = jnp.where(gy == gy_n - 1, 0.0, ends)
        ym = jnp.where(wide_lane == 0, from_below, pltpu.roll(centre, 1, 1))
        yp = jnp.where(wide_lane == BY - 1, from_above, pltpu.roll(centre, BY - 1, 1))
        zm = jnp.where(level == 0, 0.0, pltpu.roll(centre, 1, 0))
        zp = jnp.where(level == NZ - 1, 0.0, pltpu.roll(centre, NZ - 1, 0))
        t = [harmonic(centre, other) for other in (xm, xp, ym, yp, zm, zp)]
        bottom = flags[pl.ds(x, 1), :].astype(f32)
        top = flags[pl.ds(BX + x, 1), :].astype(f32)
        boundary = jnp.where(level == 0, 2.0 * centre * bottom, 0.0)
        boundary = boundary + jnp.where(level == NZ - 1, 2.0 * centre * top, 0.0)
        diagonal = t[0] + t[1] + t[2] + t[3] + t[4] + t[5] + boundary
        divisor = jnp.where(diagonal > 0, diagonal, 1.0)
        for n in range(6):
            ct[n, x] = -(t[n] / divisor)

    def spread(block, carry):
        for n in range(6):
            for x in range(BX):
                rows = ct[n, x, pl.ds(pl.multiple_of(block * 8, 8), 8), :]
                for s in range(8):
                    cb[block * 8 + s, x, n] = jnp.broadcast_to(rows[s : s + 1, :], (HALF, BY))
        return carry

    lax.fori_loop(0, NZ // 8, spread, 0)

    def advance(j, q):
        for copy in copies_of(j, q):
            copy.wait_recv()
        base = q * LEVELS
        merged = [
            jnp.where(odd, pltpu.roll(yl[j, q, h], 1, 1), pltpu.roll(yr[j, q, h], BY - 1, 1)) for h in range(2)
        ]
        packed = [jnp.zeros((HALF, BY), f32) for _ in range(2)]
        for s in range(LEVELS):
            z = base + s
            zm = lax.rem(z + NZ - 1, NZ) if s == 0 else z - 1
            zp = lax.rem(z + 1, NZ) if s == LEVELS - 1 else z + 1
            for x in range(BX):
                rr = s * BX + x
                coupling = [cb[z, x, n] for n in range(6)]
                for h in range(2):
                    here = pl.ds(j * RHS + h * HALF, HALF)
                    rows = pl.ds(h * HALF, HALF)
                    centre = v[z, x, here, :]
                    xm = v[z, x - 1, here, :] if x > 0 else xl[j, q, s, rows, :]
                    xp = v[z, x + 1, here, :] if x < BX - 1 else xr[j, q, s, rows, :]
                    ends = pltpu.roll(merged[h], BY - 1 - 2 * rr, 1)
                    ym = jnp.where(lane == 0, ends, pltpu.roll(centre, 1, 1))
                    yp = jnp.where(lane == BY - 1, ends, pltpu.roll(centre, BY - 1, 1))
                    summed = (
                        coupling[0] * xm
                        + coupling[1] * xp
                        + coupling[2] * ym
                        + coupling[3] * yp
                        + coupling[4] * v[zm, x, here, :]
                        + coupling[5] * v[zp, x, here, :]
                    )
                    value = summed if j == 0 else 2.0 * summed - v[z, x, pl.ds((j - 1) * RHS + h * HALF, HALF), :]
                    v[z, x, pl.ds((j + 1) * RHS + h * HALF, HALF), :] = value
                    if j < S - 1:
                        packed[h] = pack(value, rr, packed[h])
        if j < S - 1:
            for h in range(2):
                edge[j + 1, q, h] = packed[h]
            for copy in copies_of(j + 1, q):
                copy.start()

    def lead_products(q):
        total = jnp.zeros((LEAD, 2 * LEAD), f32)
        for s in range(LEVELS):
            wide = jnp.concatenate([v[q * LEVELS + s, x, :LEAD, :] for x in range(BX)], axis=1)
            high, low = split(wide)
            total = total + lax.dot_general(high, jnp.concatenate([high, low], axis=0), NT, preferred_element_type=f32)
        acc_lead[...] += total

    def last_products(q):
        total = jnp.zeros((2 * RHS, 2 * COLS), f32)
        for s in range(LEVELS):
            wide = jnp.concatenate([v[q * LEVELS + s, x] for x in range(BX)], axis=1)
            high, low = split(wide)
            total = total + lax.dot_general(
                jnp.concatenate([high[LEAD:], low[LEAD:]], axis=0),
                jnp.concatenate([high, low], axis=0),
                NT,
                preferred_element_type=f32,
            )
        acc_last[...] += total

    def exchange(phase, buffer, index, count, peer_of, source=None):
        def of(k):
            src = buffer.at[index] if source is None else source.at[lax.rem(index + k, count)]
            return remote(src, buffer.at[index], asend.at[phase, k - 1], arecv.at[phase, k - 1], peer_of(k))

        return [of(k) for k in range(1, count)]

    steps_lead = [
        exchange(0, lead_y, gy, gy_n, y_peer, lead_own),
        exchange(1, lead_z, zi, zg, z_peer),
        exchange(2, lead_x, xi, xg, x_peer),
        exchange(3, lead_all, gy, gy_n, y_peer),
    ]
    steps_last = [
        exchange(4, last_y, gy, gy_n, y_peer),
        exchange(5, last_z, zi, zg, z_peer),
        exchange(6, last_x, xi, xg, x_peer),
    ]

    def send(step):
        for copy in step:
            copy.start()

    def collect(step, buffer):
        for copy in step:
            copy.wait_recv()
        total = buffer[0]
        for k in range(1, len(step) + 1):
            total = total + buffer[k]
        return total

    acc_lead[...] = jnp.zeros_like(acc_lead)
    acc_last[...] = jnp.zeros_like(acc_last)

    def loop(j, more=None):
        def body(q, carry):
            advance(j, q)
            if more is not None:
                more(q)
            return carry

        lax.fori_loop(0, CHUNKS, body, 0)

    loop(0)
    loop(1)
    loop(2, lead_products)

    partial = acc_lead[...]
    mirrored = jnp.concatenate([partial, jnp.zeros((128 - LEAD, 128), f32)], axis=0).T[LEAD : 2 * LEAD]
    lead_lane = lax.broadcasted_iota(jnp.int32, (LEAD, 128), 1)
    partial = jnp.where(lead_lane < LEAD, partial + pltpu.roll(partial, LEAD, 1), 0.0) + mirrored
    for b in range(LEAD // 8):
        lead_own[b] = partial[8 * b : 8 * b + 8]
    lead_y[gy] = lead_own[gy]
    send(steps_lead[0])

    def beside(q):
        last_products(q)

        @pl.when(q == CHUNKS - 2)
        def _():
            lead_z[zi] = collect(steps_lead[0], lead_y)
            send(steps_lead[1])

    loop(3, beside)

    partial = acc_last[...]
    last_y[gy] = jnp.concatenate(
        [partial[:RHS, :COLS] + partial[:RHS, COLS:] + partial[RHS:, :COLS], jnp.zeros((RHS, 128 - COLS), f32)], axis=1
    )
    send(steps_last[0])
    lead_x[xi] = collect(steps_lead[1], lead_z)
    send(steps_lead[2])
    last_z[zi] = collect(steps_last[0], last_y)
    send(steps_last[1])
    lead_all[gy] = collect(steps_lead[2], lead_x)
    send(steps_lead[3])
    last_x[xi] = collect(steps_last[1], last_z)
    send(steps_last[2])
    for copy in steps_lead[3]:
        copy.wait_recv()
    rows, root = scale_start([lead_all[b] * (1.0 / cells) for b in range(LEAD // 8)], LEAD)
    lead[...] = jnp.concatenate(scale_end(eliminate(rows, 0, LEAD), root, LEAD), axis=0)
    last_gram[...] = collect(steps_last[2], last_x) * (1.0 / cells)

    for copy in kcopies:
        copy.wait_send()

    def drain(q, carry):
        for j in range(S):
            for copy in copies_of(j, q):
                copy.wait_send()
        return carry

    lax.fori_loop(0, CHUNKS, drain, 0)
    for step in steps_lead + steps_last:
        for copy in step:
            copy.wait_send()


def scale_start(blocks, size):
    lane = lax.broadcasted_iota(jnp.int32, (8, 128), 1)
    row = lax.broadcasted_iota(jnp.int32, (8, 128), 0)
    scales = []
    across = jnp.zeros((1, 128), f32)
    root = jnp.zeros((1, 128), f32)
    for b, block in enumerate(blocks):
        on = lane == row + 8 * b
        diagonal = jnp.sum(jnp.where(on, block, 0.0), axis=1, keepdims=True)
        rooted = jnp.sqrt(diagonal)
        scale = 1.0 / rooted
        scales.append(scale)
        across = across + jnp.sum(jnp.where(on, scale, 0.0), axis=0, keepdims=True)
        root = root + jnp.sum(jnp.where(on, rooted, 0.0), axis=0, keepdims=True)
    rows = [
        jnp.where(lane < size, block * scale * across, jnp.where(lane - size == row + 8 * b, scale, 0.0))
        for b, (block, scale) in enumerate(zip(blocks, scales))
    ]
    return rows, jnp.where(lane[:1] < size, root, 1.0)


def eliminate(rows, begin, end):
    rows = list(rows)
    sub = lax.broadcasted_iota(jnp.int32, (8, 128), 0)

    def along(block, k):
        return jnp.broadcast_to(block[:, k : k + 1], (8, 128))

    def down(block, k):
        return jnp.broadcast_to(block[k : k + 1, :], (8, 128))

    for k in range(begin, end, 4):
        b, s = divmod(k, 8)
        columns = [[along(block, k + t) for block in rows[b:]] for t in range(4)]
        r0, r1, r2, r3 = [down(rows[b], s + t) for t in range(4)]
        p = {(t, u): down(columns[u][0], s + t) for t in range(4) for u in range(t, 4)}
        i0 = 1.0 / p[0, 0]
        l1, l2, l3 = p[0, 1] * i0, p[0, 2] * i0, p[0, 3] * i0
        q11 = p[1, 1] - l1 * p[0, 1]
        q12 = p[1, 2] - l1 * p[0, 2]
        q13 = p[1, 3] - l1 * p[0, 3]
        i1 = 1.0 / q11
        m2, m3 = q12 * i1, q13 * i1
        s22 = p[2, 2] - l2 * p[0, 2] - m2 * q12
        s23 = p[2, 3] - l2 * p[0, 3] - m2 * q13
        s33 = p[3, 3] - l3 * p[0, 3] - m3 * q13
        i2 = 1.0 / s22
        n3 = s23 * i2
        i3 = 1.0 / (s33 - n3 * s23)
        u1 = r1 - l1 * r0
        u2 = r2 - l2 * r0 - m2 * u1
        u3 = r3 - l3 * r0 - m3 * u1 - n3 * u2
        z3 = i3 * u3
        z2 = i2 * u2 - n3 * z3
        z1 = i1 * u1 - m2 * z2 - m3 * z3
        z0 = i0 * r0 - l1 * z1 - l2 * z2 - l3 * z3
        for i in range(b, len(rows)):
            c0, c1, c2, c3 = [column[i - b] for column in columns]
            changed = rows[i] - (c0 * z0 + c1 * z1) - (c2 * z2 + c3 * z3)
            if i == b:
                kept = jnp.where(sub == s + 2, u2, jnp.where(sub == s + 3, u3, rows[i]))
                changed = jnp.where(sub > s + 3, changed, jnp.where(sub == s + 1, u1, kept))
            rows[i] = changed
    return rows


def scale_end(rows, root, size):
    lane = lax.broadcasted_iota(jnp.int32, (8, 128), 1)
    row = lax.broadcasted_iota(jnp.int32, (8, 128), 0)
    done = []
    for b, block in enumerate(rows):
        diagonal = jnp.sum(jnp.where(lane == row + 8 * b, block, 0.0), axis=1, keepdims=True)
        block = jnp.where((lane >= row + 8 * b) & (lane - size <= row + 8 * b), block, 0.0)
        done.append(block * (1.0 / jnp.sqrt(diagonal)) * root)
    return done


def exact(a, b, dims):
    return lax.dot_general(a, b, dims, precision=lax.Precision.HIGHEST, preferred_element_type=f32)


def finish_kernel(v, last_gram, lead, out, r_out, stage, sems):
    upper = lead[:, :LEAD]
    inverse = lead[:, LEAD:]
    against = last_gram[:, :LEAD]
    cross = exact(against, inverse, NT)
    schur = last_gram[:, LEAD:COLS] - exact(cross, cross, NT)
    back = exact(cross, inverse, NN)
    padded = jnp.concatenate([schur, jnp.zeros((RHS, 128 - RHS), f32)], axis=1)
    rows, root = scale_start([padded[:8], padded[8:]], RHS)
    rows = scale_end(eliminate(rows, 0, RHS), root, RHS)
    corner = jnp.concatenate(rows, axis=0)
    corner_upper = corner[:, :RHS]
    corner_inverse = corner[:, RHS : 2 * RHS]
    back = -exact(corner_inverse, back, NN)

    tall = jnp.concatenate([cross, jnp.zeros((RHS, 128 - LEAD), f32)], axis=1)
    tall = jnp.concatenate([tall, jnp.zeros((128 - RHS, 128), f32)], axis=0).T[:LEAD, :RHS]
    r_out[...] = jnp.concatenate(
        [
            jnp.concatenate([upper, tall], axis=1),
            jnp.concatenate([jnp.zeros((RHS, LEAD), f32), corner_upper], axis=1),
        ],
        axis=0,
    )
    whole = jnp.concatenate(
        [
            jnp.concatenate([inverse, jnp.zeros((LEAD, 256 - LEAD), f32)], axis=1),
            jnp.concatenate([back, corner_inverse, jnp.zeros((RHS, 256 - COLS), f32)], axis=1),
        ],
        axis=0,
    )
    high = whole.astype(bf16).astype(f32)
    low = whole - high
    weights = high + pltpu.roll(high, COLS, 1) + pltpu.roll(low, 2 * COLS, 1)
    weights = weights[:, : 3 * COLS].astype(bf16)
    groups = 16
    per = NZ // groups
    copies = []
    for group in range(groups):
        def block(step, carry):
            for s in range(2):
                z = step * 2 + s
                for h in range(2):
                    both = jnp.concatenate([v[z, 2 * h], v[z, 2 * h + 1]], axis=1)
                    vh, vl = split(both)
                    q = jnp.dot(weights, jnp.concatenate([vh, vl, vh], axis=0), preferred_element_type=f32)
                    r = z * BX + 2 * h
                    stage[pl.ds(r, COLS, stride=PITCH), :] = q[:, :BY]
                    stage[pl.ds(r + 1, COLS, stride=PITCH), :] = q[:, BY:]
            return carry

        lax.fori_loop(group * per // 2, (group + 1) * per // 2, block, 0)
        rows = pl.ds(group * per * BX, per * BX)
        copy = pltpu.make_async_copy(
            stage.reshape(COLS, PITCH, BY).at[:, rows, :], out.at[:, rows, :], sems.at[group]
        )
        copy.start()
        copies.append(copy)
    for copy in copies:
        copy.wait()


def per_device(sizes, cells, right_sides, region_labels, face_flags, region_perm):
    gx_n, gy_n, zg, xg = sizes
    vmem = pl.BlockSpec(memory_space=pltpu.VMEM)
    hbm = pl.BlockSpec(memory_space=pltpu.HBM)
    scratch = [
        (CHUNKS * RHS * ROWS, BY),
        (NZ * BX, BY, jnp.int32),
        (2 * BX, BY, jnp.int32),
        (S, CHUNKS, LEVELS, RHS, BY),
        (S, CHUNKS, LEVELS, RHS, BY),
        (S, CHUNKS, 2, HALF, BY),
        (S, CHUNKS, 2, HALF, BY),
        (S, CHUNKS, 2, HALF, BY),
        (BX, NZ, BY),
        (NZ, BY),
        (NZ, BY),
        (NZ, BY),
        (NZ, BY),
        (NZ, BY),
        (6, BX, NZ, BY),
        (NZ, BX, 6, HALF, BY),
        (LEAD, 2 * LEAD),
        (2 * RHS, 2 * COLS),
        (LEAD // 8, 8, 128),
        (gy_n, 8, 128),
        (zg, 8, 128),
        (xg, 8, 128),
        (LEAD // 8, 8, 128),
        (gy_n, RHS, 128),
        (zg, RHS, 128),
        (xg, RHS, 128),
    ]
    scratch = [
        pltpu.VMEM(shape[:-1], shape[-1]) if shape[-1] is jnp.int32 else pltpu.VMEM(shape, f32) for shape in scratch
    ]
    dma = pltpu.SemaphoreType.DMA
    scratch += [dma((CHUNKS + 2,)), dma((4,)), dma((4,))]
    scratch += [dma((S, CHUNKS, 2)) for _ in range(4)] + [dma((7, 8)), dma((7, 8))]
    v, last_gram, lead = pl.pallas_call(
        functools.partial(basis_kernel, sizes, cells),
        out_shape=(
            pltpu.VMEM((NZ, BX, COLS, BY), f32),
            pltpu.VMEM((RHS, 128), f32),
            pltpu.VMEM((LEAD, 2 * LEAD), f32),
        ),
        in_specs=[hbm, hbm, hbm, pl.BlockSpec(memory_space=pltpu.SMEM)],
        out_specs=(vmem, vmem, vmem),
        scratch_shapes=scratch,
        compiler_params=pltpu.CompilerParams(
            collective_id=0, has_side_effects=True, vmem_limit_bytes=40 * 1024 * 1024
        ),
        name="basis",
    )(
        *(pltpu.with_memory_space_constraint(a, pltpu.HBM) for a in (
            right_sides.reshape(RHS, NZ * BX, BY),
            region_labels.reshape(NZ * BX, BY),
            face_flags.reshape(2 * BX, BY),
            region_perm,
        )),
    )
    out, upper = pl.pallas_call(
        finish_kernel,
        out_shape=(
            jax.ShapeDtypeStruct((COLS, NZ * BX, BY), f32),
            jax.ShapeDtypeStruct((COLS, COLS), f32),
        ),
        in_specs=[vmem, vmem, vmem],
        out_specs=(hbm, vmem),
        scratch_shapes=[pltpu.VMEM((COLS * PITCH, BY), f32), dma((16,))],
        compiler_params=pltpu.CompilerParams(vmem_limit_bytes=40 * 1024 * 1024),
        name="finish",
    )(v, last_gram, lead)
    return out.reshape(COLS, NZ, BX, BY), upper


def solution(mesh):
    gx_n, gy_n = mesh.shape["gx"], mesh.shape["gy"]
    zg = 8 if gx_n % 8 == 0 else 2
    sizes = (gx_n, gy_n, zg, gx_n // zg)
    cells = NZ * BX * BY * gx_n * gy_n
    placed = (P(None, None, "gx", "gy"), P(None, "gx", "gy"), P(None, "gx", "gy"), P())
    return jax.shard_map(
        functools.partial(per_device, sizes, cells),
        mesh=mesh,
        in_specs=placed,
        out_specs=(P(None, None, "gx", "gy"), P()),
        check_vma=False,
    )
```

```python
import functools
import jax
import jax.numpy as jnp
from jax import lax
from jax.experimental import pallas as pl
from jax.experimental.pallas import tpu as pltpu
from jax.sharding import PartitionSpec as P

RHS = 16
S = 4
VECS = S + 1
COLS = RHS * VECS
NZ = 32
BX = 4
BY = 128
HALF = 8
LEAD = RHS * S
LEVELS = 8
CHUNKS = NZ // LEVELS
ROWS = LEVELS * BX
PITCH = NZ * BX + 8
NT = (((1,), (1,)), ((), ()))
NN = (((1,), (0,)), ((), ()))
MESH = pl.DeviceIdType.MESH
f32 = jnp.float32
bf16 = jnp.bfloat16


def split(value):
    high = value.astype(bf16)
    low = (value - high.astype(f32)).astype(bf16)
    return high, low


def harmonic(centre, neighbour):
    summed = centre + neighbour
    return 2.0 * centre * neighbour / jnp.where(summed > 0, summed, 1.0)


def basis_kernel(
    sizes, cells,
    rs, labels_hbm, flags_hbm, perm,
    v, last_gram, lead,
    stage, labels, flags, xl, xr, edge, yl, yr, kown, kedge, kxl, kxr, kyl, kyr, ct, cb,
    acc_lead, acc_last, lead_y, lead_z, lead_x, last_y, last_z, last_x,
    load_sem, ksend, krecv, xsend, xrecv, ysend, yrecv, asend, arecv,
):
    gx_n, gy_n, zg, xg = sizes
    gx = lax.axis_index("gx")
    gy = lax.axis_index("gy")
    right = lax.rem(gx + 1, gx_n)
    left = lax.rem(gx + gx_n - 1, gx_n)
    above = lax.rem(gy + 1, gy_n)
    below = lax.rem(gy + gy_n - 1, gy_n)
    zi = lax.rem(gx, zg)
    xi = lax.div(gx, zg)

    def z_peer(k):
        return (xi * zg + lax.rem(zi + k, zg), gy)

    def x_peer(k):
        return (lax.rem(xi + k, xg) * zg + zi, gy)

    def y_peer(k):
        return (gx, lax.rem(gy + k, gy_n))

    loads = [
        pltpu.make_async_copy(labels_hbm, labels, load_sem.at[CHUNKS]),
        pltpu.make_async_copy(flags_hbm, flags, load_sem.at[CHUNKS + 1]),
    ]

    def load_of(q):
        return pltpu.make_async_copy(
            rs.at[:, pl.ds(q * ROWS, ROWS), :], stage.reshape(CHUNKS, RHS, ROWS, BY).at[q], load_sem.at[q]
        )

    loads += [load_of(q) for q in range(CHUNKS)]
    for load in loads:
        load.start()
    peers = [z_peer(k) for k in sorted(range(1, zg), key=lambda k: abs(k - zg // 2))]
    peers += [y_peer(k) for k in sorted(range(1, gy_n), key=lambda k: abs(k - gy_n // 2))]
    peers += [x_peer(k) for k in range(1, xg)]
    peers += [(right, gy), (left, gy)]
    barrier = pltpu.get_barrier_semaphore()
    for peer in peers:
        pl.semaphore_signal(barrier, inc=1, device_id=peer, device_id_type=MESH)

    loads[0].wait()
    loads[1].wait()
    for x in range(BX):
        label = labels[pl.ds(x, NZ, stride=BX), :]
        value = jnp.zeros((NZ, BY), f32)
        for region in range(perm.shape[0]):
            value = jnp.where(label == region, perm[region], value)
        kown[x] = value

    def remote(src, dst, send, recv, peer):
        return pltpu.make_async_remote_copy(
            src_ref=src, dst_ref=dst, send_sem=send, recv_sem=recv, device_id=peer, device_id_type=MESH
        )

    wide_lane = lax.broadcasted_iota(jnp.int32, (NZ, BY), 1)
    kends = jnp.zeros((NZ, BY), f32)
    for x in range(BX):
        kends = jnp.where(lax.div(wide_lane, 2) == x, pltpu.roll(kown[x], 2 * x + 1, 1), kends)
    kedge[...] = kends
    kcopies = [
        remote(kedge, kyl, ksend.at[2], krecv.at[2], (gx, above)),
        remote(kedge, kyr, ksend.at[3], krecv.at[3], (gx, below)),
        remote(kown.at[BX - 1], kxl, ksend.at[0], krecv.at[0], (right, gy)),
        remote(kown.at[0], kxr, ksend.at[1], krecv.at[1], (left, gy)),
    ]

    def copies_of(j, q):
        levels = pl.ds(q * LEVELS, LEVELS)
        plane = pl.ds(j * RHS, RHS)
        return [
            remote(v.at[levels, BX - 1, plane, :], xl.at[j, q], xsend.at[j, q, 0], xrecv.at[j, q, 0], (right, gy)),
            remote(v.at[levels, 0, plane, :], xr.at[j, q], xsend.at[j, q, 1], xrecv.at[j, q, 1], (left, gy)),
            remote(edge.at[j, q], yl.at[j, q], ysend.at[j, q, 0], yrecv.at[j, q, 0], (gx, above)),
            remote(edge.at[j, q], yr.at[j, q], ysend.at[j, q, 1], yrecv.at[j, q, 1], (gx, below)),
        ]

    lane = lax.broadcasted_iota(jnp.int32, (HALF, BY), 1)
    pair = lax.div(lane, 2)
    odd = lax.rem(lane, 2) == 1

    def pack(value, rr, packed):
        return jnp.where(pair == rr, pltpu.roll(value, 2 * rr + 1, 1), packed)

    def relayout(q, carry):
        load_of(q).wait()
        packed = [jnp.zeros((HALF, BY), f32) for _ in range(2)]
        for s in range(LEVELS):
            for x in range(BX):
                rr = s * BX + x
                value = stage[pl.ds(q * RHS * ROWS + rr, RHS, stride=ROWS), :]
                v[q * LEVELS + s, x, :RHS, :] = value
                for h in range(2):
                    packed[h] = pack(value[h * HALF : (h + 1) * HALF], rr, packed[h])
        for h in range(2):
            edge[0, q, h] = packed[h]

        @pl.when(q == 0)
        def _():
            pl.semaphore_wait(barrier, len(peers))
            for copy in kcopies:
                copy.start()

        for copy in copies_of(0, q):
            copy.start()
        return carry

    lax.fori_loop(0, CHUNKS, relayout, 0)

    for copy in kcopies:
        copy.wait_recv()
    level = lax.broadcasted_iota(jnp.int32, (NZ, BY), 0)
    merged = jnp.where(lax.rem(wide_lane, 2) == 1, pltpu.roll(kyl[...], 1, 1), pltpu.roll(kyr[...], BY - 1, 1))
    for x in range(BX):
        centre = kown[x]
        xm = kown[x - 1] if x > 0 else jnp.where(gx == 0, 0.0, kxl[...])
        xp = kown[x + 1] if x < BX - 1 else jnp.where(gx == gx_n - 1, 0.0, kxr[...])
        ends = pltpu.roll(merged, BY - 1 - 2 * x, 1)
        from_below = jnp.where(gy == 0, 0.0, ends)
        from_above = jnp.where(gy == gy_n - 1, 0.0, ends)
        ym = jnp.where(wide_lane == 0, from_below, pltpu.roll(centre, 1, 1))
        yp = jnp.where(wide_lane == BY - 1, from_above, pltpu.roll(centre, BY - 1, 1))
        zm = jnp.where(level == 0, 0.0, pltpu.roll(centre, 1, 0))
        zp = jnp.where(level == NZ - 1, 0.0, pltpu.roll(centre, NZ - 1, 0))
        t = [harmonic(centre, other) for other in (xm, xp, ym, yp, zm, zp)]
        bottom = flags[pl.ds(x, 1), :].astype(f32)
        top = flags[pl.ds(BX + x, 1), :].astype(f32)
        boundary = jnp.where(level == 0, 2.0 * centre * bottom, 0.0)
        boundary = boundary + jnp.where(level == NZ - 1, 2.0 * centre * top, 0.0)
        diagonal = t[0] + t[1] + t[2] + t[3] + t[4] + t[5] + boundary
        divisor = jnp.where(diagonal > 0, diagonal, 1.0)
        for n in range(6):
            ct[n, x] = -(t[n] / divisor)

    def spread(block, carry):
        for n in range(6):
            for x in range(BX):
                rows = ct[n, x, pl.ds(pl.multiple_of(block * 8, 8), 8), :]
                for s in range(8):
                    cb[block * 8 + s, x, n] = jnp.broadcast_to(rows[s : s + 1, :], (HALF, BY))
        return carry

    lax.fori_loop(0, NZ // 8, spread, 0)

    def advance(j, q):
        for copy in copies_of(j, q):
            copy.wait_recv()
        base = q * LEVELS
        merged = [
            jnp.where(odd, pltpu.roll(yl[j, q, h], 1, 1), pltpu.roll(yr[j, q, h], BY - 1, 1)) for h in range(2)
        ]
        packed = [jnp.zeros((HALF, BY), f32) for _ in range(2)]
        for s in range(LEVELS):
            z = base + s
            zm = lax.rem(z + NZ - 1, NZ) if s == 0 else z - 1
            zp = lax.rem(z + 1, NZ) if s == LEVELS - 1 else z + 1
            for x in range(BX):
                rr = s * BX + x
                coupling = [cb[z, x, n] for n in range(6)]
                for h in range(2):
                    here = pl.ds(j * RHS + h * HALF, HALF)
                    rows = pl.ds(h * HALF, HALF)
                    centre = v[z, x, here, :]
                    xm = v[z, x - 1, here, :] if x > 0 else xl[j, q, s, rows, :]
                    xp = v[z, x + 1, here, :] if x < BX - 1 else xr[j, q, s, rows, :]
                    ends = pltpu.roll(merged[h], BY - 1 - 2 * rr, 1)
                    ym = jnp.where(lane == 0, ends, pltpu.roll(centre, 1, 1))
                    yp = jnp.where(lane == BY - 1, ends, pltpu.roll(centre, BY - 1, 1))
                    summed = (
                        coupling[0] * xm
                        + coupling[1] * xp
                        + coupling[2] * ym
                        + coupling[3] * yp
                        + coupling[4] * v[zm, x, here, :]
                        + coupling[5] * v[zp, x, here, :]
                    )
                    value = summed if j == 0 else 2.0 * summed - v[z, x, pl.ds((j - 1) * RHS + h * HALF, HALF), :]
                    v[z, x, pl.ds((j + 1) * RHS + h * HALF, HALF), :] = value
                    if j < S - 1:
                        packed[h] = pack(value, rr, packed[h])
        if j < S - 1:
            for h in range(2):
                edge[j + 1, q, h] = packed[h]
            for copy in copies_of(j + 1, q):
                copy.start()

    def lead_products(q):
        total = jnp.zeros((LEAD, 2 * LEAD), f32)
        for s in range(LEVELS):
            wide = jnp.concatenate([v[q * LEVELS + s, x, :LEAD, :] for x in range(BX)], axis=1)
            high, low = split(wide)
            total = total + lax.dot_general(high, jnp.concatenate([high, low], axis=0), NT, preferred_element_type=f32)
        acc_lead[...] += total

    def last_products(q):
        total = jnp.zeros((2 * RHS, 2 * COLS), f32)
        for s in range(LEVELS):
            wide = jnp.concatenate([v[q * LEVELS + s, x] for x in range(BX)], axis=1)
            high, low = split(wide)
            total = total + lax.dot_general(
                jnp.concatenate([high[LEAD:], low[LEAD:]], axis=0),
                jnp.concatenate([high, low], axis=0),
                NT,
                preferred_element_type=f32,
            )
        acc_last[...] += total

    def exchange(phase, buffer, index, count, peer_of):
        return [
            remote(buffer.at[index], buffer.at[index], asend.at[phase, k - 1], arecv.at[phase, k - 1], peer_of(k))
            for k in range(1, count)
        ]

    steps_lead = [
        exchange(0, lead_y, gy, gy_n, y_peer),
        exchange(1, lead_z, zi, zg, z_peer),
        exchange(2, lead_x, xi, xg, x_peer),
    ]
    steps_last = [
        exchange(3, last_y, gy, gy_n, y_peer),
        exchange(4, last_z, zi, zg, z_peer),
        exchange(5, last_x, xi, xg, x_peer),
    ]

    def send(step):
        for copy in step:
            copy.start()

    def collect(step, buffer):
        for copy in step:
            copy.wait_recv()
        total = buffer[0]
        for k in range(1, len(step) + 1):
            total = total + buffer[k]
        return total

    acc_lead[...] = jnp.zeros_like(acc_lead)
    acc_last[...] = jnp.zeros_like(acc_last)

    def loop(j, more=None):
        def body(q, carry):
            advance(j, q)
            if more is not None:
                more(q)
            return carry

        lax.fori_loop(0, CHUNKS, body, 0)

    loop(0)
    loop(1)
    loop(2, lead_products)

    partial = acc_lead[...]
    mirrored = jnp.concatenate([partial, jnp.zeros((128 - LEAD, 128), f32)], axis=0).T[LEAD : 2 * LEAD]
    lead_lane = lax.broadcasted_iota(jnp.int32, (LEAD, 128), 1)
    partial = jnp.where(lead_lane < LEAD, partial + pltpu.roll(partial, LEAD, 1), 0.0) + mirrored
    lead_y[gy] = partial[: LEAD // 2] + pltpu.roll(partial[LEAD // 2 :], LEAD, 1)
    send(steps_lead[0])

    def beside(q):
        last_products(q)

        @pl.when(q == CHUNKS - 2)
        def _():
            lead_z[zi] = collect(steps_lead[0], lead_y)
            send(steps_lead[1])

    loop(3, beside)

    partial = acc_last[...]
    last_y[gy] = jnp.concatenate(
        [partial[:RHS, :COLS] + partial[:RHS, COLS:] + partial[RHS:, :COLS], jnp.zeros((RHS, 128 - COLS), f32)], axis=1
    )
    send(steps_last[0])
    last_z[zi] = collect(steps_last[0], last_y)
    send(steps_last[1])
    lead_x[xi] = collect(steps_lead[1], lead_z)
    send(steps_lead[2])
    last_x[xi] = collect(steps_last[1], last_z)
    send(steps_last[2])
    summed = collect(steps_lead[2], lead_x) * (1.0 / cells)
    summed = jnp.concatenate([summed, pltpu.roll(summed, LEAD, 1)], axis=0)
    rows, root = scale_start([summed[8 * b : 8 * b + 8] for b in range(LEAD // 8)], LEAD)
    lead[...] = jnp.concatenate(scale_end(eliminate(rows, 0, LEAD), root, LEAD), axis=0)
    last_gram[...] = collect(steps_last[2], last_x) * (1.0 / cells)

    for copy in kcopies:
        copy.wait_send()

    def drain(q, carry):
        for j in range(S):
            for copy in copies_of(j, q):
                copy.wait_send()
        return carry

    lax.fori_loop(0, CHUNKS, drain, 0)
    for step in steps_lead + steps_last:
        for copy in step:
            copy.wait_send()


def scale_start(blocks, size):
    lane = lax.broadcasted_iota(jnp.int32, (8, 128), 1)
    row = lax.broadcasted_iota(jnp.int32, (8, 128), 0)
    scales = []
    across = jnp.zeros((1, 128), f32)
    root = jnp.zeros((1, 128), f32)
    for b, block in enumerate(blocks):
        on = lane == row + 8 * b
        diagonal = jnp.sum(jnp.where(on, block, 0.0), axis=1, keepdims=True)
        rooted = jnp.sqrt(diagonal)
        scale = 1.0 / rooted
        scales.append(scale)
        across = across + jnp.sum(jnp.where(on, scale, 0.0), axis=0, keepdims=True)
        root = root + jnp.sum(jnp.where(on, rooted, 0.0), axis=0, keepdims=True)
    rows = [
        jnp.where(lane < size, block * scale * across, jnp.where(lane - size == row + 8 * b, scale, 0.0))
        for b, (block, scale) in enumerate(zip(blocks, scales))
    ]
    return rows, jnp.where(lane[:1] < size, root, 1.0)


def eliminate(rows, begin, end):
    rows = list(rows)
    sub = lax.broadcasted_iota(jnp.int32, (8, 128), 0)

    def along(block, k):
        return jnp.broadcast_to(block[:, k : k + 1], (8, 128))

    def down(block, k):
        return jnp.broadcast_to(block[k : k + 1, :], (8, 128))

    for k in range(begin, end, 4):
        b, s = divmod(k, 8)
        columns = [[along(block, k + t) for block in rows[b:]] for t in range(4)]
        r0, r1, r2, r3 = [down(rows[b], s + t) for t in range(4)]
        p = {(t, u): down(columns[u][0], s + t) for t in range(4) for u in range(t, 4)}
        i0 = 1.0 / p[0, 0]
        l1, l2, l3 = p[0, 1] * i0, p[0, 2] * i0, p[0, 3] * i0
        q11 = p[1, 1] - l1 * p[0, 1]
        q12 = p[1, 2] - l1 * p[0, 2]
        q13 = p[1, 3] - l1 * p[0, 3]
        i1 = 1.0 / q11
        m2, m3 = q12 * i1, q13 * i1
        s22 = p[2, 2] - l2 * p[0, 2] - m2 * q12
        s23 = p[2, 3] - l2 * p[0, 3] - m2 * q13
        s33 = p[3, 3] - l3 * p[0, 3] - m3 * q13
        i2 = 1.0 / s22
        n3 = s23 * i2
        i3 = 1.0 / (s33 - n3 * s23)
        u1 = r1 - l1 * r0
        u2 = r2 - l2 * r0 - m2 * u1
        u3 = r3 - l3 * r0 - m3 * u1 - n3 * u2
        z3 = i3 * u3
        z2 = i2 * u2 - n3 * z3
        z1 = i1 * u1 - m2 * z2 - m3 * z3
        z0 = i0 * r0 - l1 * z1 - l2 * z2 - l3 * z3
        for i in range(b, len(rows)):
            c0, c1, c2, c3 = [column[i - b] for column in columns]
            changed = rows[i] - (c0 * z0 + c1 * z1) - (c2 * z2 + c3 * z3)
            if i == b:
                kept = jnp.where(sub == s + 2, u2, jnp.where(sub == s + 3, u3, rows[i]))
                changed = jnp.where(sub > s + 3, changed, jnp.where(sub == s + 1, u1, kept))
            rows[i] = changed
    return rows


def scale_end(rows, root, size):
    lane = lax.broadcasted_iota(jnp.int32, (8, 128), 1)
    row = lax.broadcasted_iota(jnp.int32, (8, 128), 0)
    done = []
    for b, block in enumerate(rows):
        diagonal = jnp.sum(jnp.where(lane == row + 8 * b, block, 0.0), axis=1, keepdims=True)
        block = jnp.where((lane >= row + 8 * b) & (lane - size <= row + 8 * b), block, 0.0)
        done.append(block * (1.0 / jnp.sqrt(diagonal)) * root)
    return done


def exact(a, b, dims):
    return lax.dot_general(a, b, dims, precision=lax.Precision.HIGHEST, preferred_element_type=f32)


def finish_kernel(v, last_gram, lead, out, r_out, stage, sems):
    upper = lead[:, :LEAD]
    inverse = lead[:, LEAD:]
    against = last_gram[:, :LEAD]
    cross = exact(against, inverse, NT)
    schur = last_gram[:, LEAD:COLS] - exact(cross, cross, NT)
    back = exact(cross, inverse, NN)
    padded = jnp.concatenate([schur, jnp.zeros((RHS, 128 - RHS), f32)], axis=1)
    rows, root = scale_start([padded[:8], padded[8:]], RHS)
    rows = scale_end(eliminate(rows, 0, RHS), root, RHS)
    corner = jnp.concatenate(rows, axis=0)
    corner_upper = corner[:, :RHS]
    corner_inverse = corner[:, RHS : 2 * RHS]
    back = -exact(corner_inverse, back, NN)

    tall = jnp.concatenate([cross, jnp.zeros((RHS, 128 - LEAD), f32)], axis=1)
    tall = jnp.concatenate([tall, jnp.zeros((128 - RHS, 128), f32)], axis=0).T[:LEAD, :RHS]
    r_out[...] = jnp.concatenate(
        [
            jnp.concatenate([upper, tall], axis=1),
            jnp.concatenate([jnp.zeros((RHS, LEAD), f32), corner_upper], axis=1),
        ],
        axis=0,
    )
    whole = jnp.concatenate(
        [
            jnp.concatenate([inverse, jnp.zeros((LEAD, 256 - LEAD), f32)], axis=1),
            jnp.concatenate([back, corner_inverse, jnp.zeros((RHS, 256 - COLS), f32)], axis=1),
        ],
        axis=0,
    )
    high = whole.astype(bf16).astype(f32)
    low = whole - high
    weights = high + pltpu.roll(high, COLS, 1) + pltpu.roll(low, 2 * COLS, 1)
    weights = weights[:, : 3 * COLS].astype(bf16)
    groups = 16
    per = NZ // groups
    copies = []
    for group in range(groups):
        def block(step, carry):
            for s in range(2):
                z = step * 2 + s
                for h in range(2):
                    both = jnp.concatenate([v[z, 2 * h], v[z, 2 * h + 1]], axis=1)
                    vh, vl = split(both)
                    q = jnp.dot(weights, jnp.concatenate([vh, vl, vh], axis=0), preferred_element_type=f32)
                    r = z * BX + 2 * h
                    stage[pl.ds(r, COLS, stride=PITCH), :] = q[:, :BY]
                    stage[pl.ds(r + 1, COLS, stride=PITCH), :] = q[:, BY:]
            return carry

        lax.fori_loop(group * per // 2, (group + 1) * per // 2, block, 0)
        rows = pl.ds(group * per * BX, per * BX)
        copy = pltpu.make_async_copy(
            stage.reshape(COLS, PITCH, BY).at[:, rows, :], out.at[:, rows, :], sems.at[group]
        )
        copy.start()
        copies.append(copy)
    for copy in copies:
        copy.wait()


def per_device(sizes, cells, right_sides, region_labels, face_flags, region_perm):
    gx_n, gy_n, zg, xg = sizes
    vmem = pl.BlockSpec(memory_space=pltpu.VMEM)
    hbm = pl.BlockSpec(memory_space=pltpu.HBM)
    scratch = [
        (CHUNKS * RHS * ROWS, BY),
        (NZ * BX, BY, jnp.int32),
        (2 * BX, BY, jnp.int32),
        (S, CHUNKS, LEVELS, RHS, BY),
        (S, CHUNKS, LEVELS, RHS, BY),
        (S, CHUNKS, 2, HALF, BY),
        (S, CHUNKS, 2, HALF, BY),
        (S, CHUNKS, 2, HALF, BY),
        (BX, NZ, BY),
        (NZ, BY),
        (NZ, BY),
        (NZ, BY),
        (NZ, BY),
        (NZ, BY),
        (6, BX, NZ, BY),
        (NZ, BX, 6, HALF, BY),
        (LEAD, 2 * LEAD),
        (2 * RHS, 2 * COLS),
        (gy_n, LEAD // 2, 128),
        (zg, LEAD // 2, 128),
        (xg, LEAD // 2, 128),
        (gy_n, RHS, 128),
        (zg, RHS, 128),
        (xg, RHS, 128),
    ]
    scratch = [
        pltpu.VMEM(shape[:-1], shape[-1]) if shape[-1] is jnp.int32 else pltpu.VMEM(shape, f32) for shape in scratch
    ]
    dma = pltpu.SemaphoreType.DMA
    scratch += [dma((CHUNKS + 2,)), dma((4,)), dma((4,))]
    scratch += [dma((S, CHUNKS, 2)) for _ in range(4)] + [dma((6, 8)), dma((6, 8))]
    v, last_gram, lead = pl.pallas_call(
        functools.partial(basis_kernel, sizes, cells),
        out_shape=(
            pltpu.VMEM((NZ, BX, COLS, BY), f32),
            pltpu.VMEM((RHS, 128), f32),
            pltpu.VMEM((LEAD, 2 * LEAD), f32),
        ),
        in_specs=[hbm, hbm, hbm, pl.BlockSpec(memory_space=pltpu.SMEM)],
        out_specs=(vmem, vmem, vmem),
        scratch_shapes=scratch,
        compiler_params=pltpu.CompilerParams(
            collective_id=0, has_side_effects=True, vmem_limit_bytes=40 * 1024 * 1024
        ),
        name="basis",
    )(
        *(pltpu.with_memory_space_constraint(a, pltpu.HBM) for a in (
            right_sides.reshape(RHS, NZ * BX, BY),
            region_labels.reshape(NZ * BX, BY),
            face_flags.reshape(2 * BX, BY),
            region_perm,
        )),
    )
    out, upper = pl.pallas_call(
        finish_kernel,
        out_shape=(
            jax.ShapeDtypeStruct((COLS, NZ * BX, BY), f32),
            jax.ShapeDtypeStruct((COLS, COLS), f32),
        ),
        in_specs=[vmem, vmem, vmem],
        out_specs=(hbm, vmem),
        scratch_shapes=[pltpu.VMEM((COLS * PITCH, BY), f32), dma((16,))],
        compiler_params=pltpu.CompilerParams(vmem_limit_bytes=40 * 1024 * 1024),
        name="finish",
    )(v, last_gram, lead)
    return out.reshape(COLS, NZ, BX, BY), upper


def solution(mesh):
    gx_n, gy_n = mesh.shape["gx"], mesh.shape["gy"]
    zg = 8 if gx_n % 8 == 0 else 2
    sizes = (gx_n, gy_n, zg, gx_n // zg)
    cells = NZ * BX * BY * gx_n * gy_n
    placed = (P(None, None, "gx", "gy"), P(None, "gx", "gy"), P(None, "gx", "gy"), P())
    return jax.shard_map(
        functools.partial(per_device, sizes, cells),
        mesh=mesh,
        in_specs=placed,
        out_specs=(P(None, None, "gx", "gy"), P()),
        check_vma=False,
    )
```

```python
import functools
import jax
import jax.numpy as jnp
from jax import lax
from jax.experimental import pallas as pl
from jax.experimental.pallas import tpu as pltpu
from jax.sharding import PartitionSpec as P

RHS = 16
S = 4
VECS = S + 1
COLS = RHS * VECS
NZ = 32
BX = 4
BY = 128
HALF = 8
LEAD = RHS * S
LEVELS = 8
CHUNKS = NZ // LEVELS
ROWS = LEVELS * BX
PITCH = NZ * BX + 8
PACKED = 8 + RHS * RHS // 128
NT = (((1,), (1,)), ((), ()))
NN = (((1,), (0,)), ((), ()))
MESH = pl.DeviceIdType.MESH
f32 = jnp.float32
bf16 = jnp.bfloat16


def split(value):
    high = value.astype(bf16)
    low = (value - high.astype(f32)).astype(bf16)
    return high, low


def harmonic(centre, neighbour):
    summed = centre + neighbour
    return 2.0 * centre * neighbour / jnp.where(summed > 0, summed, 1.0)


def basis_kernel(
    sizes, cells,
    rs, labels_hbm, flags_hbm, perm,
    v, last_gram, lead,
    stage, labels, flags, xl, xr, edge, yl, yr, kown, kedge, kxl, kxr, kyl, kyr, ct, cb,
    acc_lead, acc_last, lead_y, lead_z, lead_x, last_y, last_z, last_x,
    load_sem, ksend, krecv, xsend, xrecv, ysend, yrecv, asend, arecv,
):
    gx_n, gy_n, zg, xg = sizes
    gx = lax.axis_index("gx")
    gy = lax.axis_index("gy")
    right = lax.rem(gx + 1, gx_n)
    left = lax.rem(gx + gx_n - 1, gx_n)
    above = lax.rem(gy + 1, gy_n)
    below = lax.rem(gy + gy_n - 1, gy_n)
    zi = lax.rem(gx, zg)
    xi = lax.div(gx, zg)

    def z_peer(k):
        return (xi * zg + lax.rem(zi + k, zg), gy)

    def x_peer(k):
        return (lax.rem(xi + k, xg) * zg + zi, gy)

    def y_peer(k):
        return (gx, lax.rem(gy + k, gy_n))

    loads = [
        pltpu.make_async_copy(labels_hbm, labels, load_sem.at[CHUNKS]),
        pltpu.make_async_copy(flags_hbm, flags, load_sem.at[CHUNKS + 1]),
    ]

    def load_of(q):
        return pltpu.make_async_copy(
            rs.at[:, pl.ds(q * ROWS, ROWS), :], stage.reshape(CHUNKS, RHS, ROWS, BY).at[q], load_sem.at[q]
        )

    loads += [load_of(q) for q in range(CHUNKS)]
    for load in loads:
        load.start()
    peers = [z_peer(k) for k in sorted(range(1, zg), key=lambda k: abs(k - zg // 2))]
    peers += [y_peer(k) for k in sorted(range(1, gy_n), key=lambda k: abs(k - gy_n // 2))]
    peers += [x_peer(k) for k in range(1, xg)]
    peers += [(right, gy), (left, gy)]
    barrier = pltpu.get_barrier_semaphore()
    for peer in peers:
        pl.semaphore_signal(barrier, inc=1, device_id=peer, device_id_type=MESH)

    loads[0].wait()
    loads[1].wait()
    for x in range(BX):
        label = labels[pl.ds(x, NZ, stride=BX), :]
        value = jnp.zeros((NZ, BY), f32)
        for region in range(perm.shape[0]):
            value = jnp.where(label == region, perm[region], value)
        kown[x] = value

    def remote(src, dst, send, recv, peer):
        return pltpu.make_async_remote_copy(
            src_ref=src, dst_ref=dst, send_sem=send, recv_sem=recv, device_id=peer, device_id_type=MESH
        )

    wide_lane = lax.broadcasted_iota(jnp.int32, (NZ, BY), 1)
    kends = jnp.zeros((NZ, BY), f32)
    for x in range(BX):
        kends = jnp.where(lax.div(wide_lane, 2) == x, pltpu.roll(kown[x], 2 * x + 1, 1), kends)
    kedge[...] = kends
    kcopies = [
        remote(kedge, kyl, ksend.at[2], krecv.at[2], (gx, above)),
        remote(kedge, kyr, ksend.at[3], krecv.at[3], (gx, below)),
        remote(kown.at[BX - 1], kxl, ksend.at[0], krecv.at[0], (right, gy)),
        remote(kown.at[0], kxr, ksend.at[1], krecv.at[1], (left, gy)),
    ]

    def copies_of(j, q):
        levels = pl.ds(q * LEVELS, LEVELS)
        plane = pl.ds(j * RHS, RHS)
        return [
            remote(v.at[levels, BX - 1, plane, :], xl.at[j, q], xsend.at[j, q, 0], xrecv.at[j, q, 0], (right, gy)),
            remote(v.at[levels, 0, plane, :], xr.at[j, q], xsend.at[j, q, 1], xrecv.at[j, q, 1], (left, gy)),
            remote(edge.at[j, q], yl.at[j, q], ysend.at[j, q, 0], yrecv.at[j, q, 0], (gx, above)),
            remote(edge.at[j, q], yr.at[j, q], ysend.at[j, q, 1], yrecv.at[j, q, 1], (gx, below)),
        ]

    lane = lax.broadcasted_iota(jnp.int32, (HALF, BY), 1)
    pair = lax.div(lane, 2)
    odd = lax.rem(lane, 2) == 1

    def pack(value, rr, packed):
        return jnp.where(pair == rr, pltpu.roll(value, 2 * rr + 1, 1), packed)

    def relayout(q, carry):
        load_of(q).wait()
        packed = [jnp.zeros((HALF, BY), f32) for _ in range(2)]
        for s in range(LEVELS):
            for x in range(BX):
                rr = s * BX + x
                value = stage[pl.ds(q * RHS * ROWS + rr, RHS, stride=ROWS), :]
                v[q * LEVELS + s, x, :RHS, :] = value
                for h in range(2):
                    packed[h] = pack(value[h * HALF : (h + 1) * HALF], rr, packed[h])
        for h in range(2):
            edge[0, q, h] = packed[h]

        @pl.when(q == 0)
        def _():
            pl.semaphore_wait(barrier, len(peers))
            for copy in kcopies:
                copy.start()

        for copy in copies_of(0, q):
            copy.start()
        return carry

    lax.fori_loop(0, CHUNKS, relayout, 0)

    for copy in kcopies:
        copy.wait_recv()
    level = lax.broadcasted_iota(jnp.int32, (NZ, BY), 0)
    merged = jnp.where(lax.rem(wide_lane, 2) == 1, pltpu.roll(kyl[...], 1, 1), pltpu.roll(kyr[...], BY - 1, 1))
    for x in range(BX):
        centre = kown[x]
        xm = kown[x - 1] if x > 0 else jnp.where(gx == 0, 0.0, kxl[...])
        xp = kown[x + 1] if x < BX - 1 else jnp.where(gx == gx_n - 1, 0.0, kxr[...])
        ends = pltpu.roll(merged, BY - 1 - 2 * x, 1)
        from_below = jnp.where(gy == 0, 0.0, ends)
        from_above = jnp.where(gy == gy_n - 1, 0.0, ends)
        ym = jnp.where(wide_lane == 0, from_below, pltpu.roll(centre, 1, 1))
        yp = jnp.where(wide_lane == BY - 1, from_above, pltpu.roll(centre, BY - 1, 1))
        zm = jnp.where(level == 0, 0.0, pltpu.roll(centre, 1, 0))
        zp = jnp.where(level == NZ - 1, 0.0, pltpu.roll(centre, NZ - 1, 0))
        t = [harmonic(centre, other) for other in (xm, xp, ym, yp, zm, zp)]
        bottom = flags[pl.ds(x, 1), :].astype(f32)
        top = flags[pl.ds(BX + x, 1), :].astype(f32)
        boundary = jnp.where(level == 0, 2.0 * centre * bottom, 0.0)
        boundary = boundary + jnp.where(level == NZ - 1, 2.0 * centre * top, 0.0)
        diagonal = t[0] + t[1] + t[2] + t[3] + t[4] + t[5] + boundary
        divisor = jnp.where(diagonal > 0, diagonal, 1.0)
        for n in range(6):
            ct[n, x] = -(t[n] / divisor)

    def spread(block, carry):
        for n in range(6):
            for x in range(BX):
                rows = ct[n, x, pl.ds(pl.multiple_of(block * 8, 8), 8), :]
                for s in range(8):
                    cb[block * 8 + s, x, n] = jnp.broadcast_to(rows[s : s + 1, :], (HALF, BY))
        return carry

    lax.fori_loop(0, NZ // 8, spread, 0)

    def advance(j, q):
        for copy in copies_of(j, q):
            copy.wait_recv()
        base = q * LEVELS
        merged = [
            jnp.where(odd, pltpu.roll(yl[j, q, h], 1, 1), pltpu.roll(yr[j, q, h], BY - 1, 1)) for h in range(2)
        ]
        packed = [jnp.zeros((HALF, BY), f32) for _ in range(2)]
        for s in range(LEVELS):
            z = base + s
            zm = lax.rem(z + NZ - 1, NZ) if s == 0 else z - 1
            zp = lax.rem(z + 1, NZ) if s == LEVELS - 1 else z + 1
            for x in range(BX):
                rr = s * BX + x
                coupling = [cb[z, x, n] for n in range(6)]
                for h in range(2):
                    here = pl.ds(j * RHS + h * HALF, HALF)
                    rows = pl.ds(h * HALF, HALF)
                    centre = v[z, x, here, :]
                    xm = v[z, x - 1, here, :] if x > 0 else xl[j, q, s, rows, :]
                    xp = v[z, x + 1, here, :] if x < BX - 1 else xr[j, q, s, rows, :]
                    ends = pltpu.roll(merged[h], BY - 1 - 2 * rr, 1)
                    ym = jnp.where(lane == 0, ends, pltpu.roll(centre, 1, 1))
                    yp = jnp.where(lane == BY - 1, ends, pltpu.roll(centre, BY - 1, 1))
                    summed = (
                        coupling[0] * xm
                        + coupling[1] * xp
                        + coupling[2] * ym
                        + coupling[3] * yp
                        + coupling[4] * v[zm, x, here, :]
                        + coupling[5] * v[zp, x, here, :]
                    )
                    value = summed if j == 0 else 2.0 * summed - v[z, x, pl.ds((j - 1) * RHS + h * HALF, HALF), :]
                    v[z, x, pl.ds((j + 1) * RHS + h * HALF, HALF), :] = value
                    if j < S - 1:
                        packed[h] = pack(value, rr, packed[h])
        if j < S - 1:
            for h in range(2):
                edge[j + 1, q, h] = packed[h]
            for copy in copies_of(j + 1, q):
                copy.start()

    def lead_products(q):
        total = jnp.zeros((LEAD, 2 * LEAD), f32)
        for s in range(LEVELS):
            wide = jnp.concatenate([v[q * LEVELS + s, x, :LEAD, :] for x in range(BX)], axis=1)
            high, low = split(wide)
            total = total + lax.dot_general(high, jnp.concatenate([high, low], axis=0), NT, preferred_element_type=f32)
        acc_lead[...] += total

    def last_products(q):
        total = jnp.zeros((2 * RHS, 2 * COLS), f32)
        for s in range(LEVELS):
            wide = jnp.concatenate([v[q * LEVELS + s, x] for x in range(BX)], axis=1)
            high, low = split(wide)
            total = total + lax.dot_general(
                jnp.concatenate([high[LEAD:], low[LEAD:]], axis=0),
                jnp.concatenate([high, low], axis=0),
                NT,
                preferred_element_type=f32,
            )
        acc_last[...] += total

    def exchange(phase, buffer, index, count, peer_of, rows):
        part = buffer.at[index, pl.ds(0, rows)]
        return [
            remote(part, part, asend.at[phase, k - 1], arecv.at[phase, k - 1], peer_of(k))
            for k in sorted(range(1, count), key=lambda k: abs(k - count // 2))
        ]

    steps_lead = [
        exchange(0, lead_y, gy, gy_n, y_peer, LEAD // 2),
        exchange(1, lead_z, zi, zg, z_peer, LEAD // 2),
        exchange(2, lead_x, xi, xg, x_peer, LEAD // 2),
    ]
    steps_last = [
        exchange(3, last_y, gy, gy_n, y_peer, PACKED),
        exchange(4, last_z, zi, zg, z_peer, PACKED),
        exchange(5, last_x, xi, xg, x_peer, PACKED),
    ]

    def send(step):
        for copy in step:
            copy.start()

    def collect(step, buffer, rows):
        for copy in step:
            copy.wait_recv()
        total = buffer[0, :rows]
        for k in range(1, len(step) + 1):
            total = total + buffer[k, :rows]
        return total

    acc_lead[...] = jnp.zeros_like(acc_lead)
    acc_last[...] = jnp.zeros_like(acc_last)

    def loop(j, more=None):
        def body(q, carry):
            advance(j, q)
            if more is not None:
                more(q)
            return carry

        lax.fori_loop(0, CHUNKS, body, 0)

    loop(0)
    loop(1)
    loop(2, lead_products)

    partial = acc_lead[...]
    mirrored = jnp.concatenate([partial, jnp.zeros((128 - LEAD, 128), f32)], axis=0).T[LEAD : 2 * LEAD]
    lead_lane = lax.broadcasted_iota(jnp.int32, (LEAD, 128), 1)
    partial = jnp.where(lead_lane < LEAD, partial + pltpu.roll(partial, LEAD, 1), 0.0) + mirrored
    lead_y[gy] = partial[: LEAD // 2] + pltpu.roll(partial[LEAD // 2 :], LEAD, 1)
    send(steps_lead[0])

    def beside(q):
        last_products(q)

        @pl.when(q == CHUNKS - 2)
        def _():
            lead_z[zi] = collect(steps_lead[0], lead_y, LEAD // 2)
            send(steps_lead[1])

    loop(3, beside)

    partial = acc_last[...]
    partial = partial[:RHS, :COLS] + partial[:RHS, COLS:] + partial[RHS:, :COLS]
    last_y[gy, :PACKED] = pack_last(jnp.concatenate([partial, jnp.zeros((RHS, 128 - COLS), f32)], axis=1))
    send(steps_last[0])
    last_z[zi, :PACKED] = collect(steps_last[0], last_y, PACKED)
    send(steps_last[1])
    lead_x[xi] = collect(steps_lead[1], lead_z, LEAD // 2)
    send(steps_lead[2])
    last_x[xi, :PACKED] = collect(steps_last[1], last_z, PACKED)
    send(steps_last[2])
    summed = collect(steps_lead[2], lead_x, LEAD // 2) * (1.0 / cells)
    summed = jnp.concatenate([summed, pltpu.roll(summed, LEAD, 1)], axis=0)
    rows, root = scale_start([summed[8 * b : 8 * b + 8] for b in range(LEAD // 8)], LEAD)
    lead[...] = jnp.concatenate(scale_end(eliminate(rows, 0, LEAD), root, LEAD), axis=0)
    last_gram[...] = unpack_last(collect(steps_last[2], last_x, PACKED)) * (1.0 / cells)

    for copy in kcopies:
        copy.wait_send()

    def drain(q, carry):
        for j in range(S):
            for copy in copies_of(j, q):
                copy.wait_send()
        return carry

    lax.fori_loop(0, CHUNKS, drain, 0)
    for step in steps_lead + steps_last:
        for copy in step:
            copy.wait_send()


def pack_last(block):
    lane = lax.broadcasted_iota(jnp.int32, (8, 128), 1)
    row = lax.broadcasted_iota(jnp.int32, (8, 128), 0)
    packed = [jnp.where(lane < LEAD, block[:8], pltpu.roll(block[8:], LEAD, 1))]
    for h in range(2):
        corner = jnp.where(lane < RHS, pltpu.roll(block[8 * h : 8 * h + 8], LEAD, 1), 0.0)
        spread = corner
        for r in range(1, 8):
            spread = jnp.where(row == r, pltpu.roll(corner, RHS * r, 1), spread)
        packed.append(jnp.sum(spread, axis=0, keepdims=True))
    return jnp.concatenate(packed, axis=0)


def unpack_last(packed):
    lane = lax.broadcasted_iota(jnp.int32, (8, 128), 1)
    row = lax.broadcasted_iota(jnp.int32, (8, 128), 0)
    block = []
    for h in range(2):
        side = packed[:8] if h == 0 else pltpu.roll(packed[:8], LEAD, 1)
        line = jnp.broadcast_to(packed[8 + h : 9 + h], (8, 128))
        corner = pltpu.roll(line, LEAD, 1)
        for r in range(1, 8):
            shift = (LEAD - RHS * r) % 128
            corner = jnp.where(row == r, pltpu.roll(line, shift, 1) if shift else line, corner)
        block.append(jnp.where(lane < LEAD, side, jnp.where(lane < COLS, corner, 0.0)))
    return jnp.concatenate(block, axis=0)


def scale_start(blocks, size):
    lane = lax.broadcasted_iota(jnp.int32, (8, 128), 1)
    row = lax.broadcasted_iota(jnp.int32, (8, 128), 0)
    scales = []
    across = jnp.zeros((1, 128), f32)
    root = jnp.zeros((1, 128), f32)
    for b, block in enumerate(blocks):
        on = lane == row + 8 * b
        diagonal = jnp.sum(jnp.where(on, block, 0.0), axis=1, keepdims=True)
        rooted = jnp.sqrt(diagonal)
        scale = 1.0 / rooted
        scales.append(scale)
        across = across + jnp.sum(jnp.where(on, scale, 0.0), axis=0, keepdims=True)
        root = root + jnp.sum(jnp.where(on, rooted, 0.0), axis=0, keepdims=True)
    rows = [
        jnp.where(lane < size, block * scale * across, jnp.where(lane - size == row + 8 * b, scale, 0.0))
        for b, (block, scale) in enumerate(zip(blocks, scales))
    ]
    return rows, jnp.where(lane[:1] < size, root, 1.0)


def eliminate(rows, begin, end):
    rows = list(rows)
    sub = lax.broadcasted_iota(jnp.int32, (8, 128), 0)

    def along(block, k):
        return jnp.broadcast_to(block[:, k : k + 1], (8, 128))

    def down(block, k):
        return jnp.broadcast_to(block[k : k + 1, :], (8, 128))

    for k in range(begin, end, 4):
        b, s = divmod(k, 8)
        columns = [[along(block, k + t) for block in rows[b:]] for t in range(4)]
        r0, r1, r2, r3 = [down(rows[b], s + t) for t in range(4)]
        p = {(t, u): down(columns[u][0], s + t) for t in range(4) for u in range(t, 4)}
        i0 = 1.0 / p[0, 0]
        l1, l2, l3 = p[0, 1] * i0, p[0, 2] * i0, p[0, 3] * i0
        q11 = p[1, 1] - l1 * p[0, 1]
        q12 = p[1, 2] - l1 * p[0, 2]
        q13 = p[1, 3] - l1 * p[0, 3]
        i1 = 1.0 / q11
        m2, m3 = q12 * i1, q13 * i1
        s22 = p[2, 2] - l2 * p[0, 2] - m2 * q12
        s23 = p[2, 3] - l2 * p[0, 3] - m2 * q13
        s33 = p[3, 3] - l3 * p[0, 3] - m3 * q13
        i2 = 1.0 / s22
        n3 = s23 * i2
        i3 = 1.0 / (s33 - n3 * s23)
        u1 = r1 - l1 * r0
        u2 = r2 - l2 * r0 - m2 * u1
        u3 = r3 - l3 * r0 - m3 * u1 - n3 * u2
        z3 = i3 * u3
        z2 = i2 * u2 - n3 * z3
        z1 = i1 * u1 - m2 * z2 - m3 * z3
        z0 = i0 * r0 - l1 * z1 - l2 * z2 - l3 * z3
        for i in range(b, len(rows)):
            c0, c1, c2, c3 = [column[i - b] for column in columns]
            changed = rows[i] - (c0 * z0 + c1 * z1) - (c2 * z2 + c3 * z3)
            if i == b:
                kept = jnp.where(sub == s + 2, u2, jnp.where(sub == s + 3, u3, rows[i]))
                changed = jnp.where(sub > s + 3, changed, jnp.where(sub == s + 1, u1, kept))
            rows[i] = changed
    return rows


def scale_end(rows, root, size):
    lane = lax.broadcasted_iota(jnp.int32, (8, 128), 1)
    row = lax.broadcasted_iota(jnp.int32, (8, 128), 0)
    done = []
    for b, block in enumerate(rows):
        diagonal = jnp.sum(jnp.where(lane == row + 8 * b, block, 0.0), axis=1, keepdims=True)
        block = jnp.where((lane >= row + 8 * b) & (lane - size <= row + 8 * b), block, 0.0)
        done.append(block * (1.0 / jnp.sqrt(diagonal)) * root)
    return done


def exact(a, b, dims):
    return lax.dot_general(a, b, dims, precision=lax.Precision.HIGHEST, preferred_element_type=f32)


def finish_kernel(v, last_gram, lead, out, r_out, stage, sems):
    upper = lead[:, :LEAD]
    inverse = lead[:, LEAD:]
    against = last_gram[:, :LEAD]
    cross = exact(against, inverse, NT)
    schur = last_gram[:, LEAD:COLS] - exact(cross, cross, NT)
    back = exact(cross, inverse, NN)
    padded = jnp.concatenate([schur, jnp.zeros((RHS, 128 - RHS), f32)], axis=1)
    rows, root = scale_start([padded[:8], padded[8:]], RHS)
    rows = scale_end(eliminate(rows, 0, RHS), root, RHS)
    corner = jnp.concatenate(rows, axis=0)
    corner_upper = corner[:, :RHS]
    corner_inverse = corner[:, RHS : 2 * RHS]
    back = -exact(corner_inverse, back, NN)

    tall = jnp.concatenate([cross, jnp.zeros((RHS, 128 - LEAD), f32)], axis=1)
    tall = jnp.concatenate([tall, jnp.zeros((128 - RHS, 128), f32)], axis=0).T[:LEAD, :RHS]
    r_out[...] = jnp.concatenate(
        [
            jnp.concatenate([upper, tall], axis=1),
            jnp.concatenate([jnp.zeros((RHS, LEAD), f32), corner_upper], axis=1),
        ],
        axis=0,
    )
    whole = jnp.concatenate(
        [
            jnp.concatenate([inverse, jnp.zeros((LEAD, 256 - LEAD), f32)], axis=1),
            jnp.concatenate([back, corner_inverse, jnp.zeros((RHS, 256 - COLS), f32)], axis=1),
        ],
        axis=0,
    )
    high = whole.astype(bf16).astype(f32)
    low = whole - high
    weights = high + pltpu.roll(high, COLS, 1) + pltpu.roll(low, 2 * COLS, 1)
    weights = weights[:, : 3 * COLS].astype(bf16)
    groups = 16
    per = NZ // groups
    copies = []
    for group in range(groups):
        def block(step, carry):
            for s in range(2):
                z = step * 2 + s
                for h in range(2):
                    both = jnp.concatenate([v[z, 2 * h], v[z, 2 * h + 1]], axis=1)
                    vh, vl = split(both)
                    q = jnp.dot(weights, jnp.concatenate([vh, vl, vh], axis=0), preferred_element_type=f32)
                    r = z * BX + 2 * h
                    stage[pl.ds(r, COLS, stride=PITCH), :] = q[:, :BY]
                    stage[pl.ds(r + 1, COLS, stride=PITCH), :] = q[:, BY:]
            return carry

        lax.fori_loop(group * per // 2, (group + 1) * per // 2, block, 0)
        rows = pl.ds(group * per * BX, per * BX)
        copy = pltpu.make_async_copy(
            stage.reshape(COLS, PITCH, BY).at[:, rows, :], out.at[:, rows, :], sems.at[group]
        )
        copy.start()
        copies.append(copy)
    for copy in copies:
        copy.wait()


def per_device(sizes, cells, right_sides, region_labels, face_flags, region_perm):
    gx_n, gy_n, zg, xg = sizes
    vmem = pl.BlockSpec(memory_space=pltpu.VMEM)
    hbm = pl.BlockSpec(memory_space=pltpu.HBM)
    scratch = [
        (CHUNKS * RHS * ROWS, BY),
        (NZ * BX, BY, jnp.int32),
        (2 * BX, BY, jnp.int32),
        (S, CHUNKS, LEVELS, RHS, BY),
        (S, CHUNKS, LEVELS, RHS, BY),
        (S, CHUNKS, 2, HALF, BY),
        (S, CHUNKS, 2, HALF, BY),
        (S, CHUNKS, 2, HALF, BY),
        (BX, NZ, BY),
        (NZ, BY),
        (NZ, BY),
        (NZ, BY),
        (NZ, BY),
        (NZ, BY),
        (6, BX, NZ, BY),
        (NZ, BX, 6, HALF, BY),
        (LEAD, 2 * LEAD),
        (2 * RHS, 2 * COLS),
        (gy_n, LEAD // 2, 128),
        (zg, LEAD // 2, 128),
        (xg, LEAD // 2, 128),
        (gy_n, RHS, 128),
        (zg, RHS, 128),
        (xg, RHS, 128),
    ]
    scratch = [
        pltpu.VMEM(shape[:-1], shape[-1]) if shape[-1] is jnp.int32 else pltpu.VMEM(shape, f32) for shape in scratch
    ]
    dma = pltpu.SemaphoreType.DMA
    scratch += [dma((CHUNKS + 2,)), dma((4,)), dma((4,))]
    scratch += [dma((S, CHUNKS, 2)) for _ in range(4)] + [dma((6, 8)), dma((6, 8))]
    v, last_gram, lead = pl.pallas_call(
        functools.partial(basis_kernel, sizes, cells),
        out_shape=(
            pltpu.VMEM((NZ, BX, COLS, BY), f32),
            pltpu.VMEM((RHS, 128), f32),
            pltpu.VMEM((LEAD, 2 * LEAD), f32),
        ),
        in_specs=[hbm, hbm, hbm, pl.BlockSpec(memory_space=pltpu.SMEM)],
        out_specs=(vmem, vmem, vmem),
        scratch_shapes=scratch,
        compiler_params=pltpu.CompilerParams(
            collective_id=0, has_side_effects=True, vmem_limit_bytes=40 * 1024 * 1024
        ),
        name="basis",
    )(
        *(pltpu.with_memory_space_constraint(a, pltpu.HBM) for a in (
            right_sides.reshape(RHS, NZ * BX, BY),
            region_labels.reshape(NZ * BX, BY),
            face_flags.reshape(2 * BX, BY),
            region_perm,
        )),
    )
    out, upper = pl.pallas_call(
        finish_kernel,
        out_shape=(
            jax.ShapeDtypeStruct((COLS, NZ * BX, BY), f32),
            jax.ShapeDtypeStruct((COLS, COLS), f32),
        ),
        in_specs=[vmem, vmem, vmem],
        out_specs=(hbm, vmem),
        scratch_shapes=[pltpu.VMEM((COLS * PITCH, BY), f32), dma((16,))],
        compiler_params=pltpu.CompilerParams(vmem_limit_bytes=40 * 1024 * 1024),
        name="finish",
    )(v, last_gram, lead)
    return out.reshape(COLS, NZ, BX, BY), upper


def solution(mesh):
    gx_n, gy_n = mesh.shape["gx"], mesh.shape["gy"]
    zg = 8 if gx_n % 8 == 0 else 2
    sizes = (gx_n, gy_n, zg, gx_n // zg)
    cells = NZ * BX * BY * gx_n * gy_n
    placed = (P(None, None, "gx", "gy"), P(None, "gx", "gy"), P(None, "gx", "gy"), P())
    return jax.shard_map(
        functools.partial(per_device, sizes, cells),
        mesh=mesh,
        in_specs=placed,
        out_specs=(P(None, None, "gx", "gy"), P()),
        check_vma=False,
    )
```

```python
import functools
import jax
import jax.numpy as jnp
from jax import lax
from jax.experimental import pallas as pl
from jax.experimental.pallas import tpu as pltpu
from jax.sharding import PartitionSpec as P

RHS = 16
S = 4
VECS = S + 1
COLS = RHS * VECS
NZ = 32
BX = 4
BY = 128
HALF = 8
LEAD = RHS * S
LEVELS = 8
CHUNKS = NZ // LEVELS
ROWS = LEVELS * BX
PITCH = NZ * BX + 8
PACKED = 8 + RHS * RHS // 128
NT = (((1,), (1,)), ((), ()))
NN = (((1,), (0,)), ((), ()))
MESH = pl.DeviceIdType.MESH
f32 = jnp.float32
bf16 = jnp.bfloat16


def split(value):
    high = value.astype(bf16)
    low = (value - high.astype(f32)).astype(bf16)
    return high, low


def harmonic(centre, neighbour):
    summed = centre + neighbour
    return 2.0 * centre * neighbour / jnp.where(summed > 0, summed, 1.0)


def basis_kernel(
    sizes, cells,
    rs, labels_hbm, flags_hbm, perm_hbm,
    v, last_gram, lead,
    stage, labels, flags, perm, halo, edge, kown, kedge, khalo, ct, cb,
    acc_lead, acc_last, lead_y, lead_z, lead_x, last_y, last_z, last_x,
    load_sem, ksem, sent, arrived, asend, arecv,
):
    gx_n, gy_n, zg, xg = sizes
    gx = lax.axis_index("gx")
    gy = lax.axis_index("gy")
    right = lax.rem(gx + 1, gx_n)
    left = lax.rem(gx + gx_n - 1, gx_n)
    above = lax.rem(gy + 1, gy_n)
    below = lax.rem(gy + gy_n - 1, gy_n)
    zi = lax.rem(gx, zg)
    xi = lax.div(gx, zg)

    def z_peer(k):
        return (xi * zg + lax.rem(zi + k, zg), gy)

    def x_peer(k):
        return (lax.rem(xi + k, xg) * zg + zi, gy)

    def y_peer(k):
        return (gx, lax.rem(gy + k, gy_n))

    loads = [
        pltpu.make_async_copy(labels_hbm, labels, load_sem.at[CHUNKS]),
        pltpu.make_async_copy(flags_hbm, flags, load_sem.at[CHUNKS + 1]),
        pltpu.make_async_copy(perm_hbm, perm, load_sem.at[CHUNKS + 2]),
    ]

    def load_of(q):
        return pltpu.make_async_copy(
            rs.at[:, pl.ds(q * ROWS, ROWS), :], stage.reshape(CHUNKS, RHS, ROWS, BY).at[q], load_sem.at[q]
        )

    loads += [load_of(q) for q in range(CHUNKS)]
    for load in loads:
        load.start()
    peers = [z_peer(k) for k in sorted(range(1, zg), key=lambda k: abs(k - zg // 2))]
    peers += [y_peer(k) for k in sorted(range(1, gy_n), key=lambda k: abs(k - gy_n // 2))]
    peers += [x_peer(k) for k in range(1, xg)]
    peers += [(right, gy), (left, gy)]
    barrier = pltpu.get_barrier_semaphore()
    for peer in peers:
        pl.semaphore_signal(barrier, inc=1, device_id=peer, device_id_type=MESH)

    for load in loads[:3]:
        load.wait()
    for x in range(BX):
        label = labels[pl.ds(x, NZ, stride=BX), :]
        value = jnp.zeros((NZ, BY), f32)
        for region in range(perm.shape[0]):
            value = jnp.where(label == region, perm[region], value)
        kown[x] = value

    def remote(src, dst, send, recv, peer):
        return pltpu.make_async_remote_copy(
            src_ref=src, dst_ref=dst, send_sem=send, recv_sem=recv, device_id=peer, device_id_type=MESH
        )

    wide_lane = lax.broadcasted_iota(jnp.int32, (NZ, BY), 1)
    kends = jnp.zeros((NZ, BY), f32)
    for x in range(BX):
        kends = jnp.where(lax.div(wide_lane, 2) == x, pltpu.roll(kown[x], 2 * x + 1, 1), kends)
    kedge[...] = kends
    kcopies = [
        remote(kedge, khalo.at[2], ksem.at[0], ksem.at[1], (gx, above)),
        remote(kedge, khalo.at[3], ksem.at[0], ksem.at[1], (gx, below)),
        remote(kown.at[BX - 1], khalo.at[0], ksem.at[0], ksem.at[1], (right, gy)),
        remote(kown.at[0], khalo.at[1], ksem.at[0], ksem.at[1], (left, gy)),
    ]
    kall = remote(khalo, khalo, ksem.at[0], ksem.at[1], (right, gy))

    def copies_of(j, q):
        levels = pl.ds(q * LEVELS, LEVELS)
        plane = pl.ds(j * RHS, RHS)
        here = halo.at[j, q]
        return [
            remote(v.at[levels, BX - 1, plane, :], here.at[pl.ds(0, LEVELS)], sent.at[0], arrived.at[j, q], (right, gy)),
            remote(v.at[levels, 0, plane, :], here.at[pl.ds(LEVELS, LEVELS)], sent.at[1], arrived.at[j, q], (left, gy)),
            remote(edge.at[j, q], here.at[2 * LEVELS], sent.at[2], arrived.at[j, q], (gx, above)),
            remote(edge.at[j, q], here.at[2 * LEVELS + 1], sent.at[3], arrived.at[j, q], (gx, below)),
        ]

    lane = lax.broadcasted_iota(jnp.int32, (HALF, BY), 1)
    pair = lax.div(lane, 2)
    odd = lax.rem(lane, 2) == 1

    def pack(value, rr, packed):
        return jnp.where(pair == rr, pltpu.roll(value, 2 * rr + 1, 1), packed)

    def relayout(q, carry):
        load_of(q).wait()
        packed = [jnp.zeros((HALF, BY), f32) for _ in range(2)]
        for s in range(LEVELS):
            for x in range(BX):
                rr = s * BX + x
                value = stage[pl.ds(q * RHS * ROWS + rr, RHS, stride=ROWS), :]
                v[q * LEVELS + s, x, :RHS, :] = value
                for h in range(2):
                    packed[h] = pack(value[h * HALF : (h + 1) * HALF], rr, packed[h])
        for h in range(2):
            edge[0, q, pl.ds(h * HALF, HALF)] = packed[h]

        @pl.when(q == 0)
        def _():
            pl.semaphore_wait(barrier, len(peers))
            for copy in kcopies:
                copy.start()

        for copy in copies_of(0, q):
            copy.start()
        return carry

    lax.fori_loop(0, CHUNKS, relayout, 0)

    kall.wait_recv()
    level = lax.broadcasted_iota(jnp.int32, (NZ, BY), 0)
    merged = jnp.where(lax.rem(wide_lane, 2) == 1, pltpu.roll(khalo[2], 1, 1), pltpu.roll(khalo[3], BY - 1, 1))
    for x in range(BX):
        centre = kown[x]
        xm = kown[x - 1] if x > 0 else jnp.where(gx == 0, 0.0, khalo[0])
        xp = kown[x + 1] if x < BX - 1 else jnp.where(gx == gx_n - 1, 0.0, khalo[1])
        ends = pltpu.roll(merged, BY - 1 - 2 * x, 1)
        from_below = jnp.where(gy == 0, 0.0, ends)
        from_above = jnp.where(gy == gy_n - 1, 0.0, ends)
        ym = jnp.where(wide_lane == 0, from_below, pltpu.roll(centre, 1, 1))
        yp = jnp.where(wide_lane == BY - 1, from_above, pltpu.roll(centre, BY - 1, 1))
        zm = jnp.where(level == 0, 0.0, pltpu.roll(centre, 1, 0))
        zp = jnp.where(level == NZ - 1, 0.0, pltpu.roll(centre, NZ - 1, 0))
        t = [harmonic(centre, other) for other in (xm, xp, ym, yp, zm, zp)]
        bottom = flags[pl.ds(x, 1), :].astype(f32)
        top = flags[pl.ds(BX + x, 1), :].astype(f32)
        boundary = jnp.where(level == 0, 2.0 * centre * bottom, 0.0)
        boundary = boundary + jnp.where(level == NZ - 1, 2.0 * centre * top, 0.0)
        diagonal = t[0] + t[1] + t[2] + t[3] + t[4] + t[5] + boundary
        divisor = jnp.where(diagonal > 0, diagonal, 1.0)
        for n in range(6):
            ct[n, x] = -(t[n] / divisor)

    def spread(block, carry):
        for n in range(6):
            for x in range(BX):
                rows = ct[n, x, pl.ds(pl.multiple_of(block * 8, 8), 8), :]
                for s in range(8):
                    cb[block * 8 + s, x, n] = jnp.broadcast_to(rows[s : s + 1, :], (HALF, BY))
        return carry

    lax.fori_loop(0, NZ // 8, spread, 0)

    def advance(j, q):
        remote(halo.at[j, q], halo.at[j, q], sent.at[0], arrived.at[j, q], (right, gy)).wait_recv()
        base = q * LEVELS
        merged = [
            jnp.where(
                odd,
                pltpu.roll(halo[j, q, 2 * LEVELS, pl.ds(h * HALF, HALF), :], 1, 1),
                pltpu.roll(halo[j, q, 2 * LEVELS + 1, pl.ds(h * HALF, HALF), :], BY - 1, 1),
            )
            for h in range(2)
        ]
        packed = [jnp.zeros((HALF, BY), f32) for _ in range(2)]
        for s in range(LEVELS):
            z = base + s
            zm = lax.rem(z + NZ - 1, NZ) if s == 0 else z - 1
            zp = lax.rem(z + 1, NZ) if s == LEVELS - 1 else z + 1
            for x in range(BX):
                rr = s * BX + x
                coupling = [cb[z, x, n] for n in range(6)]
                for h in range(2):
                    here = pl.ds(j * RHS + h * HALF, HALF)
                    rows = pl.ds(h * HALF, HALF)
                    centre = v[z, x, here, :]
                    xm = v[z, x - 1, here, :] if x > 0 else halo[j, q, s, rows, :]
                    xp = v[z, x + 1, here, :] if x < BX - 1 else halo[j, q, LEVELS + s, rows, :]
                    ends = pltpu.roll(merged[h], BY - 1 - 2 * rr, 1)
                    ym = jnp.where(lane == 0, ends, pltpu.roll(centre, 1, 1))
                    yp = jnp.where(lane == BY - 1, ends, pltpu.roll(centre, BY - 1, 1))
                    summed = (
                        coupling[0] * xm
                        + coupling[1] * xp
                        + coupling[2] * ym
                        + coupling[3] * yp
                        + coupling[4] * v[zm, x, here, :]
                        + coupling[5] * v[zp, x, here, :]
                    )
                    value = summed if j == 0 else 2.0 * summed - v[z, x, pl.ds((j - 1) * RHS + h * HALF, HALF), :]
                    v[z, x, pl.ds((j + 1) * RHS + h * HALF, HALF), :] = value
                    if j < S - 1:
                        packed[h] = pack(value, rr, packed[h])
        if j < S - 1:
            for h in range(2):
                edge[j + 1, q, pl.ds(h * HALF, HALF)] = packed[h]
            for copy in copies_of(j + 1, q):
                copy.start()

    def lead_products(q):
        total = jnp.zeros((LEAD, 2 * LEAD), f32)
        for s in range(LEVELS):
            wide = jnp.concatenate([v[q * LEVELS + s, x, :LEAD, :] for x in range(BX)], axis=1)
            high, low = split(wide)
            total = total + lax.dot_general(high, jnp.concatenate([high, low], axis=0), NT, preferred_element_type=f32)
        acc_lead[...] += total

    def last_products(q):
        total = jnp.zeros((2 * RHS, 2 * COLS), f32)
        for s in range(LEVELS):
            wide = jnp.concatenate([v[q * LEVELS + s, x] for x in range(BX)], axis=1)
            high, low = split(wide)
            total = total + lax.dot_general(
                jnp.concatenate([high[LEAD:], low[LEAD:]], axis=0),
                jnp.concatenate([high, low], axis=0),
                NT,
                preferred_element_type=f32,
            )
        acc_last[...] += total

    def exchange(phase, buffer, index, count, peer_of, rows):
        part = buffer.at[index, pl.ds(0, rows)]
        return [
            remote(part, part, asend.at[phase], arecv.at[phase], peer_of(k))
            for k in sorted(range(1, count), key=lambda k: abs(k - count // 2))
        ], remote(
            buffer.at[pl.ds(0, count - 1), pl.ds(0, rows)],
            buffer.at[pl.ds(0, count - 1), pl.ds(0, rows)],
            asend.at[phase],
            arecv.at[phase],
            peer_of(1),
        )

    steps_lead = [
        exchange(0, lead_y, gy, gy_n, y_peer, LEAD // 2),
        exchange(1, lead_z, zi, zg, z_peer, LEAD // 2),
        exchange(2, lead_x, xi, xg, x_peer, LEAD // 2),
    ]
    steps_last = [
        exchange(3, last_y, gy, gy_n, y_peer, PACKED),
        exchange(4, last_z, zi, zg, z_peer, PACKED),
        exchange(5, last_x, xi, xg, x_peer, PACKED),
    ]

    def send(step):
        for copy in step[0]:
            copy.start()

    def collect(step, buffer, rows):
        step[1].wait_recv()
        total = buffer[0, :rows]
        for k in range(1, len(step[0]) + 1):
            total = total + buffer[k, :rows]
        return total

    acc_lead[...] = jnp.zeros_like(acc_lead)
    acc_last[...] = jnp.zeros_like(acc_last)

    def loop(j, more=None):
        def body(q, carry):
            advance(j, q)
            if more is not None:
                more(q)
            return carry

        lax.fori_loop(0, CHUNKS, body, 0)

    loop(0)
    loop(1)
    loop(2, lead_products)

    partial = acc_lead[...]
    mirrored = jnp.concatenate([partial, jnp.zeros((128 - LEAD, 128), f32)], axis=0).T[LEAD : 2 * LEAD]
    lead_lane = lax.broadcasted_iota(jnp.int32, (LEAD, 128), 1)
    partial = jnp.where(lead_lane < LEAD, partial + pltpu.roll(partial, LEAD, 1), 0.0) + mirrored
    lead_y[gy] = partial[: LEAD // 2] + pltpu.roll(partial[LEAD // 2 :], LEAD, 1)
    send(steps_lead[0])

    def beside(q):
        last_products(q)

        @pl.when(q == CHUNKS - 2)
        def _():
            lead_z[zi] = collect(steps_lead[0], lead_y, LEAD // 2)
            send(steps_lead[1])

    loop(3, beside)

    partial = acc_last[...]
    partial = partial[:RHS, :COLS] + partial[:RHS, COLS:] + partial[RHS:, :COLS]
    last_y[gy, :PACKED] = pack_last(jnp.concatenate([partial, jnp.zeros((RHS, 128 - COLS), f32)], axis=1))
    send(steps_last[0])
    kall.wait_send()
    for i in range(2):
        columns = halo.at[:, :, pl.ds(0, LEVELS)]
        remote(columns, columns, sent.at[i], arrived.at[0, 0], (right, gy)).wait_send()
        remote(edge, edge, sent.at[2 + i], arrived.at[0, 0], (right, gy)).wait_send()
    last_z[zi, :PACKED] = collect(steps_last[0], last_y, PACKED)
    send(steps_last[1])
    lead_x[xi] = collect(steps_lead[1], lead_z, LEAD // 2)
    send(steps_lead[2])
    last_x[xi, :PACKED] = collect(steps_last[1], last_z, PACKED)
    send(steps_last[2])
    summed = collect(steps_lead[2], lead_x, LEAD // 2) * (1.0 / cells)
    summed = jnp.concatenate([summed, pltpu.roll(summed, LEAD, 1)], axis=0)
    rows, root = scale_start([summed[8 * b : 8 * b + 8] for b in range(LEAD // 8)], LEAD)
    lead[...] = jnp.concatenate(scale_end(eliminate(rows, 0, LEAD), root, LEAD), axis=0)
    last_gram[...] = unpack_last(collect(steps_last[2], last_x, PACKED)) * (1.0 / cells)

    for step in steps_lead + steps_last:
        step[1].wait_send()


def pack_last(block):
    lane = lax.broadcasted_iota(jnp.int32, (8, 128), 1)
    row = lax.broadcasted_iota(jnp.int32, (8, 128), 0)
    packed = [jnp.where(lane < LEAD, block[:8], pltpu.roll(block[8:], LEAD, 1))]
    for h in range(2):
        corner = jnp.where(lane < RHS, pltpu.roll(block[8 * h : 8 * h + 8], LEAD, 1), 0.0)
        spread = corner
        for r in range(1, 8):
            spread = jnp.where(row == r, pltpu.roll(corner, RHS * r, 1), spread)
        packed.append(jnp.sum(spread, axis=0, keepdims=True))
    return jnp.concatenate(packed, axis=0)


def unpack_last(packed):
    lane = lax.broadcasted_iota(jnp.int32, (8, 128), 1)
    row = lax.broadcasted_iota(jnp.int32, (8, 128), 0)
    block = []
    for h in range(2):
        side = packed[:8] if h == 0 else pltpu.roll(packed[:8], LEAD, 1)
        line = jnp.broadcast_to(packed[8 + h : 9 + h], (8, 128))
        corner = pltpu.roll(line, LEAD, 1)
        for r in range(1, 8):
            shift = (LEAD - RHS * r) % 128
            corner = jnp.where(row == r, pltpu.roll(line, shift, 1) if shift else line, corner)
        block.append(jnp.where(lane < LEAD, side, jnp.where(lane < COLS, corner, 0.0)))
    return jnp.concatenate(block, axis=0)


def scale_start(blocks, size):
    lane = lax.broadcasted_iota(jnp.int32, (8, 128), 1)
    row = lax.broadcasted_iota(jnp.int32, (8, 128), 0)
    scales = []
    across = jnp.zeros((1, 128), f32)
    root = jnp.zeros((1, 128), f32)
    for b, block in enumerate(blocks):
        on = lane == row + 8 * b
        diagonal = jnp.sum(jnp.where(on, block, 0.0), axis=1, keepdims=True)
        rooted = jnp.sqrt(diagonal)
        scale = 1.0 / rooted
        scales.append(scale)
        across = across + jnp.sum(jnp.where(on, scale, 0.0), axis=0, keepdims=True)
        root = root + jnp.sum(jnp.where(on, rooted, 0.0), axis=0, keepdims=True)
    rows = [
        jnp.where(lane < size, block * scale * across, jnp.where(lane - size == row + 8 * b, scale, 0.0))
        for b, (block, scale) in enumerate(zip(blocks, scales))
    ]
    return rows, jnp.where(lane[:1] < size, root, 1.0)


def eliminate(rows, begin, end):
    rows = list(rows)
    sub = lax.broadcasted_iota(jnp.int32, (8, 128), 0)

    def along(block, k):
        return jnp.broadcast_to(block[:, k : k + 1], (8, 128))

    def down(block, k):
        return jnp.broadcast_to(block[k : k + 1, :], (8, 128))

    for k in range(begin, end, 4):
        b, s = divmod(k, 8)
        columns = [[along(block, k + t) for block in rows[b:]] for t in range(4)]
        r0, r1, r2, r3 = [down(rows[b], s + t) for t in range(4)]
        p = {(t, u): down(columns[u][0], s + t) for t in range(4) for u in range(t, 4)}
        i0 = 1.0 / p[0, 0]
        l1, l2, l3 = p[0, 1] * i0, p[0, 2] * i0, p[0, 3] * i0
        q11 = p[1, 1] - l1 * p[0, 1]
        q12 = p[1, 2] - l1 * p[0, 2]
        q13 = p[1, 3] - l1 * p[0, 3]
        i1 = 1.0 / q11
        m2, m3 = q12 * i1, q13 * i1
        s22 = p[2, 2] - l2 * p[0, 2] - m2 * q12
        s23 = p[2, 3] - l2 * p[0, 3] - m2 * q13
        s33 = p[3, 3] - l3 * p[0, 3] - m3 * q13
        i2 = 1.0 / s22
        n3 = s23 * i2
        i3 = 1.0 / (s33 - n3 * s23)
        u1 = r1 - l1 * r0
        u2 = r2 - l2 * r0 - m2 * u1
        u3 = r3 - l3 * r0 - m3 * u1 - n3 * u2
        z3 = i3 * u3
        z2 = i2 * u2 - n3 * z3
        z1 = i1 * u1 - m2 * z2 - m3 * z3
        z0 = i0 * r0 - l1 * z1 - l2 * z2 - l3 * z3
        for i in range(b, len(rows)):
            c0, c1, c2, c3 = [column[i - b] for column in columns]
            changed = rows[i] - (c0 * z0 + c1 * z1) - (c2 * z2 + c3 * z3)
            if i == b:
                kept = jnp.where(sub == s + 2, u2, jnp.where(sub == s + 3, u3, rows[i]))
                changed = jnp.where(sub > s + 3, changed, jnp.where(sub == s + 1, u1, kept))
            rows[i] = changed
    return rows


def scale_end(rows, root, size):
    lane = lax.broadcasted_iota(jnp.int32, (8, 128), 1)
    row = lax.broadcasted_iota(jnp.int32, (8, 128), 0)
    done = []
    for b, block in enumerate(rows):
        diagonal = jnp.sum(jnp.where(lane == row + 8 * b, block, 0.0), axis=1, keepdims=True)
        block = jnp.where((lane >= row + 8 * b) & (lane - size <= row + 8 * b), block, 0.0)
        done.append(block * (1.0 / jnp.sqrt(diagonal)) * root)
    return done


def exact(a, b, dims):
    return lax.dot_general(a, b, dims, precision=lax.Precision.HIGHEST, preferred_element_type=f32)


def finish_kernel(v, last_gram, lead, out, r_out, stage, sems):
    upper = lead[:, :LEAD]
    inverse = lead[:, LEAD:]
    against = last_gram[:, :LEAD]
    cross = exact(against, inverse, NT)
    schur = last_gram[:, LEAD:COLS] - exact(cross, cross, NT)
    back = exact(cross, inverse, NN)
    padded = jnp.concatenate([schur, jnp.zeros((RHS, 128 - RHS), f32)], axis=1)
    rows, root = scale_start([padded[:8], padded[8:]], RHS)
    rows = scale_end(eliminate(rows, 0, RHS), root, RHS)
    corner = jnp.concatenate(rows, axis=0)
    corner_upper = corner[:, :RHS]
    corner_inverse = corner[:, RHS : 2 * RHS]
    back = -exact(corner_inverse, back, NN)

    tall = jnp.concatenate([cross, jnp.zeros((RHS, 128 - LEAD), f32)], axis=1)
    tall = jnp.concatenate([tall, jnp.zeros((128 - RHS, 128), f32)], axis=0).T[:LEAD, :RHS]
    r_out[...] = jnp.concatenate(
        [
            jnp.concatenate([upper, tall], axis=1),
            jnp.concatenate([jnp.zeros((RHS, LEAD), f32), corner_upper], axis=1),
        ],
        axis=0,
    )
    whole = jnp.concatenate(
        [
            jnp.concatenate([inverse, jnp.zeros((LEAD, 256 - LEAD), f32)], axis=1),
            jnp.concatenate([back, corner_inverse, jnp.zeros((RHS, 256 - COLS), f32)], axis=1),
        ],
        axis=0,
    )
    high = whole.astype(bf16).astype(f32)
    low = whole - high
    weights = high + pltpu.roll(high, COLS, 1) + pltpu.roll(low, 2 * COLS, 1)
    weights = weights[:, : 3 * COLS].astype(bf16)
    groups = 16
    per = NZ // groups
    copies = []
    for group in range(groups):
        def block(step, carry):
            for s in range(2):
                z = step * 2 + s
                for h in range(2):
                    both = jnp.concatenate([v[z, 2 * h], v[z, 2 * h + 1]], axis=1)
                    vh, vl = split(both)
                    q = jnp.dot(weights, jnp.concatenate([vh, vl, vh], axis=0), preferred_element_type=f32)
                    r = z * BX + 2 * h
                    stage[pl.ds(r, COLS, stride=PITCH), :] = q[:, :BY]
                    stage[pl.ds(r + 1, COLS, stride=PITCH), :] = q[:, BY:]
            return carry

        lax.fori_loop(group * per // 2, (group + 1) * per // 2, block, 0)
        rows = pl.ds(group * per * BX, per * BX)
        copy = pltpu.make_async_copy(
            stage.reshape(COLS, PITCH, BY).at[:, rows, :], out.at[:, rows, :], sems.at[group]
        )
        copy.start()
        copies.append(copy)
    for copy in copies:
        copy.wait()


def per_device(sizes, cells, right_sides, region_labels, face_flags, region_perm):
    gx_n, gy_n, zg, xg = sizes
    vmem = pl.BlockSpec(memory_space=pltpu.VMEM)
    hbm = pl.BlockSpec(memory_space=pltpu.HBM)
    scratch = [
        (CHUNKS * RHS * ROWS, BY),
        (NZ * BX, BY, jnp.int32),
        (2 * BX, BY, jnp.int32),
        None,
        (S, CHUNKS, 2 * LEVELS + 2, RHS, BY),
        (S, CHUNKS, RHS, BY),
        (BX, NZ, BY),
        (NZ, BY),
        (4, NZ, BY),
        (6, BX, NZ, BY),
        (NZ, BX, 6, HALF, BY),
        (LEAD, 2 * LEAD),
        (2 * RHS, 2 * COLS),
        (gy_n, LEAD // 2, 128),
        (zg, LEAD // 2, 128),
        (xg, LEAD // 2, 128),
        (gy_n, RHS, 128),
        (zg, RHS, 128),
        (xg, RHS, 128),
    ]
    scratch = [
        pltpu.SMEM(region_perm.shape, f32) if shape is None
        else pltpu.VMEM(shape[:-1], shape[-1]) if shape[-1] is jnp.int32
        else pltpu.VMEM(shape, f32)
        for shape in scratch
    ]
    dma = pltpu.SemaphoreType.DMA
    scratch += [dma((CHUNKS + 3,)), dma((2,)), dma((4,)), dma((S, CHUNKS)), dma((6,)), dma((6,))]
    v, last_gram, lead = pl.pallas_call(
        functools.partial(basis_kernel, sizes, cells),
        out_shape=(
            pltpu.VMEM((NZ, BX, COLS, BY), f32),
            pltpu.VMEM((RHS, 128), f32),
            pltpu.VMEM((LEAD, 2 * LEAD), f32),
        ),
        in_specs=[hbm, hbm, hbm, hbm],
        out_specs=(vmem, vmem, vmem),
        scratch_shapes=scratch,
        compiler_params=pltpu.CompilerParams(
            collective_id=0, has_side_effects=True, vmem_limit_bytes=40 * 1024 * 1024
        ),
        name="basis",
    )(
        *(pltpu.with_memory_space_constraint(a, pltpu.HBM) for a in (
            right_sides.reshape(RHS, NZ * BX, BY),
            region_labels.reshape(NZ * BX, BY),
            face_flags.reshape(2 * BX, BY),
            region_perm,
        )),
    )
    out, upper = pl.pallas_call(
        finish_kernel,
        out_shape=(
            jax.ShapeDtypeStruct((COLS, NZ * BX, BY), f32),
            jax.ShapeDtypeStruct((COLS, COLS), f32),
        ),
        in_specs=[vmem, vmem, vmem],
        out_specs=(hbm, vmem),
        scratch_shapes=[pltpu.VMEM((COLS * PITCH, BY), f32), dma((16,))],
        compiler_params=pltpu.CompilerParams(vmem_limit_bytes=40 * 1024 * 1024),
        name="finish",
    )(v, last_gram, lead)
    return out.reshape(COLS, NZ, BX, BY), upper


def solution(mesh):
    gx_n, gy_n = mesh.shape["gx"], mesh.shape["gy"]
    zg = 8 if gx_n % 8 == 0 else 2
    sizes = (gx_n, gy_n, zg, gx_n // zg)
    cells = NZ * BX * BY * gx_n * gy_n
    placed = (P(None, None, "gx", "gy"), P(None, "gx", "gy"), P(None, "gx", "gy"), P())
    return jax.shard_map(
        functools.partial(per_device, sizes, cells),
        mesh=mesh,
        in_specs=placed,
        out_specs=(P(None, None, "gx", "gy"), P()),
        check_vma=False,
    )
```

```python
import functools
import jax
import jax.numpy as jnp
from jax import lax
from jax.experimental import pallas as pl
from jax.experimental.pallas import tpu as pltpu
from jax.sharding import PartitionSpec as P

RHS = 16
S = 4
VECS = S + 1
COLS = RHS * VECS
NZ = 32
BX = 4
BY = 128
HALF = 8
LEAD = RHS * S
LEVELS = 8
CHUNKS = NZ // LEVELS
ROWS = LEVELS * BX
PITCH = NZ * BX + 8
PACKED = 8 + RHS * RHS // 128
NT = (((1,), (1,)), ((), ()))
NN = (((1,), (0,)), ((), ()))
MESH = pl.DeviceIdType.MESH
f32 = jnp.float32
bf16 = jnp.bfloat16


def split(value):
    high = value.astype(bf16)
    low = (value - high.astype(f32)).astype(bf16)
    return high, low


def harmonic(centre, neighbour):
    summed = centre + neighbour
    return 2.0 * centre * neighbour / jnp.where(summed > 0, summed, 1.0)


def basis_kernel(
    sizes, cells,
    rs, labels_hbm, flags_hbm, perm_hbm,
    v, last_gram, lead,
    stage, labels, flags, perm, halo, edge, kown, kedge, khalo, ct, cb,
    acc_lead, acc_last, lead_y, lead_z, lead_x, last_y, last_z, last_x,
    load_sem, ksem, sent, arrived, asend, arecv,
):
    gx_n, gy_n, zg, xg = sizes
    gx = lax.axis_index("gx")
    gy = lax.axis_index("gy")
    right = lax.rem(gx + 1, gx_n)
    left = lax.rem(gx + gx_n - 1, gx_n)
    above = lax.rem(gy + 1, gy_n)
    below = lax.rem(gy + gy_n - 1, gy_n)
    zi = lax.rem(gx, zg)
    xi = lax.div(gx, zg)

    def z_peer(k):
        return (xi * zg + lax.rem(zi + k, zg), gy)

    def x_peer(k):
        return (lax.rem(xi + k, xg) * zg + zi, gy)

    def y_peer(k):
        return (gx, lax.rem(gy + k, gy_n))

    loads = [
        pltpu.make_async_copy(labels_hbm, labels, load_sem.at[CHUNKS]),
        pltpu.make_async_copy(flags_hbm, flags, load_sem.at[CHUNKS + 1]),
        pltpu.make_async_copy(perm_hbm, perm, load_sem.at[CHUNKS + 2]),
    ]

    def load_of(q):
        return pltpu.make_async_copy(
            rs.at[:, pl.ds(q * ROWS, ROWS), :], stage.reshape(CHUNKS, RHS, ROWS, BY).at[q], load_sem.at[q]
        )

    loads += [load_of(q) for q in range(CHUNKS)]
    for load in loads:
        load.start()
    peers = [z_peer(k) for k in sorted(range(1, zg), key=lambda k: abs(k - zg // 2))]
    peers += [y_peer(k) for k in sorted(range(1, gy_n), key=lambda k: abs(k - gy_n // 2))]
    peers += [x_peer(k) for k in range(1, xg)]
    peers += [(right, gy), (left, gy)]
    barrier = pltpu.get_barrier_semaphore()
    for peer in peers:
        pl.semaphore_signal(barrier, inc=1, device_id=peer, device_id_type=MESH)

    for load in loads[:3]:
        load.wait()
    for x in range(BX):
        label = labels[pl.ds(x, NZ, stride=BX), :]
        value = jnp.zeros((NZ, BY), f32)
        for region in range(perm.shape[0]):
            value = jnp.where(label == region, perm[region], value)
        kown[x] = value

    def remote(src, dst, send, recv, peer):
        return pltpu.make_async_remote_copy(
            src_ref=src, dst_ref=dst, send_sem=send, recv_sem=recv, device_id=peer, device_id_type=MESH
        )

    wide_lane = lax.broadcasted_iota(jnp.int32, (NZ, BY), 1)
    kends = jnp.zeros((NZ, BY), f32)
    for x in range(BX):
        kends = jnp.where(lax.div(wide_lane, 2) == x, pltpu.roll(kown[x], 2 * x + 1, 1), kends)
    kedge[...] = kends
    kcopies = [
        remote(kedge, khalo.at[2], ksem.at[0], ksem.at[1], (gx, above)),
        remote(kedge, khalo.at[3], ksem.at[0], ksem.at[1], (gx, below)),
        remote(kown.at[BX - 1], khalo.at[0], ksem.at[0], ksem.at[1], (right, gy)),
        remote(kown.at[0], khalo.at[1], ksem.at[0], ksem.at[1], (left, gy)),
    ]
    kall = remote(khalo, khalo, ksem.at[0], ksem.at[1], (right, gy))

    def copies_of(j, q):
        levels = pl.ds(q * LEVELS, LEVELS)
        plane = pl.ds(j * RHS, RHS)
        here = halo.at[j, q]
        return [
            remote(v.at[levels, BX - 1, plane, :], here.at[pl.ds(0, LEVELS)], sent.at[0], arrived.at[j, q], (right, gy)),
            remote(v.at[levels, 0, plane, :], here.at[pl.ds(LEVELS, LEVELS)], sent.at[1], arrived.at[j, q], (left, gy)),
            remote(edge.at[j, q], here.at[2 * LEVELS], sent.at[2], arrived.at[j, q], (gx, above)),
            remote(edge.at[j, q], here.at[2 * LEVELS + 1], sent.at[3], arrived.at[j, q], (gx, below)),
        ]

    lane = lax.broadcasted_iota(jnp.int32, (HALF, BY), 1)
    pair = lax.div(lane, 2)
    odd = lax.rem(lane, 2) == 1

    def pack(value, rr, packed):
        return jnp.where(pair == rr, pltpu.roll(value, 2 * rr + 1, 1), packed)

    def relayout(q, carry):
        load_of(q).wait()
        packed = [jnp.zeros((HALF, BY), f32) for _ in range(2)]
        for s in range(LEVELS):
            for x in range(BX):
                rr = s * BX + x
                value = stage[pl.ds(q * RHS * ROWS + rr, RHS, stride=ROWS), :]
                v[q * LEVELS + s, x, :RHS, :] = value
                for h in range(2):
                    packed[h] = pack(value[h * HALF : (h + 1) * HALF], rr, packed[h])
        for h in range(2):
            edge[0, q, pl.ds(h * HALF, HALF)] = packed[h]

        @pl.when(q == 0)
        def _():
            pl.semaphore_wait(barrier, len(peers))
            for copy in kcopies:
                copy.start()

        for copy in copies_of(0, q):
            copy.start()
        return carry

    lax.fori_loop(0, CHUNKS, relayout, 0)

    kall.wait_recv()
    level = lax.broadcasted_iota(jnp.int32, (NZ, BY), 0)
    merged = jnp.where(lax.rem(wide_lane, 2) == 1, pltpu.roll(khalo[2], 1, 1), pltpu.roll(khalo[3], BY - 1, 1))
    for x in range(BX):
        centre = kown[x]
        xm = kown[x - 1] if x > 0 else jnp.where(gx == 0, 0.0, khalo[0])
        xp = kown[x + 1] if x < BX - 1 else jnp.where(gx == gx_n - 1, 0.0, khalo[1])
        ends = pltpu.roll(merged, BY - 1 - 2 * x, 1)
        from_below = jnp.where(gy == 0, 0.0, ends)
        from_above = jnp.where(gy == gy_n - 1, 0.0, ends)
        ym = jnp.where(wide_lane == 0, from_below, pltpu.roll(centre, 1, 1))
        yp = jnp.where(wide_lane == BY - 1, from_above, pltpu.roll(centre, BY - 1, 1))
        zm = jnp.where(level == 0, 0.0, pltpu.roll(centre, 1, 0))
        zp = jnp.where(level == NZ - 1, 0.0, pltpu.roll(centre, NZ - 1, 0))
        t = [harmonic(centre, other) for other in (xm, xp, ym, yp, zm, zp)]
        bottom = flags[pl.ds(x, 1), :].astype(f32)
        top = flags[pl.ds(BX + x, 1), :].astype(f32)
        boundary = jnp.where(level == 0, 2.0 * centre * bottom, 0.0)
        boundary = boundary + jnp.where(level == NZ - 1, 2.0 * centre * top, 0.0)
        diagonal = t[0] + t[1] + t[2] + t[3] + t[4] + t[5] + boundary
        divisor = jnp.where(diagonal > 0, diagonal, 1.0)
        for n in range(6):
            ct[n, x] = -(t[n] / divisor)

    def spread(block, carry):
        for n in range(6):
            for x in range(BX):
                rows = ct[n, x, pl.ds(pl.multiple_of(block * 8, 8), 8), :]
                for s in range(8):
                    cb[block * 8 + s, x, n] = jnp.broadcast_to(rows[s : s + 1, :], (HALF, BY))
        return carry

    lax.fori_loop(0, NZ // 8, spread, 0)

    def advance(j, q):
        remote(halo.at[j, q], halo.at[j, q], sent.at[0], arrived.at[j, q], (right, gy)).wait_recv()
        base = q * LEVELS
        merged = [
            jnp.where(
                odd,
                pltpu.roll(halo[j, q, 2 * LEVELS, pl.ds(h * HALF, HALF), :], 1, 1),
                pltpu.roll(halo[j, q, 2 * LEVELS + 1, pl.ds(h * HALF, HALF), :], BY - 1, 1),
            )
            for h in range(2)
        ]
        packed = [jnp.zeros((HALF, BY), f32) for _ in range(2)]
        for s in range(LEVELS):
            z = base + s
            zm = lax.rem(z + NZ - 1, NZ) if s == 0 else z - 1
            zp = lax.rem(z + 1, NZ) if s == LEVELS - 1 else z + 1
            for x in range(BX):
                rr = s * BX + x
                coupling = [cb[z, x, n] for n in range(6)]
                for h in range(2):
                    here = pl.ds(j * RHS + h * HALF, HALF)
                    rows = pl.ds(h * HALF, HALF)
                    centre = v[z, x, here, :]
                    xm = v[z, x - 1, here, :] if x > 0 else halo[j, q, s, rows, :]
                    xp = v[z, x + 1, here, :] if x < BX - 1 else halo[j, q, LEVELS + s, rows, :]
                    ends = pltpu.roll(merged[h], BY - 1 - 2 * rr, 1)
                    ym = jnp.where(lane == 0, ends, pltpu.roll(centre, 1, 1))
                    yp = jnp.where(lane == BY - 1, ends, pltpu.roll(centre, BY - 1, 1))
                    summed = (
                        coupling[0] * xm
                        + coupling[1] * xp
                        + coupling[2] * ym
                        + coupling[3] * yp
                        + coupling[4] * v[zm, x, here, :]
                        + coupling[5] * v[zp, x, here, :]
                    )
                    value = summed if j == 0 else 2.0 * summed - v[z, x, pl.ds((j - 1) * RHS + h * HALF, HALF), :]
                    v[z, x, pl.ds((j + 1) * RHS + h * HALF, HALF), :] = value
                    if j < S - 1:
                        packed[h] = pack(value, rr, packed[h])
        if j < S - 1:
            for h in range(2):
                edge[j + 1, q, pl.ds(h * HALF, HALF)] = packed[h]
            for copy in copies_of(j + 1, q):
                copy.start()

    def lead_products(q):
        total = jnp.zeros((LEAD, 2 * LEAD), f32)
        for s in range(LEVELS):
            wide = jnp.concatenate([v[q * LEVELS + s, x, :LEAD, :] for x in range(BX)], axis=1)
            high, low = split(wide)
            total = total + lax.dot_general(high, jnp.concatenate([high, low], axis=0), NT, preferred_element_type=f32)
        acc_lead[...] += total

    def last_products(q):
        total = jnp.zeros((2 * RHS, 2 * COLS), f32)
        for s in range(LEVELS):
            wide = jnp.concatenate([v[q * LEVELS + s, x] for x in range(BX)], axis=1)
            high, low = split(wide)
            total = total + lax.dot_general(
                jnp.concatenate([high[LEAD:], low[LEAD:]], axis=0),
                jnp.concatenate([high, low], axis=0),
                NT,
                preferred_element_type=f32,
            )
        acc_last[...] += total

    def exchange(phase, buffer, index, count, peer_of, rows):
        part = buffer.at[index, pl.ds(0, rows)]
        return [
            remote(part, part, asend.at[phase], arecv.at[phase], peer_of(k))
            for k in sorted(range(1, count), key=lambda k: abs(k - count // 2))
        ], remote(
            buffer.at[pl.ds(0, count - 1), pl.ds(0, rows)],
            buffer.at[pl.ds(0, count - 1), pl.ds(0, rows)],
            asend.at[phase],
            arecv.at[phase],
            peer_of(1),
        )

    steps_lead = [
        exchange(0, lead_y, gy, gy_n, y_peer, LEAD // 2),
        exchange(1, lead_z, zi, zg, z_peer, LEAD // 2),
        exchange(2, lead_x, xi, xg, x_peer, LEAD // 2),
    ]
    steps_last = [
        exchange(3, last_y, gy, gy_n, y_peer, PACKED),
        exchange(4, last_z, zi, zg, z_peer, PACKED),
        exchange(5, last_x, xi, xg, x_peer, PACKED),
    ]

    def send(step):
        for copy in step[0]:
            copy.start()

    def collect(step, buffer, rows):
        step[1].wait_recv()
        total = buffer[0, :rows]
        for k in range(1, len(step[0]) + 1):
            total = total + buffer[k, :rows]
        return total

    acc_lead[...] = jnp.zeros_like(acc_lead)
    acc_last[...] = jnp.zeros_like(acc_last)

    def loop(j, more=None):
        def body(q, carry):
            advance(j, q)
            if more is not None:
                more(q)
            return carry

        lax.fori_loop(0, CHUNKS, body, 0)

    loop(0)
    loop(1)
    loop(2, lead_products)

    partial = acc_lead[...]
    mirrored = jnp.concatenate([partial, jnp.zeros((128 - LEAD, 128), f32)], axis=0).T[LEAD : 2 * LEAD]
    lead_lane = lax.broadcasted_iota(jnp.int32, (LEAD, 128), 1)
    partial = jnp.where(lead_lane < LEAD, partial + pltpu.roll(partial, LEAD, 1), 0.0) + mirrored
    lead_y[gy] = partial[: LEAD // 2] + pltpu.roll(partial[LEAD // 2 :], LEAD, 1)
    send(steps_lead[0])

    def beside(q):
        last_products(q)

        @pl.when(q == CHUNKS - 2)
        def _():
            lead_z[zi] = collect(steps_lead[0], lead_y, LEAD // 2)
            send(steps_lead[1])

    loop(3, beside)

    partial = acc_last[...]
    partial = partial[:RHS, :COLS] + partial[:RHS, COLS:] + partial[RHS:, :COLS]
    last_y[gy, :PACKED] = pack_last(jnp.concatenate([partial, jnp.zeros((RHS, 128 - COLS), f32)], axis=1))
    send(steps_last[0])
    kall.wait_send()
    for i in range(2):
        columns = halo.at[:, :, pl.ds(0, LEVELS)]
        remote(columns, columns, sent.at[i], arrived.at[0, 0], (right, gy)).wait_send()
        remote(edge, edge, sent.at[2 + i], arrived.at[0, 0], (right, gy)).wait_send()
    last_z[zi, :PACKED] = collect(steps_last[0], last_y, PACKED)
    send(steps_last[1])
    lead_x[xi] = collect(steps_lead[1], lead_z, LEAD // 2)
    send(steps_lead[2])
    last_x[xi, :PACKED] = collect(steps_last[1], last_z, PACKED)
    send(steps_last[2])
    summed = collect(steps_lead[2], lead_x, LEAD // 2) * (1.0 / cells)
    summed = jnp.concatenate([summed, pltpu.roll(summed, LEAD, 1)], axis=0)
    rows, root = scale_start([summed[8 * b : 8 * b + 8] for b in range(LEAD // 8)], LEAD)
    lead[...] = jnp.concatenate(scale_end(eliminate(rows, 0, LEAD), root, LEAD), axis=0)
    last_gram[...] = unpack_last(collect(steps_last[2], last_x, PACKED)) * (1.0 / cells)

    for step in steps_lead + steps_last:
        step[1].wait_send()


def pack_last(block):
    lane = lax.broadcasted_iota(jnp.int32, (8, 128), 1)
    row = lax.broadcasted_iota(jnp.int32, (8, 128), 0)
    packed = [jnp.where(lane < LEAD, block[:8], pltpu.roll(block[8:], LEAD, 1))]
    for h in range(2):
        corner = jnp.where(lane < RHS, pltpu.roll(block[8 * h : 8 * h + 8], LEAD, 1), 0.0)
        spread = corner
        for r in range(1, 8):
            spread = jnp.where(row == r, pltpu.roll(corner, RHS * r, 1), spread)
        packed.append(jnp.sum(spread, axis=0, keepdims=True))
    return jnp.concatenate(packed, axis=0)


def unpack_last(packed):
    lane = lax.broadcasted_iota(jnp.int32, (8, 128), 1)
    row = lax.broadcasted_iota(jnp.int32, (8, 128), 0)
    block = []
    for h in range(2):
        side = packed[:8] if h == 0 else pltpu.roll(packed[:8], LEAD, 1)
        line = jnp.broadcast_to(packed[8 + h : 9 + h], (8, 128))
        corner = pltpu.roll(line, LEAD, 1)
        for r in range(1, 8):
            shift = (LEAD - RHS * r) % 128
            corner = jnp.where(row == r, pltpu.roll(line, shift, 1) if shift else line, corner)
        block.append(jnp.where(lane < LEAD, side, jnp.where(lane < COLS, corner, 0.0)))
    return jnp.concatenate(block, axis=0)


def scale_start(blocks, size):
    lane = lax.broadcasted_iota(jnp.int32, (8, 128), 1)
    row = lax.broadcasted_iota(jnp.int32, (8, 128), 0)
    scales = []
    across = jnp.zeros((1, 128), f32)
    root = jnp.zeros((1, 128), f32)
    for b, block in enumerate(blocks):
        on = lane == row + 8 * b
        diagonal = jnp.sum(jnp.where(on, block, 0.0), axis=1, keepdims=True)
        rooted = jnp.sqrt(diagonal)
        scale = 1.0 / rooted
        scales.append(scale)
        across = across + jnp.sum(jnp.where(on, scale, 0.0), axis=0, keepdims=True)
        root = root + jnp.sum(jnp.where(on, rooted, 0.0), axis=0, keepdims=True)
    rows = [
        jnp.where(lane < size, block * scale * across, jnp.where(lane - size == row + 8 * b, scale, 0.0))
        for b, (block, scale) in enumerate(zip(blocks, scales))
    ]
    return rows, jnp.where(lane[:1] < size, root, 1.0)


def eliminate(rows, begin, end):
    rows = list(rows)
    sub = lax.broadcasted_iota(jnp.int32, (8, 128), 0)

    def along(block, k):
        return jnp.broadcast_to(block[:, k : k + 1], (8, 128))

    def down(block, k):
        return jnp.broadcast_to(block[k : k + 1, :], (8, 128))

    for k in range(begin, end, 4):
        b, s = divmod(k, 8)
        columns = [[along(block, k + t) for block in rows[b:]] for t in range(4)]
        r0, r1, r2, r3 = [down(rows[b], s + t) for t in range(4)]
        p = {(t, u): down(columns[u][0], s + t) for t in range(4) for u in range(t, 4)}
        i0 = 1.0 / p[0, 0]
        l1, l2, l3 = p[0, 1] * i0, p[0, 2] * i0, p[0, 3] * i0
        q11 = p[1, 1] - l1 * p[0, 1]
        q12 = p[1, 2] - l1 * p[0, 2]
        q13 = p[1, 3] - l1 * p[0, 3]
        i1 = 1.0 / q11
        m2, m3 = q12 * i1, q13 * i1
        s22 = p[2, 2] - l2 * p[0, 2] - m2 * q12
        s23 = p[2, 3] - l2 * p[0, 3] - m2 * q13
        s33 = p[3, 3] - l3 * p[0, 3] - m3 * q13
        i2 = 1.0 / s22
        n3 = s23 * i2
        i3 = 1.0 / (s33 - n3 * s23)
        u1 = r1 - l1 * r0
        u2 = r2 - l2 * r0 - m2 * u1
        u3 = r3 - l3 * r0 - m3 * u1 - n3 * u2
        z3 = i3 * u3
        z2 = i2 * u2 - n3 * z3
        z1 = i1 * u1 - m2 * z2 - m3 * z3
        z0 = i0 * r0 - l1 * z1 - l2 * z2 - l3 * z3
        for i in range(b, len(rows)):
            c0, c1, c2, c3 = [column[i - b] for column in columns]
            changed = rows[i] - (c0 * z0 + c1 * z1) - (c2 * z2 + c3 * z3)
            if i == b:
                kept = jnp.where(sub == s + 2, u2, jnp.where(sub == s + 3, u3, rows[i]))
                changed = jnp.where(sub > s + 3, changed, jnp.where(sub == s + 1, u1, kept))
            rows[i] = changed
    return rows


def scale_end(rows, root, size):
    lane = lax.broadcasted_iota(jnp.int32, (8, 128), 1)
    row = lax.broadcasted_iota(jnp.int32, (8, 128), 0)
    done = []
    for b, block in enumerate(rows):
        diagonal = jnp.sum(jnp.where(lane == row + 8 * b, block, 0.0), axis=1, keepdims=True)
        block = jnp.where((lane >= row + 8 * b) & (lane - size <= row + 8 * b), block, 0.0)
        done.append(block * (1.0 / jnp.sqrt(diagonal)) * root)
    return done


def exact(a, b, dims):
    return lax.dot_general(a, b, dims, precision=lax.Precision.HIGHEST, preferred_element_type=f32)


def finish_kernel(v, last_gram, lead, out, r_out, stage, r_stage, sems):
    upper = lead[:, :LEAD]
    inverse = lead[:, LEAD:]
    against = last_gram[:, :LEAD]
    cross = exact(against, inverse, NT)
    schur = last_gram[:, LEAD:COLS] - exact(cross, cross, NT)
    back = exact(cross, inverse, NN)
    padded = jnp.concatenate([schur, jnp.zeros((RHS, 128 - RHS), f32)], axis=1)
    rows, root = scale_start([padded[:8], padded[8:]], RHS)
    rows = scale_end(eliminate(rows, 0, RHS), root, RHS)
    corner = jnp.concatenate(rows, axis=0)
    corner_upper = corner[:, :RHS]
    corner_inverse = corner[:, RHS : 2 * RHS]
    back = -exact(corner_inverse, back, NN)

    tall = jnp.concatenate([cross, jnp.zeros((RHS, 128 - LEAD), f32)], axis=1)
    tall = jnp.concatenate([tall, jnp.zeros((128 - RHS, 128), f32)], axis=0).T[:LEAD, :RHS]
    r_stage[...] = jnp.concatenate(
        [
            jnp.concatenate([upper, tall], axis=1),
            jnp.concatenate([jnp.zeros((RHS, LEAD), f32), corner_upper], axis=1),
        ],
        axis=0,
    )
    r_copy = pltpu.make_async_copy(r_stage, r_out, sems.at[0])
    r_copy.start()
    whole = jnp.concatenate(
        [
            jnp.concatenate([inverse, jnp.zeros((LEAD, 256 - LEAD), f32)], axis=1),
            jnp.concatenate([back, corner_inverse, jnp.zeros((RHS, 256 - COLS), f32)], axis=1),
        ],
        axis=0,
    )
    high = whole.astype(bf16).astype(f32)
    low = whole - high
    weights = high + pltpu.roll(high, COLS, 1) + pltpu.roll(low, 2 * COLS, 1)
    weights = weights[:, : 3 * COLS].astype(bf16)
    groups = 16
    per = NZ // groups
    planes = stage.reshape(COLS, PITCH, BY)
    for group in range(groups):
        def block(step, carry):
            for s in range(2):
                z = step * 2 + s
                for h in range(2):
                    both = jnp.concatenate([v[z, 2 * h], v[z, 2 * h + 1]], axis=1)
                    vh, vl = split(both)
                    q = jnp.dot(weights, jnp.concatenate([vh, vl, vh], axis=0), preferred_element_type=f32)
                    r = z * BX + 2 * h
                    stage[pl.ds(r, COLS, stride=PITCH), :] = q[:, :BY]
                    stage[pl.ds(r + 1, COLS, stride=PITCH), :] = q[:, BY:]
            return carry

        lax.fori_loop(group * per // 2, (group + 1) * per // 2, block, 0)
        rows = pl.ds(group * per * BX, per * BX)
        pltpu.make_async_copy(planes.at[:, rows, :], out.at[:, rows, :], sems.at[1]).start()
    pltpu.make_async_copy(planes.at[:, pl.ds(0, NZ * BX), :], out, sems.at[1]).wait()
    r_copy.wait()


def per_device(sizes, cells, right_sides, region_labels, face_flags, region_perm):
    gx_n, gy_n, zg, xg = sizes
    vmem = pl.BlockSpec(memory_space=pltpu.VMEM)
    hbm = pl.BlockSpec(memory_space=pltpu.HBM)
    scratch = [
        (CHUNKS * RHS * ROWS, BY),
        (NZ * BX, BY, jnp.int32),
        (2 * BX, BY, jnp.int32),
        None,
        (S, CHUNKS, 2 * LEVELS + 2, RHS, BY),
        (S, CHUNKS, RHS, BY),
        (BX, NZ, BY),
        (NZ, BY),
        (4, NZ, BY),
        (6, BX, NZ, BY),
        (NZ, BX, 6, HALF, BY),
        (LEAD, 2 * LEAD),
        (2 * RHS, 2 * COLS),
        (gy_n, LEAD // 2, 128),
        (zg, LEAD // 2, 128),
        (xg, LEAD // 2, 128),
        (gy_n, RHS, 128),
        (zg, RHS, 128),
        (xg, RHS, 128),
    ]
    scratch = [
        pltpu.SMEM(region_perm.shape, f32) if shape is None
        else pltpu.VMEM(shape[:-1], shape[-1]) if shape[-1] is jnp.int32
        else pltpu.VMEM(shape, f32)
        for shape in scratch
    ]
    dma = pltpu.SemaphoreType.DMA
    scratch += [dma((CHUNKS + 3,)), dma((2,)), dma((4,)), dma((S, CHUNKS)), dma((6,)), dma((6,))]
    v, last_gram, lead = pl.pallas_call(
        functools.partial(basis_kernel, sizes, cells),
        out_shape=(
            pltpu.VMEM((NZ, BX, COLS, BY), f32),
            pltpu.VMEM((RHS, 128), f32),
            pltpu.VMEM((LEAD, 2 * LEAD), f32),
        ),
        in_specs=[hbm, hbm, hbm, hbm],
        out_specs=(vmem, vmem, vmem),
        scratch_shapes=scratch,
        compiler_params=pltpu.CompilerParams(
            collective_id=0, has_side_effects=True, vmem_limit_bytes=40 * 1024 * 1024
        ),
        name="basis",
    )(
        *(pltpu.with_memory_space_constraint(a, pltpu.HBM) for a in (
            right_sides.reshape(RHS, NZ * BX, BY),
            region_labels.reshape(NZ * BX, BY),
            face_flags.reshape(2 * BX, BY),
            region_perm,
        )),
    )
    out, upper = pl.pallas_call(
        finish_kernel,
        out_shape=(
            jax.ShapeDtypeStruct((COLS, NZ * BX, BY), f32),
            jax.ShapeDtypeStruct((COLS, COLS), f32),
        ),
        in_specs=[vmem, vmem, vmem],
        out_specs=(hbm, hbm),
        scratch_shapes=[pltpu.VMEM((COLS * PITCH, BY), f32), pltpu.VMEM((COLS, COLS), f32), dma((2,))],
        compiler_params=pltpu.CompilerParams(vmem_limit_bytes=40 * 1024 * 1024),
        name="finish",
    )(v, last_gram, lead)
    return out.reshape(COLS, NZ, BX, BY), upper


def solution(mesh):
    gx_n, gy_n = mesh.shape["gx"], mesh.shape["gy"]
    zg = 8 if gx_n % 8 == 0 else 2
    sizes = (gx_n, gy_n, zg, gx_n // zg)
    cells = NZ * BX * BY * gx_n * gy_n
    placed = (P(None, None, "gx", "gy"), P(None, "gx", "gy"), P(None, "gx", "gy"), P())
    return jax.shard_map(
        functools.partial(per_device, sizes, cells),
        mesh=mesh,
        in_specs=placed,
        out_specs=(P(None, None, "gx", "gy"), P()),
        check_vma=False,
    )
```

```python
import functools
import jax
import jax.numpy as jnp
from jax import lax
from jax.experimental import pallas as pl
from jax.experimental.pallas import tpu as pltpu
from jax.sharding import PartitionSpec as P

RHS = 16
S = 4
VECS = S + 1
COLS = RHS * VECS
NZ = 32
BX = 4
BY = 128
HALF = 8
LEAD = RHS * S
LEVELS = 4
CHUNKS = NZ // LEVELS
ROWS = LEVELS * BX
PITCH = NZ * BX + 8
PACKED = 8 + RHS * RHS // 128
NT = (((1,), (1,)), ((), ()))
NN = (((1,), (0,)), ((), ()))
MESH = pl.DeviceIdType.MESH
f32 = jnp.float32
bf16 = jnp.bfloat16


def split(value):
    high = value.astype(bf16)
    low = (value - high.astype(f32)).astype(bf16)
    return high, low


def harmonic(centre, neighbour):
    summed = centre + neighbour
    return 2.0 * centre * neighbour / jnp.where(summed > 0, summed, 1.0)


def basis_kernel(
    sizes, cells,
    rs, labels_hbm, flags_hbm, perm_hbm,
    v, last_gram, lead,
    stage, labels, flags, perm, halo, edge, kown, kedge, khalo, ct, cb,
    acc_lead, acc_last, lead_y, lead_z, lead_x, last_y, last_z, last_x,
    load_sem, ksem, sent, arrived, asend, arecv,
):
    gx_n, gy_n, zg, xg = sizes
    gx = lax.axis_index("gx")
    gy = lax.axis_index("gy")
    right = lax.rem(gx + 1, gx_n)
    left = lax.rem(gx + gx_n - 1, gx_n)
    above = lax.rem(gy + 1, gy_n)
    below = lax.rem(gy + gy_n - 1, gy_n)
    zi = lax.rem(gx, zg)
    xi = lax.div(gx, zg)

    def z_peer(k):
        return (xi * zg + lax.rem(zi + k, zg), gy)

    def x_peer(k):
        return (lax.rem(xi + k, xg) * zg + zi, gy)

    def y_peer(k):
        return (gx, lax.rem(gy + k, gy_n))

    loads = [
        pltpu.make_async_copy(labels_hbm, labels, load_sem.at[CHUNKS]),
        pltpu.make_async_copy(flags_hbm, flags, load_sem.at[CHUNKS + 1]),
        pltpu.make_async_copy(perm_hbm, perm, load_sem.at[CHUNKS + 2]),
    ]

    def load_of(q):
        return pltpu.make_async_copy(
            rs.at[:, pl.ds(q * ROWS, ROWS), :], stage.reshape(CHUNKS, RHS, ROWS, BY).at[q], load_sem.at[q]
        )

    loads += [load_of(q) for q in range(CHUNKS)]
    for load in loads:
        load.start()
    peers = [z_peer(k) for k in sorted(range(1, zg), key=lambda k: abs(k - zg // 2))]
    peers += [y_peer(k) for k in sorted(range(1, gy_n), key=lambda k: abs(k - gy_n // 2))]
    peers += [x_peer(k) for k in range(1, xg)]
    peers += [(right, gy), (left, gy)]
    barrier = pltpu.get_barrier_semaphore()
    for peer in peers:
        pl.semaphore_signal(barrier, inc=1, device_id=peer, device_id_type=MESH)

    for load in loads[:3]:
        load.wait()
    for x in range(BX):
        label = labels[pl.ds(x, NZ, stride=BX), :]
        value = jnp.zeros((NZ, BY), f32)
        for region in range(perm.shape[0]):
            value = jnp.where(label == region, perm[region], value)
        kown[x] = value

    def remote(src, dst, send, recv, peer):
        return pltpu.make_async_remote_copy(
            src_ref=src, dst_ref=dst, send_sem=send, recv_sem=recv, device_id=peer, device_id_type=MESH
        )

    wide_lane = lax.broadcasted_iota(jnp.int32, (NZ, BY), 1)
    kends = jnp.zeros((NZ, BY), f32)
    for x in range(BX):
        kends = jnp.where(lax.div(wide_lane, 2) == x, pltpu.roll(kown[x], 2 * x + 1, 1), kends)
    kedge[...] = kends
    kcopies = [
        remote(kedge, khalo.at[2], ksem.at[0], ksem.at[1], (gx, above)),
        remote(kedge, khalo.at[3], ksem.at[0], ksem.at[1], (gx, below)),
        remote(kown.at[BX - 1], khalo.at[0], ksem.at[0], ksem.at[1], (right, gy)),
        remote(kown.at[0], khalo.at[1], ksem.at[0], ksem.at[1], (left, gy)),
    ]
    kall = remote(khalo, khalo, ksem.at[0], ksem.at[1], (right, gy))

    def copies_of(j, q):
        levels = pl.ds(q * LEVELS, LEVELS)
        plane = pl.ds(j * RHS, RHS)
        here = halo.at[j, q]
        return [
            remote(v.at[levels, BX - 1, plane, :], here.at[pl.ds(0, LEVELS)], sent.at[0], arrived.at[j, q], (right, gy)),
            remote(v.at[levels, 0, plane, :], here.at[pl.ds(LEVELS, LEVELS)], sent.at[1], arrived.at[j, q], (left, gy)),
            remote(edge.at[j, q], here.at[2 * LEVELS], sent.at[2], arrived.at[j, q], (gx, above)),
            remote(edge.at[j, q], here.at[2 * LEVELS + 1], sent.at[3], arrived.at[j, q], (gx, below)),
        ]

    lane = lax.broadcasted_iota(jnp.int32, (HALF, BY), 1)
    pair = lax.div(lane, 2)
    odd = lax.rem(lane, 2) == 1

    def pack(value, rr, packed):
        return jnp.where(pair == rr, pltpu.roll(value, 2 * rr + 1, 1), packed)

    def relayout(q, carry):
        load_of(q).wait()
        packed = [jnp.zeros((HALF, BY), f32) for _ in range(2)]
        for s in range(LEVELS):
            for x in range(BX):
                rr = s * BX + x
                value = stage[pl.ds(q * RHS * ROWS + rr, RHS, stride=ROWS), :]
                v[q * LEVELS + s, x, :RHS, :] = value
                for h in range(2):
                    packed[h] = pack(value[h * HALF : (h + 1) * HALF], rr, packed[h])
        for h in range(2):
            edge[0, q, pl.ds(h * HALF, HALF)] = packed[h]

        @pl.when(q == 0)
        def _():
            pl.semaphore_wait(barrier, len(peers))
            for copy in kcopies:
                copy.start()

        for copy in copies_of(0, q):
            copy.start()
        return carry

    lax.fori_loop(0, CHUNKS, relayout, 0)

    kall.wait_recv()
    level = lax.broadcasted_iota(jnp.int32, (NZ, BY), 0)
    merged = jnp.where(lax.rem(wide_lane, 2) == 1, pltpu.roll(khalo[2], 1, 1), pltpu.roll(khalo[3], BY - 1, 1))
    for x in range(BX):
        centre = kown[x]
        xm = kown[x - 1] if x > 0 else jnp.where(gx == 0, 0.0, khalo[0])
        xp = kown[x + 1] if x < BX - 1 else jnp.where(gx == gx_n - 1, 0.0, khalo[1])
        ends = pltpu.roll(merged, BY - 1 - 2 * x, 1)
        from_below = jnp.where(gy == 0, 0.0, ends)
        from_above = jnp.where(gy == gy_n - 1, 0.0, ends)
        ym = jnp.where(wide_lane == 0, from_below, pltpu.roll(centre, 1, 1))
        yp = jnp.where(wide_lane == BY - 1, from_above, pltpu.roll(centre, BY - 1, 1))
        zm = jnp.where(level == 0, 0.0, pltpu.roll(centre, 1, 0))
        zp = jnp.where(level == NZ - 1, 0.0, pltpu.roll(centre, NZ - 1, 0))
        t = [harmonic(centre, other) for other in (xm, xp, ym, yp, zm, zp)]
        bottom = flags[pl.ds(x, 1), :].astype(f32)
        top = flags[pl.ds(BX + x, 1), :].astype(f32)
        boundary = jnp.where(level == 0, 2.0 * centre * bottom, 0.0)
        boundary = boundary + jnp.where(level == NZ - 1, 2.0 * centre * top, 0.0)
        diagonal = t[0] + t[1] + t[2] + t[3] + t[4] + t[5] + boundary
        divisor = jnp.where(diagonal > 0, diagonal, 1.0)
        for n in range(6):
            ct[n, x] = -(t[n] / divisor)

    def spread(block, carry):
        for n in range(6):
            for x in range(BX):
                rows = ct[n, x, pl.ds(pl.multiple_of(block * 8, 8), 8), :]
                for s in range(8):
                    cb[block * 8 + s, x, n] = jnp.broadcast_to(rows[s : s + 1, :], (HALF, BY))
        return carry

    lax.fori_loop(0, NZ // 8, spread, 0)

    def advance(j, q):
        remote(halo.at[j, q], halo.at[j, q], sent.at[0], arrived.at[j, q], (right, gy)).wait_recv()
        base = q * LEVELS
        merged = [
            jnp.where(
                odd,
                pltpu.roll(halo[j, q, 2 * LEVELS, pl.ds(h * HALF, HALF), :], 1, 1),
                pltpu.roll(halo[j, q, 2 * LEVELS + 1, pl.ds(h * HALF, HALF), :], BY - 1, 1),
            )
            for h in range(2)
        ]
        packed = [jnp.zeros((HALF, BY), f32) for _ in range(2)]
        for s in range(LEVELS):
            z = base + s
            zm = lax.rem(z + NZ - 1, NZ) if s == 0 else z - 1
            zp = lax.rem(z + 1, NZ) if s == LEVELS - 1 else z + 1
            for x in range(BX):
                rr = s * BX + x
                coupling = [cb[z, x, n] for n in range(6)]
                for h in range(2):
                    here = pl.ds(j * RHS + h * HALF, HALF)
                    rows = pl.ds(h * HALF, HALF)
                    centre = v[z, x, here, :]
                    xm = v[z, x - 1, here, :] if x > 0 else halo[j, q, s, rows, :]
                    xp = v[z, x + 1, here, :] if x < BX - 1 else halo[j, q, LEVELS + s, rows, :]
                    ends = pltpu.roll(merged[h], BY - 1 - 2 * rr, 1)
                    ym = jnp.where(lane == 0, ends, pltpu.roll(centre, 1, 1))
                    yp = jnp.where(lane == BY - 1, ends, pltpu.roll(centre, BY - 1, 1))
                    summed = (
                        coupling[0] * xm
                        + coupling[1] * xp
                        + coupling[2] * ym
                        + coupling[3] * yp
                        + coupling[4] * v[zm, x, here, :]
                        + coupling[5] * v[zp, x, here, :]
                    )
                    value = summed if j == 0 else 2.0 * summed - v[z, x, pl.ds((j - 1) * RHS + h * HALF, HALF), :]
                    v[z, x, pl.ds((j + 1) * RHS + h * HALF, HALF), :] = value
                    if j < S - 1:
                        packed[h] = pack(value, rr, packed[h])
        if j < S - 1:
            for h in range(2):
                edge[j + 1, q, pl.ds(h * HALF, HALF)] = packed[h]
            for copy in copies_of(j + 1, q):
                copy.start()

    def lead_products(q):
        total = jnp.zeros((LEAD, 2 * LEAD), f32)
        for s in range(LEVELS):
            wide = jnp.concatenate([v[q * LEVELS + s, x, :LEAD, :] for x in range(BX)], axis=1)
            high, low = split(wide)
            total = total + lax.dot_general(high, jnp.concatenate([high, low], axis=0), NT, preferred_element_type=f32)
        acc_lead[...] += total

    def last_products(q):
        total = jnp.zeros((2 * RHS, 2 * COLS), f32)
        for s in range(LEVELS):
            wide = jnp.concatenate([v[q * LEVELS + s, x] for x in range(BX)], axis=1)
            high, low = split(wide)
            total = total + lax.dot_general(
                jnp.concatenate([high[LEAD:], low[LEAD:]], axis=0),
                jnp.concatenate([high, low], axis=0),
                NT,
                preferred_element_type=f32,
            )
        acc_last[...] += total

    def exchange(phase, buffer, index, count, peer_of, rows):
        part = buffer.at[index, pl.ds(0, rows)]
        return [
            remote(part, part, asend.at[phase], arecv.at[phase], peer_of(k))
            for k in sorted(range(1, count), key=lambda k: abs(k - count // 2))
        ], remote(
            buffer.at[pl.ds(0, count - 1), pl.ds(0, rows)],
            buffer.at[pl.ds(0, count - 1), pl.ds(0, rows)],
            asend.at[phase],
            arecv.at[phase],
            peer_of(1),
        )

    steps_lead = [
        exchange(0, lead_y, gy, gy_n, y_peer, LEAD // 2),
        exchange(1, lead_z, zi, zg, z_peer, LEAD // 2),
        exchange(2, lead_x, xi, xg, x_peer, LEAD // 2),
    ]
    steps_last = [
        exchange(3, last_y, gy, gy_n, y_peer, PACKED),
        exchange(4, last_z, zi, zg, z_peer, PACKED),
        exchange(5, last_x, xi, xg, x_peer, PACKED),
    ]

    def send(step):
        for copy in step[0]:
            copy.start()

    def collect(step, buffer, rows):
        step[1].wait_recv()
        total = buffer[0, :rows]
        for k in range(1, len(step[0]) + 1):
            total = total + buffer[k, :rows]
        return total

    acc_lead[...] = jnp.zeros_like(acc_lead)
    acc_last[...] = jnp.zeros_like(acc_last)

    def loop(j, more=None):
        def body(q, carry):
            advance(j, q)
            if more is not None:
                more(q)
            return carry

        lax.fori_loop(0, CHUNKS, body, 0)

    loop(0)
    loop(1)
    loop(2, lead_products)

    partial = acc_lead[...]
    mirrored = jnp.concatenate([partial, jnp.zeros((128 - LEAD, 128), f32)], axis=0).T[LEAD : 2 * LEAD]
    lead_lane = lax.broadcasted_iota(jnp.int32, (LEAD, 128), 1)
    partial = jnp.where(lead_lane < LEAD, partial + pltpu.roll(partial, LEAD, 1), 0.0) + mirrored
    lead_y[gy] = partial[: LEAD // 2] + pltpu.roll(partial[LEAD // 2 :], LEAD, 1)
    send(steps_lead[0])

    def beside(q):
        last_products(q)

        @pl.when(q == CHUNKS - 2)
        def _():
            lead_z[zi] = collect(steps_lead[0], lead_y, LEAD // 2)
            send(steps_lead[1])

    loop(3, beside)

    partial = acc_last[...]
    partial = partial[:RHS, :COLS] + partial[:RHS, COLS:] + partial[RHS:, :COLS]
    last_y[gy, :PACKED] = pack_last(jnp.concatenate([partial, jnp.zeros((RHS, 128 - COLS), f32)], axis=1))
    send(steps_last[0])
    kall.wait_send()
    for i in range(2):
        columns = halo.at[:, :, pl.ds(0, LEVELS)]
        remote(columns, columns, sent.at[i], arrived.at[0, 0], (right, gy)).wait_send()
        remote(edge, edge, sent.at[2 + i], arrived.at[0, 0], (right, gy)).wait_send()
    last_z[zi, :PACKED] = collect(steps_last[0], last_y, PACKED)
    send(steps_last[1])
    lead_x[xi] = collect(steps_lead[1], lead_z, LEAD // 2)
    send(steps_lead[2])
    last_x[xi, :PACKED] = collect(steps_last[1], last_z, PACKED)
    send(steps_last[2])
    summed = collect(steps_lead[2], lead_x, LEAD // 2) * (1.0 / cells)
    summed = jnp.concatenate([summed, pltpu.roll(summed, LEAD, 1)], axis=0)
    rows, root = scale_start([summed[8 * b : 8 * b + 8] for b in range(LEAD // 8)], LEAD)
    lead[...] = jnp.concatenate(scale_end(eliminate(rows, 0, LEAD), root, LEAD), axis=0)
    last_gram[...] = unpack_last(collect(steps_last[2], last_x, PACKED)) * (1.0 / cells)

    for step in steps_lead + steps_last:
        step[1].wait_send()


def pack_last(block):
    lane = lax.broadcasted_iota(jnp.int32, (8, 128), 1)
    row = lax.broadcasted_iota(jnp.int32, (8, 128), 0)
    packed = [jnp.where(lane < LEAD, block[:8], pltpu.roll(block[8:], LEAD, 1))]
    for h in range(2):
        corner = jnp.where(lane < RHS, pltpu.roll(block[8 * h : 8 * h + 8], LEAD, 1), 0.0)
        spread = corner
        for r in range(1, 8):
            spread = jnp.where(row == r, pltpu.roll(corner, RHS * r, 1), spread)
        packed.append(jnp.sum(spread, axis=0, keepdims=True))
    return jnp.concatenate(packed, axis=0)


def unpack_last(packed):
    lane = lax.broadcasted_iota(jnp.int32, (8, 128), 1)
    row = lax.broadcasted_iota(jnp.int32, (8, 128), 0)
    block = []
    for h in range(2):
        side = packed[:8] if h == 0 else pltpu.roll(packed[:8], LEAD, 1)
        line = jnp.broadcast_to(packed[8 + h : 9 + h], (8, 128))
        corner = pltpu.roll(line, LEAD, 1)
        for r in range(1, 8):
            shift = (LEAD - RHS * r) % 128
            corner = jnp.where(row == r, pltpu.roll(line, shift, 1) if shift else line, corner)
        block.append(jnp.where(lane < LEAD, side, jnp.where(lane < COLS, corner, 0.0)))
    return jnp.concatenate(block, axis=0)


def scale_start(blocks, size):
    lane = lax.broadcasted_iota(jnp.int32, (8, 128), 1)
    row = lax.broadcasted_iota(jnp.int32, (8, 128), 0)
    scales = []
    across = jnp.zeros((1, 128), f32)
    root = jnp.zeros((1, 128), f32)
    for b, block in enumerate(blocks):
        on = lane == row + 8 * b
        diagonal = jnp.sum(jnp.where(on, block, 0.0), axis=1, keepdims=True)
        rooted = jnp.sqrt(diagonal)
        scale = 1.0 / rooted
        scales.append(scale)
        across = across + jnp.sum(jnp.where(on, scale, 0.0), axis=0, keepdims=True)
        root = root + jnp.sum(jnp.where(on, rooted, 0.0), axis=0, keepdims=True)
    rows = [
        jnp.where(lane < size, block * scale * across, jnp.where(lane - size == row + 8 * b, scale, 0.0))
        for b, (block, scale) in enumerate(zip(blocks, scales))
    ]
    return rows, jnp.where(lane[:1] < size, root, 1.0)


def eliminate(rows, begin, end):
    rows = list(rows)
    sub = lax.broadcasted_iota(jnp.int32, (8, 128), 0)

    def along(block, k):
        return jnp.broadcast_to(block[:, k : k + 1], (8, 128))

    def down(block, k):
        return jnp.broadcast_to(block[k : k + 1, :], (8, 128))

    for k in range(begin, end, 4):
        b, s = divmod(k, 8)
        columns = [[along(block, k + t) for block in rows[b:]] for t in range(4)]
        r0, r1, r2, r3 = [down(rows[b], s + t) for t in range(4)]
        p = {(t, u): down(columns[u][0], s + t) for t in range(4) for u in range(t, 4)}
        i0 = 1.0 / p[0, 0]
        l1, l2, l3 = p[0, 1] * i0, p[0, 2] * i0, p[0, 3] * i0
        q11 = p[1, 1] - l1 * p[0, 1]
        q12 = p[1, 2] - l1 * p[0, 2]
        q13 = p[1, 3] - l1 * p[0, 3]
        i1 = 1.0 / q11
        m2, m3 = q12 * i1, q13 * i1
        s22 = p[2, 2] - l2 * p[0, 2] - m2 * q12
        s23 = p[2, 3] - l2 * p[0, 3] - m2 * q13
        s33 = p[3, 3] - l3 * p[0, 3] - m3 * q13
        i2 = 1.0 / s22
        n3 = s23 * i2
        i3 = 1.0 / (s33 - n3 * s23)
        u1 = r1 - l1 * r0
        u2 = r2 - l2 * r0 - m2 * u1
        u3 = r3 - l3 * r0 - m3 * u1 - n3 * u2
        z3 = i3 * u3
        z2 = i2 * u2 - n3 * z3
        z1 = i1 * u1 - m2 * z2 - m3 * z3
        z0 = i0 * r0 - l1 * z1 - l2 * z2 - l3 * z3
        for i in range(b, len(rows)):
            c0, c1, c2, c3 = [column[i - b] for column in columns]
            changed = rows[i] - (c0 * z0 + c1 * z1) - (c2 * z2 + c3 * z3)
            if i == b:
                kept = jnp.where(sub == s + 2, u2, jnp.where(sub == s + 3, u3, rows[i]))
                changed = jnp.where(sub > s + 3, changed, jnp.where(sub == s + 1, u1, kept))
            rows[i] = changed
    return rows


def scale_end(rows, root, size):
    lane = lax.broadcasted_iota(jnp.int32, (8, 128), 1)
    row = lax.broadcasted_iota(jnp.int32, (8, 128), 0)
    done = []
    for b, block in enumerate(rows):
        diagonal = jnp.sum(jnp.where(lane == row + 8 * b, block, 0.0), axis=1, keepdims=True)
        block = jnp.where((lane >= row + 8 * b) & (lane - size <= row + 8 * b), block, 0.0)
        done.append(block * (1.0 / jnp.sqrt(diagonal)) * root)
    return done


def exact(a, b, dims):
    return lax.dot_general(a, b, dims, precision=lax.Precision.HIGHEST, preferred_element_type=f32)


def finish_kernel(v, last_gram, lead, out, r_out, stage, r_stage, sems):
    upper = lead[:, :LEAD]
    inverse = lead[:, LEAD:]
    against = last_gram[:, :LEAD]
    cross = exact(against, inverse, NT)
    schur = last_gram[:, LEAD:COLS] - exact(cross, cross, NT)
    back = exact(cross, inverse, NN)
    padded = jnp.concatenate([schur, jnp.zeros((RHS, 128 - RHS), f32)], axis=1)
    rows, root = scale_start([padded[:8], padded[8:]], RHS)
    rows = scale_end(eliminate(rows, 0, RHS), root, RHS)
    corner = jnp.concatenate(rows, axis=0)
    corner_upper = corner[:, :RHS]
    corner_inverse = corner[:, RHS : 2 * RHS]
    back = -exact(corner_inverse, back, NN)

    tall = jnp.concatenate([cross, jnp.zeros((RHS, 128 - LEAD), f32)], axis=1)
    tall = jnp.concatenate([tall, jnp.zeros((128 - RHS, 128), f32)], axis=0).T[:LEAD, :RHS]
    r_stage[...] = jnp.concatenate(
        [
            jnp.concatenate([upper, tall], axis=1),
            jnp.concatenate([jnp.zeros((RHS, LEAD), f32), corner_upper], axis=1),
        ],
        axis=0,
    )
    r_copy = pltpu.make_async_copy(r_stage, r_out, sems.at[0])
    r_copy.start()
    whole = jnp.concatenate(
        [
            jnp.concatenate([inverse, jnp.zeros((LEAD, 256 - LEAD), f32)], axis=1),
            jnp.concatenate([back, corner_inverse, jnp.zeros((RHS, 256 - COLS), f32)], axis=1),
        ],
        axis=0,
    )
    high = whole.astype(bf16).astype(f32)
    low = whole - high
    weights = high + pltpu.roll(high, COLS, 1) + pltpu.roll(low, 2 * COLS, 1)
    weights = weights[:, : 3 * COLS].astype(bf16)
    groups = 16
    per = NZ // groups
    planes = stage.reshape(COLS, PITCH, BY)
    for group in range(groups):
        def block(step, carry):
            for s in range(2):
                z = step * 2 + s
                for h in range(2):
                    both = jnp.concatenate([v[z, 2 * h], v[z, 2 * h + 1]], axis=1)
                    vh, vl = split(both)
                    q = jnp.dot(weights, jnp.concatenate([vh, vl, vh], axis=0), preferred_element_type=f32)
                    r = z * BX + 2 * h
                    stage[pl.ds(r, COLS, stride=PITCH), :] = q[:, :BY]
                    stage[pl.ds(r + 1, COLS, stride=PITCH), :] = q[:, BY:]
            return carry

        lax.fori_loop(group * per // 2, (group + 1) * per // 2, block, 0)
        rows = pl.ds(group * per * BX, per * BX)
        pltpu.make_async_copy(planes.at[:, rows, :], out.at[:, rows, :], sems.at[1]).start()
    pltpu.make_async_copy(planes.at[:, pl.ds(0, NZ * BX), :], out, sems.at[1]).wait()
    r_copy.wait()


def per_device(sizes, cells, right_sides, region_labels, face_flags, region_perm):
    gx_n, gy_n, zg, xg = sizes
    vmem = pl.BlockSpec(memory_space=pltpu.VMEM)
    hbm = pl.BlockSpec(memory_space=pltpu.HBM)
    scratch = [
        (CHUNKS * RHS * ROWS, BY),
        (NZ * BX, BY, jnp.int32),
        (2 * BX, BY, jnp.int32),
        None,
        (S, CHUNKS, 2 * LEVELS + 2, RHS, BY),
        (S, CHUNKS, RHS, BY),
        (BX, NZ, BY),
        (NZ, BY),
        (4, NZ, BY),
        (6, BX, NZ, BY),
        (NZ, BX, 6, HALF, BY),
        (LEAD, 2 * LEAD),
        (2 * RHS, 2 * COLS),
        (gy_n, LEAD // 2, 128),
        (zg, LEAD // 2, 128),
        (xg, LEAD // 2, 128),
        (gy_n, RHS, 128),
        (zg, RHS, 128),
        (xg, RHS, 128),
    ]
    scratch = [
        pltpu.SMEM(region_perm.shape, f32) if shape is None
        else pltpu.VMEM(shape[:-1], shape[-1]) if shape[-1] is jnp.int32
        else pltpu.VMEM(shape, f32)
        for shape in scratch
    ]
    dma = pltpu.SemaphoreType.DMA
    scratch += [dma((CHUNKS + 3,)), dma((2,)), dma((4,)), dma((S, CHUNKS)), dma((6,)), dma((6,))]
    v, last_gram, lead = pl.pallas_call(
        functools.partial(basis_kernel, sizes, cells),
        out_shape=(
            pltpu.VMEM((NZ, BX, COLS, BY), f32),
            pltpu.VMEM((RHS, 128), f32),
            pltpu.VMEM((LEAD, 2 * LEAD), f32),
        ),
        in_specs=[hbm, hbm, hbm, hbm],
        out_specs=(vmem, vmem, vmem),
        scratch_shapes=scratch,
        compiler_params=pltpu.CompilerParams(
            collective_id=0, has_side_effects=True, vmem_limit_bytes=40 * 1024 * 1024
        ),
        name="basis",
    )(
        *(pltpu.with_memory_space_constraint(a, pltpu.HBM) for a in (
            right_sides.reshape(RHS, NZ * BX, BY),
            region_labels.reshape(NZ * BX, BY),
            face_flags.reshape(2 * BX, BY),
            region_perm,
        )),
    )
    out, upper = pl.pallas_call(
        finish_kernel,
        out_shape=(
            jax.ShapeDtypeStruct((COLS, NZ * BX, BY), f32),
            jax.ShapeDtypeStruct((COLS, COLS), f32),
        ),
        in_specs=[vmem, vmem, vmem],
        out_specs=(hbm, hbm),
        scratch_shapes=[pltpu.VMEM((COLS * PITCH, BY), f32), pltpu.VMEM((COLS, COLS), f32), dma((2,))],
        compiler_params=pltpu.CompilerParams(vmem_limit_bytes=40 * 1024 * 1024),
        name="finish",
    )(v, last_gram, lead)
    return out.reshape(COLS, NZ, BX, BY), upper


def solution(mesh):
    gx_n, gy_n = mesh.shape["gx"], mesh.shape["gy"]
    zg = 8 if gx_n % 8 == 0 else 2
    sizes = (gx_n, gy_n, zg, gx_n // zg)
    cells = NZ * BX * BY * gx_n * gy_n
    placed = (P(None, None, "gx", "gy"), P(None, "gx", "gy"), P(None, "gx", "gy"), P())
    return jax.shard_map(
        functools.partial(per_device, sizes, cells),
        mesh=mesh,
        in_specs=placed,
        out_specs=(P(None, None, "gx", "gy"), P()),
        check_vma=False,
    )
```
